128 devices in a mesh: dp: 16 (over x, y), mp: 8 (over z, core).
Axes of the slice: x: 4, y: 4, z: 4, core: 2. Of those that a mesh axis runs over, the one named last changes fastest.
Arguments:
- tokens: bfloat16 [12288, 3072], P('dp', 'mp'), may hold values from -50 to 50
- target: bfloat16 [12288, 12288], P('dp', 'mp'), may hold values from -90 to 90
- weight: bfloat16 [3072, 12288], P('dp', 'mp'), may hold values from -0.0234375 to 0.0234375
Outputs:
- update: float32 [3072, 12288], P('dp', 'mp')
The draws below stay inside these ranges and needn't reach their ends.
All inputs are finite; a program needn't handle non-finite values.
Results may differ from the reference program's by a relative error of at most 0.029.
Values may be sent and summed in bfloat16 or wider, within the bound.
No kernel may reach another device: no remote copies, remote signals or barrier semaphores. Data moves between devices by JAX's collectives and lax.ppermute only.
A program may use at most 128 MiB of HBM per device.

```python
import math
import jax
import jax.numpy as jnp
from jax import lax

D = 3072
FF = 12288
TOK_DEV = 768
TOKENS = 12288
N_DP = 16


def rising_scales(key, count, top):
    jitter = jax.random.uniform(key, (count,), jnp.float32)
    place = jnp.arange(count, dtype=jnp.float32)
    return top ** ((place + 0.1 * count * jitter) / (1.1 * count))


def group_signs(rows, group_rows):
    place = jnp.arange(rows, dtype=jnp.int32) // group_rows
    return (1 - 2 * (place % 2)).astype(jnp.float32)


def draw_tokens(key, part):
    key = jax.random.fold_in(key, 11)
    key_scale, key_value = jax.random.split(key)
    scales = 10.0 * rising_scales(key_scale, D, 0.1)
    values = jnp.clip(jax.random.normal(key_value, (TOKENS, D), jnp.float32), -5.0, 5.0)
    return (values * scales[None, :]).astype(jnp.bfloat16)


def draw_target(key, part):
    key = jax.random.fold_in(key, 23)
    key_scale, key_value, key_common = jax.random.split(key, 3)
    scales = rising_scales(key_scale, FF, 10.0)
    signs = group_signs(TOKENS, TOK_DEV)
    common = jnp.clip(jax.random.normal(key_common, (FF,), jnp.float32), -3.0, 3.0)
    values = jnp.clip(jax.random.normal(key_value, (TOKENS, FF), jnp.float32), -4.0, 4.0)
    values = values + 1.5 * signs[:, None] * common[None, :]
    return (values * scales[None, :]).astype(jnp.bfloat16)


def block_scale(key, dims, cuts, least, high):
    factor_of, own = 1.0, jax.random.fold_in(key, 6)
    for dim, shards_of in cuts:
        draws = jnp.exp(jax.random.uniform(jax.random.fold_in(own, dim), (shards_of,), jnp.float32, least / len(cuts), high / len(cuts)))
        factor_of = factor_of * jnp.repeat(draws, dims[dim] // shards_of).reshape([-1 if axis == dim else 1 for axis in range(len(dims))])
    return factor_of


def centred(own_key, shape, deviation, bound, cuts=(), kind=jnp.bfloat16):
    entries = jax.random.normal(own_key, shape, jnp.float32) * deviation
    if len(cuts) > 0:
        entries = block_scale(own_key, shape, cuts, -0.22, 0.18) * entries
    return jnp.clip(entries, min=-bound, max=bound).astype(kind)


def setup_inputs(seed: int = 0) -> dict:
    seeds = jax.random.split(jax.random.key(seed), 4)
    tokens = draw_tokens(jax.random.fold_in(seeds[3], 71), 0)
    target = draw_target(jax.random.fold_in(seeds[3], 71), 0)
    weight = centred(seeds[2], (D, FF), (21 * D) ** -0.5, 0.0234375, ((0, 16), (1, 8)))
    return dict(tokens=tokens, target=target, weight=weight)


def slope_of(hidden, target):
    values, pullback = jax.vjp(jax.nn.gelu, hidden)
    deriv, = pullback(jnp.ones_like(hidden))
    return ((values - target.astype(jnp.float32)) * deriv).astype(jnp.bfloat16)

def gradient(tokens, target, weight):
    grouped_x = tokens.reshape(N_DP, TOK_DEV, D)
    grouped_t = target.reshape(N_DP, TOK_DEV, FF)

    def step(total, pieces):
        rows_x, rows_t = pieces
        hidden = jnp.dot(rows_x, weight, preferred_element_type=jnp.float32)
        slope = slope_of(hidden, rows_t)
        term = lax.dot_general(rows_x, slope, (((0,), (0,)), ((), ())), preferred_element_type=jnp.float32)
        term = lax.optimization_barrier(term.astype(jnp.bfloat16))
        return (total + term.astype(jnp.float32), None)
    total, unused = lax.scan(step, jnp.zeros((D, FF), jnp.float32), (grouped_x, grouped_t))
    return total

def reference(tokens, target, weight):
    first = gradient(tokens, target, weight)
    scale = 0.5 * math.sqrt(FF) / jnp.sqrt(jnp.sum(first * first) + 1e-06)
    perturbed = (weight.astype(jnp.float32) + scale * first).astype(jnp.bfloat16)
    second = gradient(tokens, target, perturbed)
    factor = jnp.minimum(1.0, math.sqrt(D * FF) / jnp.sqrt(jnp.sum(second * second) + 1e-06))
    return second * factor
```

```python
import functools
import math

import jax
import jax.numpy as jnp
from jax import lax
from jax.experimental import pallas as pl
from jax.experimental.pallas import tpu as pltpu
from jax.sharding import Mesh, PartitionSpec as P

BF16, F32 = jnp.bfloat16, jnp.float32
N = 4
TILE = 512


def shift(value, axis, step):
    return lax.ppermute(value, axis, [(i, (i + step) % N) for i in range(N)])


def slope_of(hidden, target):
    root = math.sqrt(2.0 / math.pi)
    square = hidden * hidden
    bend = jnp.tanh(root * hidden * (1.0 + 0.044715 * square))
    half = 0.5 * (1.0 + bend)
    deriv = half + (0.5 * root) * hidden * (1.0 - bend * bend) * (1.0 + (3 * 0.044715) * square)
    return ((hidden * half - target.astype(F32)) * deriv).astype(BF16)


def product(x_ref, w_ref):
    x = jnp.concatenate([x_ref[k] for k in range(x_ref.shape[0])], axis=1)
    return jnp.dot(x, w_ref[...], preferred_element_type=F32)


def first_kernel(x_ref, w_ref, t_ref, h_ref, s_ref):
    hidden = product(x_ref, w_ref)
    h_ref[...] = hidden
    s_ref[...] = slope_of(hidden, t_ref[...])


def second_kernel(scale_ref, x_ref, w_ref, t_ref, h_ref, s_ref):
    hidden = h_ref[...] + scale_ref[0, 0] * product(x_ref, w_ref)
    s_ref[...] = slope_of(hidden, t_ref[...])


def slopes(x, w, t, hidden=None, scale=None):
    blocks, rows, wide = x.shape
    cols = w.shape[1]
    tile = pl.BlockSpec((TILE, cols), lambda i: (i, 0))
    x_spec = pl.BlockSpec((blocks, TILE, wide), lambda i: (0, i, 0))
    w_spec = pl.BlockSpec(w.shape, lambda i: (0, 0))
    s_shape = jax.ShapeDtypeStruct((rows, cols), BF16)
    params = pltpu.CompilerParams(vmem_limit_bytes=48 << 20)
    cost = pl.CostEstimate(flops=2 * rows * cols * blocks * wide, bytes_accessed=x.size * 2, transcendentals=rows * cols)
    if hidden is None:
        return pl.pallas_call(
            first_kernel,
            grid=(rows // TILE,),
            in_specs=[x_spec, w_spec, tile],
            out_specs=[tile, tile],
            out_shape=[jax.ShapeDtypeStruct((rows, cols), F32), s_shape],
            compiler_params=params,
            cost_estimate=cost,
        )(x, w, t)
    return pl.pallas_call(
        second_kernel,
        grid=(rows // TILE,),
        in_specs=[pl.BlockSpec(memory_space=pltpu.SMEM), x_spec, w_spec, tile, tile],
        out_specs=tile,
        out_shape=s_shape,
        compiler_params=params,
        cost_estimate=cost,
    )(scale, x, w, t, hidden)


def term_kernel(which_ref, x_ref, s_ref, o_ref):
    o_ref[...] = lax.dot_general(
        x_ref[0], s_ref[...], (((0,), (0,)), ((), ())), preferred_element_type=F32
    )


def term(x, s, block):
    blocks, rows, wide = x.shape
    cols = s.shape[1]
    return pl.pallas_call(
        term_kernel,
        grid_spec=pltpu.PrefetchScalarGridSpec(
            num_scalar_prefetch=1,
            grid=(2,),
            in_specs=[
                pl.BlockSpec((1, rows, wide), lambda k, which: (2 * which[0] + k, 0, 0)),
                pl.BlockSpec((rows, cols), lambda k, which: (0, 0)),
            ],
            out_specs=pl.BlockSpec((wide, cols), lambda k, which: (k, 0)),
        ),
        out_shape=jax.ShapeDtypeStruct((2 * wide, cols), F32),
        compiler_params=pltpu.CompilerParams(vmem_limit_bytes=48 << 20),
        cost_estimate=pl.CostEstimate(flops=4 * rows * cols * wide, bytes_accessed=rows * wide * 4, transcendentals=0),
    )(jnp.reshape(block, (1,)).astype(jnp.int32), x, s)


def ring_sum(part, me):
    block = lambda step: part(lax.rem(me + step, N))
    far = block(2).astype(BF16)
    half = far.shape[0] // 2
    far_next, far_prev = shift(far[:half], "x", 1), shift(far[half:], "x", -1)
    to_next, to_prev = block(1), block(3)
    next_low = shift(to_next[half:].astype(BF16), "x", 1)
    prev_high = shift(to_prev[:half].astype(BF16), "x", -1)
    next_high = shift((to_next[:half] + far_next.astype(F32)).astype(BF16), "x", 1)
    prev_low = shift((to_prev[half:] + far_prev.astype(F32)).astype(BF16), "x", -1)
    own = block(0)
    high = own[:half] + next_high.astype(F32) + prev_high.astype(F32)
    low = own[half:] + next_low.astype(F32) + prev_low.astype(F32)
    return jnp.concatenate([high, low], axis=0)


def ring_gather(value, axis):
    half = value.shape[0] // 2
    high, low = value[:half], value[half:]
    prev_high, next_low = shift(high, axis, 1), shift(low, axis, -1)
    prev_low, next_high = shift(low, axis, 1), shift(high, axis, -1)
    far_high, far_low = shift(prev_high, axis, 1), shift(next_low, axis, -1)
    join = lambda a, b: jnp.concatenate([a, b], axis=0)
    return jnp.stack([value, join(next_high, next_low), join(far_high, far_low), join(prev_high, prev_low)])


def ring_swap(chunk, axis):
    far = chunk(2)
    half = far.shape[0] // 2
    from_prev, from_next = shift(chunk(1), axis, 1), shift(chunk(3), axis, -1)
    far_high = shift(shift(far[:half], axis, 1), axis, 1)
    far_low = shift(shift(far[half:], axis, -1), axis, -1)
    return jnp.stack([chunk(0), from_next, jnp.concatenate([far_high, far_low], axis=0), from_prev])


def in_order(stacked, me):
    twice = jnp.concatenate([stacked, stacked], axis=0)
    return lax.dynamic_slice_in_dim(twice, lax.rem(N - me, N), N, axis=0)


def total_of(value):
    total = jnp.full((8, 128), jnp.sum(value * value), F32)
    total = total + lax.ppermute(total, "c", [(0, 1), (1, 0)])
    for axis in ("x", "y", "z"):
        total = total + shift(total, axis, 1) + shift(total, axis, -1) + shift(total, axis, 2)
    return total[0, 0]


def per_device(tokens, target, weight):
    ix, iy = lax.axis_index("x"), lax.axis_index("y")
    rows, wide = tokens.shape
    cols = weight.shape[1] // N
    width = wide * 2 * N
    hidden_all = weight.shape[1] * 2 * N

    x = lax.all_gather(tokens, ("z", "c", "y"), axis=0, tiled=True).reshape(2 * N, N * rows, wide)

    def columns(array):
        return lambda k: lax.dynamic_slice_in_dim(array, lax.rem(iy + k, N) * cols, cols, axis=1)

    w_rows = in_order(ring_swap(columns(weight), "y"), iy).reshape(-1, cols)
    w = in_order(ring_gather(w_rows, "x"), ix).reshape(width, cols)
    t = in_order(ring_swap(columns(target), "y"), iy).reshape(N * rows, cols)

    hidden, slope = slopes(x, w, t)
    first = ring_sum(lambda b: term(x, slope, b), ix)
    scale = 0.5 * math.sqrt(hidden_all) / jnp.sqrt(total_of(first) + 1e-06)
    shifts = in_order(ring_gather(first.astype(BF16), "x"), ix).reshape(width, cols)
    slope = slopes(x, shifts, t, hidden, scale.reshape(1, 1))
    second = ring_sum(lambda b: term(x, slope, b), ix)
    total = total_of(second)
    factor = jnp.minimum(1.0, math.sqrt(width * hidden_all) / jnp.sqrt(total + 1e-06))
    held = second.astype(BF16).reshape(N, -1, cols)
    parts = in_order(ring_swap(lambda k: lax.dynamic_index_in_dim(held, lax.rem(iy + k, N), 0, keepdims=False), "y"), iy)
    whole = jnp.concatenate([parts[k] for k in range(N)], axis=1)
    return whole.astype(F32) * factor


def solution(mesh):
    grid = Mesh(mesh.devices.reshape(N, N, N, 2), ("x", "y", "z", "c"))
    spec = P(("x", "y"), ("z", "c"))
    return jax.shard_map(
        per_device, mesh=grid, in_specs=(spec, spec, spec), out_specs=spec, check_vma=False
    )
```

```python
import math

import jax
import jax.numpy as jnp
from jax import lax
from jax.experimental import pallas as pl
from jax.experimental.pallas import tpu as pltpu
from jax.sharding import Mesh, PartitionSpec as P

BF16, F32 = jnp.bfloat16, jnp.float32
N = 4
NT = (((1,), (1,)), ((), ()))
PARAMS = pltpu.CompilerParams(vmem_limit_bytes=32 << 20)


def shift(value, axis, step):
    return lax.ppermute(value, axis, [(i, (i + step) % N) for i in range(N)])


def slope_of(hidden, target):
    root = math.sqrt(2.0 / math.pi)
    square = hidden * hidden
    bend = jnp.tanh(hidden * (root + (root * 0.044715) * square))
    half = 0.5 + 0.5 * bend
    deriv = half + (hidden * (1.0 - bend * bend)) * (0.5 * root + (1.5 * root * 0.044715) * square)
    return ((hidden * half - target.astype(F32)) * deriv).astype(BF16)


def joined(x_ref):
    return jnp.concatenate([x_ref[k] for k in range(x_ref.shape[0])], axis=1)


def cost(rows, deep, cols, exps=0):
    return pl.CostEstimate(
        flops=2 * rows * deep * cols, bytes_accessed=2 * deep * (rows + cols) + 4 * rows * cols, transcendentals=exps
    )


def first_kernel(x_ref, w_ref, t_ref, h_ref, s_ref):
    hidden = lax.dot_general(w_ref[...], joined(x_ref), NT, preferred_element_type=F32)
    h_ref[...] = hidden
    s_ref[...] = slope_of(hidden, t_ref[...])


def first_slopes(x, w, t):
    blocks, rows, wide = x.shape
    cols = w.shape[0]
    tile = rows // N
    out = pl.BlockSpec((cols, tile), lambda i: (0, i))
    return pl.pallas_call(
        first_kernel,
        grid=(N,),
        in_specs=[
            pl.BlockSpec((blocks, tile, wide), lambda i: (0, i, 0)),
            pl.BlockSpec(w.shape, lambda i: (0, 0)),
            out,
        ],
        out_specs=[out, out],
        out_shape=[jax.ShapeDtypeStruct((cols, rows), F32), jax.ShapeDtypeStruct((cols, rows), BF16)],
        compiler_params=PARAMS,
        cost_estimate=cost(cols, blocks * wide, rows, rows * cols),
    )(x, w, t)


def moved_kernel(count, started, last, *refs):
    refs = list(refs[1:])
    xs, fs = refs[:count], refs[count : 2 * count]
    rest = refs[2 * count :]
    part = sum(
        lax.dot_general(f[...], joined(x), NT, preferred_element_type=F32) for x, f in zip(xs, fs)
    )
    if started:
        part = part + rest.pop(0)[...]
    if last:
        scale, hidden, target, out = rest
        out[...] = slope_of(hidden[...] + scale[0, 0] * part, target[...])
    else:
        rest[0][...] = part


def moved(x, pieces, which, part=None, last=None):
    blocks, rows, wide = x.shape
    cols, deep = pieces[0].shape
    per = deep // wide
    tile = rows // N
    count = len(pieces)
    at = lambda j: pl.BlockSpec((per, tile, wide), lambda i, which: (which[j], i, 0))
    out = pl.BlockSpec((cols, tile), lambda i, which: (0, i))
    specs = [at(j) for j in range(count)] + [pl.BlockSpec((cols, deep), lambda i, which: (0, 0))] * count
    args = [x] * count + list(pieces)
    alias = {}
    if part is not None:
        if last is None:
            alias = {1 + len(args): 0}
        specs.append(out)
        args.append(part)
    if last is not None:
        specs += [pl.BlockSpec(memory_space=pltpu.SMEM), out, out]
        args += list(last)

    def kernel(*refs):
        moved_kernel(count, part is not None, last is not None, *refs)

    return pl.pallas_call(
        kernel,
        grid_spec=pltpu.PrefetchScalarGridSpec(
            num_scalar_prefetch=1, grid=(N,), in_specs=specs, out_specs=out
        ),
        out_shape=jax.ShapeDtypeStruct((cols, rows), F32 if last is None else BF16),
        input_output_aliases=alias,
        compiler_params=PARAMS,
        cost_estimate=cost(cols, deep * count, rows, 0 if last is None else rows * cols),
    )(jnp.stack(which).astype(jnp.int32), *args)


def term_kernel(which_ref, x_ref, s_ref, o_ref):
    part = jnp.dot(s_ref[...], joined(x_ref), preferred_element_type=F32)

    @pl.when(pl.program_id(0) == 0)
    def _():
        o_ref[...] = part

    @pl.when(pl.program_id(0) > 0)
    def _():
        o_ref[...] += part


def term(x, s, block):
    blocks, rows, wide = x.shape
    cols = s.shape[0]
    tile = rows // 2
    per = blocks // N
    return pl.pallas_call(
        term_kernel,
        grid_spec=pltpu.PrefetchScalarGridSpec(
            num_scalar_prefetch=1,
            grid=(rows // tile,),
            in_specs=[
                pl.BlockSpec((per, tile, wide), lambda i, which: (which[0], i, 0)),
                pl.BlockSpec((cols, tile), lambda i, which: (0, i)),
            ],
            out_specs=pl.BlockSpec((cols, per * wide), lambda i, which: (0, 0)),
        ),
        out_shape=jax.ShapeDtypeStruct((cols, per * wide), F32),
        compiler_params=PARAMS,
        cost_estimate=cost(cols, rows, per * wide),
    )(jnp.reshape(block, (1,)).astype(jnp.int32), x, s)


def ring_sum(part, me):
    block = lambda step: part(lax.rem(me + step, N))
    far = block(2).astype(BF16)
    half = far.shape[0] // 2
    far_next, far_prev = shift(far[:half], "x", 1), shift(far[half:], "x", -1)
    to_next, to_prev = block(1), block(3)
    next_low = shift(to_next[half:].astype(BF16), "x", 1)
    prev_high = shift(to_prev[:half].astype(BF16), "x", -1)
    next_high = shift((to_next[:half] + far_next.astype(F32)).astype(BF16), "x", 1)
    prev_low = shift((to_prev[half:] + far_prev.astype(F32)).astype(BF16), "x", -1)
    own = block(0)
    high = own[:half] + next_high.astype(F32) + prev_high.astype(F32)
    low = own[half:] + next_low.astype(F32) + prev_low.astype(F32)
    return jnp.concatenate([high, low], axis=0)


def ring_gather(value, axis):
    half = value.shape[0] // 2
    high, low = value[:half], value[half:]
    prev_high, next_low = shift(high, axis, 1), shift(low, axis, -1)
    prev_low, next_high = shift(low, axis, 1), shift(high, axis, -1)
    far_high, far_low = shift(prev_high, axis, 1), shift(next_low, axis, -1)
    join = lambda a, b: jnp.concatenate([a, b], axis=0)
    return [value, join(next_high, next_low), join(far_high, far_low), join(prev_high, prev_low)]


def ring_swap(chunk, axis):
    far = chunk(2)
    half = far.shape[0] // 2
    from_prev, from_next = shift(chunk(1), axis, 1), shift(chunk(3), axis, -1)
    far_high = shift(shift(far[:half], axis, 1), axis, 1)
    far_low = shift(shift(far[half:], axis, -1), axis, -1)
    return [chunk(0), from_next, jnp.concatenate([far_high, far_low], axis=0), from_prev]


def in_order(pieces, me):
    twice = jnp.stack(pieces + pieces)
    return lax.dynamic_slice_in_dim(twice, lax.rem(N - me, N), N, axis=0)


def total_of(value):
    total = jnp.full((8, 128), jnp.sum(value * value), F32)
    total = total + lax.ppermute(total, "c", [(0, 1), (1, 0)])
    each = lax.all_to_all(
        jnp.broadcast_to(total[:1], (N * N * N, 128)), ("x", "y", "z"), split_axis=0, concat_axis=0, tiled=True
    )
    return jnp.sum(each[:, 0])


def per_device(tokens, target, weight):
    ix, iy = lax.axis_index("x"), lax.axis_index("y")
    rows, wide = tokens.shape
    cols = weight.shape[1] // N
    width = wide * 2 * N
    hidden_all = weight.shape[1] * 2 * N

    x = lax.all_gather(tokens, ("z", "c", "y"), axis=0, tiled=True).reshape(2 * N, N * rows, wide)

    def columns(array):
        return lambda k: lax.dynamic_slice_in_dim(array, lax.rem(iy + k, N) * cols, cols, axis=1)

    w_rows = in_order(ring_swap(columns(weight), "y"), iy).reshape(-1, cols)
    w = in_order(ring_gather(w_rows.T, "x"), ix)
    w = jnp.concatenate([w[k] for k in range(N)], axis=1)
    t = in_order(ring_swap(columns(target), "y"), iy)
    t = jnp.concatenate([t[k].T for k in range(N)], axis=1)

    hidden, slope = first_slopes(x, w, t)
    first = ring_sum(lambda b: term(x, slope, b), ix)
    own, after, far, before = ring_gather(first.astype(BF16), "x")
    scale = 0.5 * math.sqrt(hidden_all) / jnp.sqrt(total_of(first) + 1e-06)
    at = lambda k: lax.rem(ix + k, N)
    part = moved(x, [own], [at(0)])
    part = moved(x, [after, before], [at(1), at(3)], part)
    slope = moved(x, [far], [at(2)], part, (scale.reshape(1, 1), hidden, t))
    second = ring_sum(lambda b: term(x, slope, b), ix)
    total = total_of(second)
    factor = jnp.minimum(1.0, math.sqrt(width * hidden_all) / jnp.sqrt(total + 1e-06))
    held = second.astype(BF16).T.reshape(N, -1, cols)
    parts = in_order(ring_swap(lambda k: lax.dynamic_index_in_dim(held, lax.rem(iy + k, N), 0, keepdims=False), "y"), iy)
    whole = jnp.concatenate([parts[k] for k in range(N)], axis=1)
    return whole.astype(F32) * factor


def solution(mesh):
    grid = Mesh(mesh.devices.reshape(N, N, N, 2), ("x", "y", "z", "c"))
    spec = P(("x", "y"), ("z", "c"))
    return jax.shard_map(
        per_device, mesh=grid, in_specs=(spec, spec, spec), out_specs=spec, check_vma=False
    )
```

```python
import math

import jax
import jax.numpy as jnp
from jax import lax
from jax.experimental import pallas as pl
from jax.experimental.pallas import tpu as pltpu
from jax.sharding import Mesh, PartitionSpec as P

BF16, F32 = jnp.bfloat16, jnp.float32
N = 4
NT = (((1,), (1,)), ((), ()))
PARAMS = pltpu.CompilerParams(vmem_limit_bytes=52 << 20)


def shift(value, axis, step):
    return lax.ppermute(value, axis, [(i, (i + step) % N) for i in range(N)])


def slope_of(hidden, target):
    root = math.sqrt(2.0 / math.pi)
    square = hidden * hidden
    bend = jnp.tanh(hidden * (root + (root * 0.044715) * square))
    half = 0.5 + 0.5 * bend
    deriv = half + (hidden * (1.0 - bend * bend)) * (0.5 * root + (1.5 * root * 0.044715) * square)
    return ((hidden * half - target.astype(F32)) * deriv).astype(BF16)


def joined(x_ref):
    return jnp.concatenate([x_ref[k] for k in range(x_ref.shape[0])], axis=1)


def cost(rows, deep, cols, exps=0):
    return pl.CostEstimate(
        flops=2 * rows * deep * cols, bytes_accessed=2 * deep * (rows + cols) + 4 * rows * cols, transcendentals=exps
    )


def arrived_kernel(block, started, last, which_ref, *refs):
    mine, theirs, w_ref = refs[:N], refs[N : 2 * N], refs[2 * N]
    rest = list(refs[2 * N + 1 :])
    if started:
        rest.pop(0)
        part_ref = rest.pop(0)
    if last:
        target_ref = rest.pop(0)
    x_ref, h_ref = rest[:2]
    for k in range(N):

        @pl.when(pl.program_id(0) == k)
        def _():
            x = jnp.concatenate([mine[k][...], theirs[k][...]], axis=1)
            x_ref[0] = x
            hidden = lax.dot_general(w_ref[0], x, NT, preferred_element_type=F32)
            if started:
                hidden = hidden + part_ref[...]
            h_ref[...] = hidden
            if last:
                rest[2][...] = slope_of(hidden, target_ref[...])


def arrived(block, mine, theirs, w, which, held=None, target=None):
    tile, wide = mine[0].shape
    cols = w.shape[1]
    rows = N * tile
    whole = lambda shape: pl.BlockSpec(shape, lambda i, which: (0,) * len(shape))
    out = pl.BlockSpec((cols, tile), lambda i, which: (0, i))
    specs = [whole((tile, wide))] * (2 * N) + [pl.BlockSpec((1, cols, 2 * wide), lambda i, which: (which[0], 0, 0))]
    args = list(mine) + list(theirs) + [w]
    alias = {}
    if held is not None:
        alias = {1 + len(args): 0, 2 + len(args): 1}
        specs += [pl.BlockSpec(memory_space=pl.ANY), out]
        args += list(held)
    if target is not None:
        specs.append(out)
        args.append(target)
    out_specs = [pl.BlockSpec((1, tile, 2 * wide), lambda i, which: (block, i, 0)), out]
    out_shape = [jax.ShapeDtypeStruct((N, rows, 2 * wide), BF16), jax.ShapeDtypeStruct((cols, rows), F32)]
    if target is not None:
        out_specs.append(out)
        out_shape.append(jax.ShapeDtypeStruct((cols, rows), BF16))

    def kernel(*refs):
        arrived_kernel(block, held is not None, target is not None, *refs)

    return pl.pallas_call(
        kernel,
        grid_spec=pltpu.PrefetchScalarGridSpec(
            num_scalar_prefetch=1, grid=(N,), in_specs=specs, out_specs=out_specs
        ),
        out_shape=out_shape,
        input_output_aliases=alias,
        compiler_params=PARAMS,
        cost_estimate=cost(cols, 2 * wide, rows, 0 if target is None else rows * cols),
    )(jnp.reshape(which, (1,)).astype(jnp.int32), *args)


def moved_kernel(count, started, last, *refs):
    refs = list(refs[1:])
    xs, fs = refs[:count], refs[count : 2 * count]
    rest = refs[2 * count :]
    part = sum(
        lax.dot_general(f[...], joined(x), NT, preferred_element_type=F32) for x, f in zip(xs, fs)
    )
    if started:
        part = part + rest.pop(0)[...]
    if last:
        scale, hidden, target, out = rest
        out[...] = slope_of(hidden[...] + scale[0, 0] * part, target[...])
    else:
        rest[0][...] = part


def moved(x, pieces, which, part=None, last=None):
    blocks, rows, wide = x.shape
    cols, deep = pieces[0].shape
    per = deep // wide
    tile = rows // N
    count = len(pieces)
    at = lambda j: pl.BlockSpec((per, tile, wide), lambda i, which: (which[j], i, 0))
    out = pl.BlockSpec((cols, tile), lambda i, which: (0, i))
    specs = [at(j) for j in range(count)] + [pl.BlockSpec((cols, deep), lambda i, which: (0, 0))] * count
    args = [x] * count + list(pieces)
    alias = {}
    if part is not None:
        if last is None:
            alias = {1 + len(args): 0}
        specs.append(out)
        args.append(part)
    if last is not None:
        specs += [pl.BlockSpec(memory_space=pltpu.SMEM), out, out]
        args += list(last)

    def kernel(*refs):
        moved_kernel(count, part is not None, last is not None, *refs)

    return pl.pallas_call(
        kernel,
        grid_spec=pltpu.PrefetchScalarGridSpec(
            num_scalar_prefetch=1, grid=(N,), in_specs=specs, out_specs=out
        ),
        out_shape=jax.ShapeDtypeStruct((cols, rows), F32 if last is None else BF16),
        input_output_aliases=alias,
        compiler_params=PARAMS,
        cost_estimate=cost(cols, deep * count, rows, 0 if last is None else rows * cols),
    )(jnp.stack(which).astype(jnp.int32), *args)


def term_kernel(which_ref, x_ref, s_ref, o_ref):
    part = jnp.dot(s_ref[...], joined(x_ref), preferred_element_type=F32)

    @pl.when(pl.program_id(0) == 0)
    def _():
        o_ref[...] = part

    @pl.when(pl.program_id(0) > 0)
    def _():
        o_ref[...] += part


def term(x, s, block):
    blocks, rows, wide = x.shape
    cols = s.shape[0]
    tile = rows // 2
    per = blocks // N
    return pl.pallas_call(
        term_kernel,
        grid_spec=pltpu.PrefetchScalarGridSpec(
            num_scalar_prefetch=1,
            grid=(rows // tile,),
            in_specs=[
                pl.BlockSpec((per, tile, wide), lambda i, which: (which[0], i, 0)),
                pl.BlockSpec((cols, tile), lambda i, which: (0, i)),
            ],
            out_specs=pl.BlockSpec((cols, per * wide), lambda i, which: (0, 0)),
        ),
        out_shape=jax.ShapeDtypeStruct((cols, per * wide), F32),
        compiler_params=PARAMS,
        cost_estimate=cost(cols, rows, per * wide),
    )(jnp.reshape(block, (1,)).astype(jnp.int32), x, s)


def ring_sum(block):
    far = block(2).astype(BF16)
    half = far.shape[0] // 2
    far_next, far_prev = shift(far[:half], "x", 1), shift(far[half:], "x", -1)
    to_next, to_prev = block(1), block(3)
    next_low = shift(to_next[half:].astype(BF16), "x", 1)
    prev_high = shift(to_prev[:half].astype(BF16), "x", -1)
    next_high = shift((to_next[:half] + far_next.astype(F32)).astype(BF16), "x", 1)
    prev_low = shift((to_prev[half:] + far_prev.astype(F32)).astype(BF16), "x", -1)
    own = block(0)
    high = own[:half] + next_high.astype(F32) + prev_high.astype(F32)
    low = own[half:] + next_low.astype(F32) + prev_low.astype(F32)
    return jnp.concatenate([high, low], axis=0)


def ring_gather(value, axis):
    half = value.shape[0] // 2
    high, low = value[:half], value[half:]
    prev_high, next_low = shift(high, axis, 1), shift(low, axis, -1)
    prev_low, next_high = shift(low, axis, 1), shift(high, axis, -1)
    far_high, far_low = shift(prev_high, axis, 1), shift(next_low, axis, -1)
    join = lambda a, b: jnp.concatenate([a, b], axis=0)
    return [value, join(next_high, next_low), join(far_high, far_low), join(prev_high, prev_low)]


def ring_swap(chunk, axis):
    return [chunk(0), shift(chunk(3), axis, -1), shift(chunk(2), axis, 2), shift(chunk(1), axis, 1)]


def in_order(pieces, me):
    twice = jnp.stack(pieces + pieces)
    return lax.dynamic_slice_in_dim(twice, lax.rem(N - me, N), N, axis=0)


def total_of(value):
    total = jnp.full((8, 128), jnp.sum(value * value), F32)
    total = total + lax.ppermute(total, "c", [(0, 1), (1, 0)])
    each = lax.all_to_all(
        jnp.broadcast_to(total[:1], (N * N * N, 128)), ("x", "y", "z"), split_axis=0, concat_axis=0, tiled=True
    )
    return jnp.sum(each[:, 0])


def per_device(tokens, target, weight):
    ix, iy, iz, ic = (lax.axis_index(axis) for axis in ("x", "y", "z", "c"))
    wide = tokens.shape[1]
    cols = weight.shape[1] // N
    width = wide * 2 * N
    hidden_all = weight.shape[1] * 2 * N

    def columns(array):
        return lambda k: lax.dynamic_slice_in_dim(array, lax.rem(iy + k, N) * cols, cols, axis=1)

    groups = [tokens, shift(tokens, "y", -1), shift(tokens, "y", 1)]
    groups.append(shift(groups[2], "y", 1))
    after = [shift(piece, "z", -1) for piece in groups]
    before = [shift(piece, "z", 1) for piece in groups]
    far = [shift(before[k], "z", 1) if k % 2 == 0 else shift(after[k], "z", -1) for k in range(N)]
    other = lambda pieces: [lax.ppermute(piece, "c", [(0, 1), (1, 0)]) for piece in pieces]

    w_rows = in_order(ring_swap(columns(weight), "y"), lax.rem(iy + 2 * ic, N)).reshape(-1, cols)
    w = jnp.stack(ring_gather(w_rows.T, "x"))
    own_t = columns(target)
    far_t = shift(shift(own_t(2), "y", -1), "y", -1)
    t = jnp.concatenate(
        [part.T for part in (own_t(0), shift(own_t(3), "y", -1), shift(own_t(1), "y", 1), far_t)], axis=1
    )

    place = lambda k: lax.rem(iz + k + N - ix, N)
    held = arrived(0, groups, other(groups), w, place(0))
    held = arrived(1, after, other(after), w, place(1), held)
    held = arrived(3, before, other(before), w, place(3), held)
    x, hidden, slope = arrived(2, far, other(far), w, place(2), held, t)
    at = lambda k: lax.rem(ix + k + N - iz, N)
    first = ring_sum(lambda k: term(x, slope, at(k)))
    own, after, far, before = ring_gather(first.astype(BF16), "x")
    scale = 0.5 * math.sqrt(hidden_all) / jnp.sqrt(total_of(first) + 1e-06)
    part = moved(x, [own], [at(0)])
    part = moved(x, [after, before], [at(1), at(3)], part)
    slope = moved(x, [far], [at(2)], part, (scale.reshape(1, 1), hidden, t))
    second = ring_sum(lambda k: term(x, slope, at(k)))
    total = total_of(second)
    factor = jnp.minimum(1.0, math.sqrt(width * hidden_all) / jnp.sqrt(total + 1e-06))
    held = second.astype(BF16).T.reshape(N, -1, cols)
    parts = in_order(ring_swap(lambda k: lax.dynamic_index_in_dim(held, lax.rem(iy + k + 2 * ic, N), 0, keepdims=False), "y"), iy)
    whole = jnp.concatenate([parts[k] for k in range(N)], axis=1)
    return whole.astype(F32) * factor


def solution(mesh):
    grid = Mesh(mesh.devices.reshape(N, N, N, 2), ("x", "y", "z", "c"))
    spec = P(("x", "y"), ("z", "c"))
    return jax.shard_map(
        per_device, mesh=grid, in_specs=(spec, spec, spec), out_specs=spec, check_vma=False
    )
```

```python
import math

import jax
import jax.numpy as jnp
from jax import lax
from jax.experimental import pallas as pl
from jax.experimental.pallas import tpu as pltpu
from jax.sharding import Mesh, PartitionSpec as P

BF16, F32 = jnp.bfloat16, jnp.float32
N = 4
NT = (((1,), (1,)), ((), ()))
PARAMS = pltpu.CompilerParams(vmem_limit_bytes=52 << 20)


def shift(value, axis, step):
    return lax.ppermute(value, axis, [(i, (i + step) % N) for i in range(N)])


def slope_of(hidden, target):
    root = math.sqrt(2.0 / math.pi)
    square = hidden * hidden
    bend = jnp.tanh(hidden * (root + (root * 0.044715) * square))
    half = 0.5 + 0.5 * bend
    deriv = half + (hidden * (1.0 - bend * bend)) * (0.5 * root + (1.5 * root * 0.044715) * square)
    return ((hidden * half - target.astype(F32)) * deriv).astype(BF16)


def joined(x_ref):
    return jnp.concatenate([x_ref[k] for k in range(x_ref.shape[0])], axis=1)


def cost(rows, deep, cols, exps=0):
    return pl.CostEstimate(
        flops=2 * rows * deep * cols, bytes_accessed=2 * deep * (rows + cols) + 4 * rows * cols, transcendentals=exps
    )


def first_kernel(x_ref, w_ref, t_ref, h_ref, s_ref):
    hidden = lax.dot_general(w_ref[...], joined(x_ref), NT, preferred_element_type=F32)
    h_ref[...] = hidden
    s_ref[...] = slope_of(hidden, t_ref[...])


def first_slopes(x, w, t):
    blocks, rows, wide = x.shape
    cols = w.shape[0]
    tile = rows // N
    out = pl.BlockSpec((cols, tile), lambda i: (0, i))
    return pl.pallas_call(
        first_kernel,
        grid=(N,),
        in_specs=[
            pl.BlockSpec((blocks, tile, wide), lambda i: (0, i, 0)),
            pl.BlockSpec(w.shape, lambda i: (0, 0)),
            out,
        ],
        out_specs=[out, out],
        out_shape=[jax.ShapeDtypeStruct((cols, rows), F32), jax.ShapeDtypeStruct((cols, rows), BF16)],
        compiler_params=PARAMS,
        cost_estimate=cost(cols, blocks * wide, rows, rows * cols),
    )(x, w, t)


def moved_kernel(count, started, last, *refs):
    refs = list(refs[1:])
    xs, fs = refs[:count], refs[count : 2 * count]
    rest = refs[2 * count :]
    part = sum(
        lax.dot_general(f[...], joined(x), NT, preferred_element_type=F32) for x, f in zip(xs, fs)
    )
    if started:
        part = part + rest.pop(0)[...]
    if last:
        scale, hidden, target, out = rest
        out[...] = slope_of(hidden[...] + scale[0, 0] * part, target[...])
    else:
        rest[0][...] = part


def moved(x, pieces, which, part=None, last=None):
    blocks, rows, wide = x.shape
    cols, deep = pieces[0].shape
    per = deep // wide
    tile = rows // N
    count = len(pieces)
    at = lambda j: pl.BlockSpec((per, tile, wide), lambda i, which: (which[j], i, 0))
    out = pl.BlockSpec((cols, tile), lambda i, which: (0, i))
    specs = [at(j) for j in range(count)] + [pl.BlockSpec((cols, deep), lambda i, which: (0, 0))] * count
    args = [x] * count + list(pieces)
    alias = {}
    if part is not None:
        if last is None:
            alias = {1 + len(args): 0}
        specs.append(out)
        args.append(part)
    if last is not None:
        specs += [pl.BlockSpec(memory_space=pltpu.SMEM), out, out]
        args += list(last)

    def kernel(*refs):
        moved_kernel(count, part is not None, last is not None, *refs)

    return pl.pallas_call(
        kernel,
        grid_spec=pltpu.PrefetchScalarGridSpec(
            num_scalar_prefetch=1, grid=(N,), in_specs=specs, out_specs=out
        ),
        out_shape=jax.ShapeDtypeStruct((cols, rows), F32 if last is None else BF16),
        input_output_aliases=alias,
        compiler_params=PARAMS,
        cost_estimate=cost(cols, deep * count, rows, 0 if last is None else rows * cols),
    )(jnp.stack(which).astype(jnp.int32), *args)


def term_kernel(which_ref, x_ref, s_ref, o_ref):
    part = jnp.dot(s_ref[...], joined(x_ref), preferred_element_type=F32)

    @pl.when(pl.program_id(0) == 0)
    def _():
        o_ref[...] = part

    @pl.when(pl.program_id(0) > 0)
    def _():
        o_ref[...] += part


def term(x, s, block):
    blocks, rows, wide = x.shape
    cols = s.shape[0]
    tile = rows // 2
    per = blocks // N
    return pl.pallas_call(
        term_kernel,
        grid_spec=pltpu.PrefetchScalarGridSpec(
            num_scalar_prefetch=1,
            grid=(rows // tile,),
            in_specs=[
                pl.BlockSpec((per, tile, wide), lambda i, which: (which[0], i, 0)),
                pl.BlockSpec((cols, tile), lambda i, which: (0, i)),
            ],
            out_specs=pl.BlockSpec((cols, per * wide), lambda i, which: (0, 0)),
        ),
        out_shape=jax.ShapeDtypeStruct((cols, per * wide), F32),
        compiler_params=PARAMS,
        cost_estimate=cost(cols, rows, per * wide),
    )(jnp.reshape(block, (1,)).astype(jnp.int32), x, s)


def ring_sum(part, me):
    block = lambda step: part(lax.rem(me + step, N))
    far = block(2).astype(BF16)
    half = far.shape[0] // 2
    far_next, far_prev = shift(far[:half], "x", 1), shift(far[half:], "x", -1)
    to_next, to_prev = block(1), block(3)
    next_low = shift(to_next[half:].astype(BF16), "x", 1)
    prev_high = shift(to_prev[:half].astype(BF16), "x", -1)
    next_high = shift((to_next[:half] + far_next.astype(F32)).astype(BF16), "x", 1)
    prev_low = shift((to_prev[half:] + far_prev.astype(F32)).astype(BF16), "x", -1)
    own = block(0)
    high = own[:half] + next_high.astype(F32) + prev_high.astype(F32)
    low = own[half:] + next_low.astype(F32) + prev_low.astype(F32)
    return jnp.concatenate([high, low], axis=0)


def ring_gather(value, axis):
    return [value, shift(value, axis, -1), shift(value, axis, 2), shift(value, axis, 1)]


def ring_swap(chunk, axis):
    return [chunk(0), shift(chunk(3), axis, -1), shift(chunk(2), axis, 2), shift(chunk(1), axis, 1)]


def in_order(pieces, me):
    twice = jnp.stack(pieces + pieces)
    return lax.dynamic_slice_in_dim(twice, lax.rem(N - me, N), N, axis=0)


def total_of(value):
    total = jnp.full((8, 128), jnp.sum(value * value), F32)
    total = total + lax.ppermute(total, "c", [(0, 1), (1, 0)])
    each = lax.all_to_all(
        jnp.broadcast_to(total[:1], (N * N * N, 128)), ("x", "y", "z"), split_axis=0, concat_axis=0, tiled=True
    )
    return jnp.sum(each[:, 0])


def per_device(tokens, target, weight):
    ix, iy = lax.axis_index("x"), lax.axis_index("y")
    rows, wide = tokens.shape
    cols = weight.shape[1] // N
    width = wide * 2 * N
    hidden_all = weight.shape[1] * 2 * N

    x = lax.all_gather(tokens, ("z", "c", "y"), axis=0, tiled=True).reshape(2 * N, N * rows, wide)

    def columns(array):
        return lambda k: lax.dynamic_slice_in_dim(array, lax.rem(iy + k, N) * cols, cols, axis=1)

    w_rows = in_order(ring_swap(columns(weight), "y"), iy).reshape(-1, cols)
    w = in_order(ring_gather(w_rows.T, "x"), ix)
    w = jnp.concatenate([w[k] for k in range(N)], axis=1)
    t = in_order(ring_swap(columns(target), "y"), iy)
    t = jnp.concatenate([t[k].T for k in range(N)], axis=1)

    hidden, slope = first_slopes(x, w, t)
    first = ring_sum(lambda b: term(x, slope, b), ix)
    own, after, far, before = ring_gather(first.astype(BF16), "x")
    scale = 0.5 * math.sqrt(hidden_all) / jnp.sqrt(total_of(first) + 1e-06)
    at = lambda k: lax.rem(ix + k, N)
    part = moved(x, [own, after, before], [at(0), at(1), at(3)])
    slope = moved(x, [far], [at(2)], part, (scale.reshape(1, 1), hidden, t))
    second = ring_sum(lambda b: term(x, slope, b), ix)
    total = total_of(second)
    factor = jnp.minimum(1.0, math.sqrt(width * hidden_all) / jnp.sqrt(total + 1e-06))
    held = second.astype(BF16).T.reshape(N, -1, cols)
    parts = in_order(ring_swap(lambda k: lax.dynamic_index_in_dim(held, lax.rem(iy + k, N), 0, keepdims=False), "y"), iy)
    whole = jnp.concatenate([parts[k] for k in range(N)], axis=1)
    return whole.astype(F32) * factor


def solution(mesh):
    grid = Mesh(mesh.devices.reshape(N, N, N, 2), ("x", "y", "z", "c"))
    spec = P(("x", "y"), ("z", "c"))
    return jax.shard_map(
        per_device, mesh=grid, in_specs=(spec, spec, spec), out_specs=spec, check_vma=False
    )
```

```python
import math

import jax
import jax.numpy as jnp
from jax import lax
from jax.experimental import pallas as pl
from jax.experimental.pallas import tpu as pltpu
from jax.sharding import Mesh, PartitionSpec as P

BF16, F32 = jnp.bfloat16, jnp.float32
N = 4
NT = (((1,), (1,)), ((), ()))
PARAMS = pltpu.CompilerParams(vmem_limit_bytes=52 << 20)


def shift(value, axis, step):
    return lax.ppermute(value, axis, [(i, (i + step) % N) for i in range(N)])


def core(value):
    return lax.ppermute(value, "c", [(0, 1), (1, 0)])


def behind(value, *others):
    return lax.optimization_barrier((value, *others))[0]


def slope_of(hidden, target):
    root = math.sqrt(2.0 / math.pi)
    square = hidden * hidden
    bend = jnp.tanh(hidden * (root + (root * 0.044715) * square))
    half = 0.5 + 0.5 * bend
    deriv = half + (hidden * (1.0 - bend * bend)) * (0.5 * root + (1.5 * root * 0.044715) * square)
    return ((hidden * half - target.astype(F32)) * deriv).astype(BF16)


def cost(rows, deep, cols, exps=0):
    return pl.CostEstimate(
        flops=2 * rows * deep * cols, bytes_accessed=2 * deep * (rows + cols) + 4 * rows * cols, transcendentals=exps
    )


def arrived(blocks, pieces, w, which, held=None, target=None):
    small, deep = pieces[0][0].shape
    cols = w.shape[1]
    tile = 2 * small
    rows = 2 * tile
    count = len(blocks)
    once = lambda shape: pl.BlockSpec(shape, lambda i, which: (0,) * len(shape), pipeline_mode=pl.Buffered(1))
    out = pl.BlockSpec((cols, tile), lambda i, which: (0, i))
    specs = [once(piece.shape) for three in pieces for piece in three] + [once(w.shape)]
    args = [piece for three in pieces for piece in three] + [w]
    alias = {}
    if held is not None:
        alias = {1 + len(args): 0, 2 + len(args): 1}
        specs += [pl.BlockSpec(memory_space=pl.ANY), out]
        args += list(held)
    if target is not None:
        specs.append(out)
        args.append(target)
    start = min(blocks)
    if count > 1:
        x_spec = pl.BlockSpec((N, tile, deep), lambda i, which: (0, i, 0))
    else:
        x_spec = pl.BlockSpec((1, tile, deep), lambda i, which: (start, i, 0))
    out_specs = [x_spec, out]
    out_shape = [jax.ShapeDtypeStruct((N, rows, deep), BF16), jax.ShapeDtypeStruct((cols, rows), F32)]
    if target is not None:
        out_specs.append(out)
        out_shape.append(jax.ShapeDtypeStruct((cols, rows), BF16))

    def kernel(which_ref, *refs):
        parts, w_ref = refs[: 3 * count], refs[3 * count]
        rest = list(refs[3 * count + 1 :])
        before = None
        if held is not None:
            rest.pop(0)
            before = rest.pop(0)
        target_ref = rest.pop(0) if target is not None else None
        x_ref, h_ref = rest[:2]
        for step in range(2):

            @pl.when(pl.program_id(0) == step)
            def _():
                hidden = None if before is None else before[...]
                for n, block in enumerate(blocks):
                    own, pair, far = parts[3 * n : 3 * n + 3]
                    x = jnp.concatenate([own[...], far[...]], axis=0) if step == 0 else pair[...]
                    x_ref[block if count > 1 else 0] = x
                    part = lax.dot_general(w_ref[which_ref[n]], x, NT, preferred_element_type=F32)
                    hidden = part if hidden is None else hidden + part
                h_ref[...] = hidden
                if target is not None:
                    rest[2][...] = slope_of(hidden, target_ref[...])

    return pl.pallas_call(
        kernel,
        grid_spec=pltpu.PrefetchScalarGridSpec(
            num_scalar_prefetch=1, grid=(2,), in_specs=specs, out_specs=out_specs
        ),
        out_shape=out_shape,
        input_output_aliases=alias,
        compiler_params=PARAMS,
        cost_estimate=cost(cols, deep * count, rows, 0 if target is None else rows * cols),
    )(jnp.stack(which).astype(jnp.int32), *args)


def swapped(value):
    half = value.shape[1] // 2
    return jnp.concatenate([value[:, half:], value[:, :half]], axis=1)


def moved(x, pieces, which, part=None, last=None):
    rows, deep = x.shape[1:]
    half = pieces[0][0].shape[0]
    cols = 2 * half
    tile = rows // N
    count = len(pieces)
    at = lambda j: pl.BlockSpec((1, tile, deep), lambda i, which: (which[j], i, 0))
    out = pl.BlockSpec((cols, tile), lambda i, which: (0, i))
    specs = [at(j) for j in range(count)]
    specs += [pl.BlockSpec((half, deep), lambda i, which: (0, 0), pipeline_mode=pl.Buffered(1))] * (2 * count)
    args = [x] * count + [half_of for pair in pieces for half_of in pair]
    if part is not None:
        specs.append(out)
        args.append(part)
    if last is not None:
        specs += [pl.BlockSpec(memory_space=pltpu.SMEM), out, out]
        args += list(last)

    def kernel(which_ref, *refs):
        xs, fs = refs[:count], refs[count : 3 * count]
        rest = list(refs[3 * count :])
        total = rest.pop(0)[...] if part is not None else None
        for j in range(count):
            f = jnp.concatenate([fs[2 * j][...], swapped(fs[2 * j + 1][...])], axis=0)
            more = lax.dot_general(f, xs[j][0], NT, preferred_element_type=F32)
            total = more if total is None else total + more
        if last is not None:
            scale, hidden, target, out_ref = rest
            out_ref[...] = slope_of(hidden[...] + scale[0, 0] * total, target[...])
        else:
            rest[0][...] = total

    return pl.pallas_call(
        kernel,
        grid_spec=pltpu.PrefetchScalarGridSpec(
            num_scalar_prefetch=1, grid=(N,), in_specs=specs, out_specs=out
        ),
        out_shape=jax.ShapeDtypeStruct((cols, rows), F32 if last is None else BF16),
        compiler_params=PARAMS,
        cost_estimate=cost(cols, deep * count, rows, 0 if last is None else rows * cols),
    )(jnp.stack(which).astype(jnp.int32), *args)


def term_kernel(which_ref, x_ref, s_ref, own_ref, other_ref, total_ref):
    part = jnp.dot(s_ref[...], x_ref[0], preferred_element_type=F32)
    half = own_ref.shape[0]

    @pl.when(pl.program_id(0) == 0)
    def _():
        total_ref[...] = part

    @pl.when(pl.program_id(0) == 1)
    def _():
        total = total_ref[...] + part
        own_ref[...] = total[:half]
        other_ref[...] = total[half:].astype(BF16)


def term(x, s, block):
    rows, deep = x.shape[1:]
    cols = s.shape[0]
    tile = rows // 2
    out = pl.BlockSpec((cols // 2, deep), lambda i, which: (0, 0))
    own, other = pl.pallas_call(
        term_kernel,
        grid_spec=pltpu.PrefetchScalarGridSpec(
            num_scalar_prefetch=1,
            grid=(2,),
            in_specs=[
                pl.BlockSpec((1, tile, deep), lambda i, which: (which[0], i, 0)),
                pl.BlockSpec((cols, tile), lambda i, which: (0, i)),
            ],
            out_specs=[out, out],
            scratch_shapes=[pltpu.VMEM((cols, deep), F32)],
        ),
        out_shape=[jax.ShapeDtypeStruct((cols // 2, deep), F32), jax.ShapeDtypeStruct((cols // 2, deep), BF16)],
        compiler_params=PARAMS,
        cost_estimate=cost(cols, rows, deep),
    )(jnp.reshape(block, (1,)).astype(jnp.int32), x, s)
    return own + swapped(core(other)).astype(F32)


def ring_sum(block):
    far = block(2, ()).astype(BF16)
    half = far.shape[0] // 2
    to_next = block(1, ())
    far_next, far_prev = shift(far[:half], "x", 1), shift(far[half:], "x", -1)
    to_prev = block(3, (far,))
    next_low = shift(to_next[half:].astype(BF16), "x", 1)
    prev_high = shift(to_prev[:half].astype(BF16), "x", -1)
    next_high = shift((to_next[:half] + far_next.astype(F32)).astype(BF16), "x", 1)
    prev_low = shift((to_prev[half:] + far_prev.astype(F32)).astype(BF16), "x", -1)
    own = block(0, (to_next,))
    high = own[:half] + next_high.astype(F32) + prev_high.astype(F32)
    low = own[half:] + next_low.astype(F32) + prev_low.astype(F32)
    return jnp.concatenate([high, low], axis=0)


def ring_gather(value, axis):
    return [value, shift(value, axis, -1), shift(value, axis, 2), shift(value, axis, 1)]


def ring_swap(chunk, axis):
    return [chunk(0), shift(chunk(3), axis, -1), shift(chunk(2), axis, 2), shift(chunk(1), axis, 1)]


def in_order(pieces, me):
    twice = jnp.stack(pieces + pieces)
    return lax.dynamic_slice_in_dim(twice, lax.rem(N - me, N), N, axis=0)


def total_of(value, beside):
    total = jnp.full((8, 128), jnp.sum(value * value), F32)
    total = total + core(total)
    each = lax.all_to_all(
        jnp.broadcast_to(total[:1], (N * N * N, 128)), ("x", "y", "z"), split_axis=0, concat_axis=0, tiled=True
    )
    if beside is not None:
        each, beside = lax.optimization_barrier((each, beside))
    return jnp.sum(each[:, 0]), beside


def per_device(tokens, target, weight):
    ix, iy, iz, ic = (lax.axis_index(axis) for axis in ("x", "y", "z", "c"))
    half = tokens.shape[0] // 2
    cols = weight.shape[1] // N
    width = tokens.shape[1] * 2 * N
    hidden_all = weight.shape[1] * 2 * N

    def shared(array):
        keep = lax.dynamic_slice_in_dim(array, ic * half, half, axis=0)
        return keep, core(lax.dynamic_slice_in_dim(array, (1 - ic) * half, half, axis=0))

    def chunk(pair):
        def part(k):
            at = lax.rem(iy + k, N) * cols
            return jnp.concatenate([lax.dynamic_slice_in_dim(array, at, cols, axis=1) for array in pair], axis=1)

        return part

    own = jnp.concatenate(shared(tokens), axis=1)
    after_y, before_y = shift(own, "y", -1), shift(own, "y", 1)
    near = (own, jnp.concatenate([after_y, before_y], axis=0), shift(behind(own, after_y, before_y), "y", 2))
    after = [shift(piece, "z", -1) for piece in near]
    before = [shift(piece, "z", 1) for piece in near]
    far = (shift(after[0], "z", -1), shift(before[1], "z", 1), shift(after[2], "z", -1))

    w_rows = in_order(ring_swap(chunk((weight, core(weight))), "y"), lax.rem(iy + 2 * ic, N))
    w = jnp.stack(ring_gather(w_rows.reshape(-1, 2 * cols).T, "x"))
    keep, other = shared(target)
    t_own, t_after, t_far, t_before = ring_swap(chunk((behind(keep, near[2]), other)), "y")
    t = jnp.concatenate([part.T for part in (t_own, t_far, t_after, t_before)], axis=1)

    place = lambda k: lax.rem(iz + k + N - ix, N)
    held = arrived((0, 1, 3), (near, after, before), w, [place(0), place(1), place(3)])
    x, hidden, slope = arrived((2,), (far,), w, [place(2)], held, t)
    at = lambda k: lax.rem(ix + k + N - iz, N)
    first = ring_sum(lambda k, others: term(x, behind(slope, *others), at(k)))
    blocks = [(block, core(block)) for block in ring_gather(first.astype(BF16), "x")]
    part = moved(x, [blocks[0], blocks[1], blocks[3]], [at(0), at(1), at(3)])
    total, part = total_of(first, part)
    scale = 0.5 * math.sqrt(hidden_all) / jnp.sqrt(total + 1e-06)
    slope = moved(x, [blocks[2]], [at(2)], part, (scale.reshape(1, 1), hidden, t))
    second = ring_sum(lambda k, others: term(x, behind(slope, *others), at(k)))
    total, _ = total_of(second, None)
    factor = jnp.minimum(1.0, math.sqrt(width * hidden_all) / jnp.sqrt(total + 1e-06))
    held = second.astype(BF16).T.reshape(N, -1, cols)
    parts = in_order(ring_swap(lambda k: lax.dynamic_index_in_dim(held, lax.rem(iy + k + 2 * ic, N), 0, keepdims=False), "y"), iy)
    whole = jnp.concatenate([parts[k] for k in range(N)], axis=1)
    return whole.astype(F32) * factor


def solution(mesh):
    grid = Mesh(mesh.devices.reshape(N, N, N, 2), ("x", "y", "z", "c"))
    spec = P(("x", "y"), ("z", "c"))
    return jax.shard_map(
        per_device, mesh=grid, in_specs=(spec, spec, spec), out_specs=spec, check_vma=False
    )
```

```python
import math

import jax
import jax.numpy as jnp
from jax import lax
from jax.experimental import pallas as pl
from jax.experimental.pallas import tpu as pltpu
from jax.sharding import Mesh, PartitionSpec as P

BF16, F32 = jnp.bfloat16, jnp.float32
N = 4
NT = (((1,), (1,)), ((), ()))
PARAMS = pltpu.CompilerParams(vmem_limit_bytes=52 << 20)


def shift(value, axis, step):
    return lax.ppermute(value, axis, [(i, (i + step) % N) for i in range(N)])


def behind(value, *others):
    return lax.optimization_barrier((value, *others))[0]


def slope_of(hidden, target):
    root = math.sqrt(2.0 / math.pi)
    square = hidden * hidden
    bend = jnp.tanh(hidden * (root + (root * 0.044715) * square))
    half = 0.5 + 0.5 * bend
    deriv = half + (hidden * (1.0 - bend * bend)) * (0.5 * root + (1.5 * root * 0.044715) * square)
    return ((hidden * half - target.astype(F32)) * deriv).astype(BF16)


def joined(x_ref):
    return jnp.concatenate([x_ref[k] for k in range(x_ref.shape[0])], axis=1)


def cost(rows, deep, cols, exps=0):
    return pl.CostEstimate(
        flops=2 * rows * deep * cols, bytes_accessed=2 * deep * (rows + cols) + 4 * rows * cols, transcendentals=exps
    )


def first_kernel(x_ref, w_ref, t_ref, h_ref, s_ref):
    hidden = lax.dot_general(w_ref[...], joined(x_ref), NT, preferred_element_type=F32)
    h_ref[...] = hidden
    s_ref[...] = slope_of(hidden, t_ref[...])


def first_slopes(x, w, t):
    blocks, rows, wide = x.shape
    cols = w.shape[0]
    tile = rows // N
    out = pl.BlockSpec((cols, tile), lambda i: (0, i))
    return pl.pallas_call(
        first_kernel,
        grid=(N,),
        in_specs=[
            pl.BlockSpec((blocks, tile, wide), lambda i: (0, i, 0)),
            pl.BlockSpec(w.shape, lambda i: (0, 0)),
            out,
        ],
        out_specs=[out, out],
        out_shape=[jax.ShapeDtypeStruct((cols, rows), F32), jax.ShapeDtypeStruct((cols, rows), BF16)],
        compiler_params=PARAMS,
        cost_estimate=cost(cols, blocks * wide, rows, rows * cols),
    )(x, w, t)


def moved_kernel(count, started, last, *refs):
    refs = list(refs[1:])
    xs, fs = refs[:count], refs[count : 2 * count]
    rest = refs[2 * count :]
    part = sum(
        lax.dot_general(f[...], joined(x), NT, preferred_element_type=F32) for x, f in zip(xs, fs)
    )
    if started:
        part = part + rest.pop(0)[...]
    if last:
        scale, hidden, target, out = rest
        out[...] = slope_of(hidden[...] + scale[0, 0] * part, target[...])
    else:
        rest[0][...] = part


def moved(x, pieces, which, part=None, last=None):
    blocks, rows, wide = x.shape
    cols, deep = pieces[0].shape
    per = deep // wide
    tile = rows // N
    count = len(pieces)
    at = lambda j: pl.BlockSpec((per, tile, wide), lambda i, which: (which[j], i, 0))
    out = pl.BlockSpec((cols, tile), lambda i, which: (0, i))
    specs = [at(j) for j in range(count)] + [pl.BlockSpec((cols, deep), lambda i, which: (0, 0))] * count
    args = [x] * count + list(pieces)
    alias = {}
    if part is not None:
        if last is None:
            alias = {1 + len(args): 0}
        specs.append(out)
        args.append(part)
    if last is not None:
        specs += [pl.BlockSpec(memory_space=pltpu.SMEM), out, out]
        args += list(last)

    def kernel(*refs):
        moved_kernel(count, part is not None, last is not None, *refs)

    return pl.pallas_call(
        kernel,
        grid_spec=pltpu.PrefetchScalarGridSpec(
            num_scalar_prefetch=1, grid=(N,), in_specs=specs, out_specs=out
        ),
        out_shape=jax.ShapeDtypeStruct((cols, rows), F32 if last is None else BF16),
        input_output_aliases=alias,
        compiler_params=PARAMS,
        cost_estimate=cost(cols, deep * count, rows, 0 if last is None else rows * cols),
    )(jnp.stack(which).astype(jnp.int32), *args)


def term_kernel(which_ref, x_ref, s_ref, o_ref):
    part = jnp.dot(s_ref[...], joined(x_ref), preferred_element_type=F32)

    @pl.when(pl.program_id(0) == 0)
    def _():
        o_ref[...] = part

    @pl.when(pl.program_id(0) > 0)
    def _():
        o_ref[...] += part


def term(x, s, block):
    blocks, rows, wide = x.shape
    cols = s.shape[0]
    tile = rows // 2
    per = blocks // N
    return pl.pallas_call(
        term_kernel,
        grid_spec=pltpu.PrefetchScalarGridSpec(
            num_scalar_prefetch=1,
            grid=(rows // tile,),
            in_specs=[
                pl.BlockSpec((per, tile, wide), lambda i, which: (which[0], i, 0)),
                pl.BlockSpec((cols, tile), lambda i, which: (0, i)),
            ],
            out_specs=pl.BlockSpec((cols, per * wide), lambda i, which: (0, 0)),
        ),
        out_shape=jax.ShapeDtypeStruct((cols, per * wide), F32),
        compiler_params=PARAMS,
        cost_estimate=cost(cols, rows, per * wide),
    )(jnp.reshape(block, (1,)).astype(jnp.int32), x, s)


def ring_sum(part, me):
    block = lambda step: part(lax.rem(me + step, N))
    far = block(2).astype(BF16)
    half = far.shape[0] // 2
    far_next, far_prev = shift(far[:half], "x", 1), shift(far[half:], "x", -1)
    to_next, to_prev = block(1), block(3)
    next_low = shift(to_next[half:].astype(BF16), "x", 1)
    prev_high = shift(to_prev[:half].astype(BF16), "x", -1)
    next_high = shift((to_next[:half] + far_next.astype(F32)).astype(BF16), "x", 1)
    prev_low = shift((to_prev[half:] + far_prev.astype(F32)).astype(BF16), "x", -1)
    own = block(0)
    high = own[:half] + next_high.astype(F32) + prev_high.astype(F32)
    low = own[half:] + next_low.astype(F32) + prev_low.astype(F32)
    return jnp.concatenate([high, low], axis=0)


def ring_gather(value, axis):
    return [value, shift(value, axis, -1), shift(value, axis, 2), shift(value, axis, 1)]


def ring_swap(chunk, axis):
    return [chunk(0), shift(chunk(3), axis, -1), shift(chunk(2), axis, 2), shift(chunk(1), axis, 1)]


def ring_swap_halves(chunk, axis):
    far = chunk(2)
    half = far.shape[0] // 2
    rows = 2 * half
    prev = shift(jnp.concatenate([chunk(1), far[:half]], axis=0), axis, 1)
    after = shift(jnp.concatenate([chunk(3), far[half:]], axis=0), axis, -1)
    high, low = shift(prev[rows:], axis, 1), shift(after[rows:], axis, -1)
    return [chunk(0), after[:rows], jnp.concatenate([high, low], axis=0), prev[:rows]]


def in_order(pieces, me):
    twice = jnp.stack(pieces + pieces)
    return lax.dynamic_slice_in_dim(twice, lax.rem(N - me, N), N, axis=0)


def total_of(value, beside):
    total = jnp.full((8, 128), jnp.sum(value * value), F32)
    total = total + lax.ppermute(total, "c", [(0, 1), (1, 0)])
    each = lax.all_to_all(
        jnp.broadcast_to(total[:1], (N * N * N, 128)), ("x", "y", "z"), split_axis=0, concat_axis=0, tiled=True
    )
    if beside is not None:
        each, beside = lax.optimization_barrier((each, beside))
    return jnp.sum(each[:, 0]), beside


def per_device(tokens, target, weight):
    ix, iy = lax.axis_index("x"), lax.axis_index("y")
    rows, wide = tokens.shape
    cols = weight.shape[1] // N
    width = wide * 2 * N
    hidden_all = weight.shape[1] * 2 * N

    x = lax.all_gather(tokens, ("z", "c", "y"), axis=0, tiled=True).reshape(2 * N, N * rows, wide)

    def columns(array):
        return lambda k: lax.dynamic_slice_in_dim(array, lax.rem(iy + k, N) * cols, cols, axis=1)

    w_pieces = ring_swap(columns(weight), "y")
    w_rows = in_order(w_pieces, iy).reshape(-1, cols)
    w = in_order(ring_gather(w_rows.T, "x"), ix)
    w = jnp.concatenate([w[k] for k in range(N)], axis=1)
    t = in_order(ring_swap_halves(columns(behind(target, *w_pieces)), "y"), iy)
    t = jnp.concatenate([t[k].T for k in range(N)], axis=1)

    hidden, slope = first_slopes(x, w, t)
    first = ring_sum(lambda b: term(x, slope, b), ix)
    own, after, far, before = ring_gather(first.astype(BF16), "x")
    at = lambda k: lax.rem(ix + k, N)
    part = moved(x, [own, after, before], [at(0), at(1), at(3)])
    total, part = total_of(first, part)
    scale = 0.5 * math.sqrt(hidden_all) / jnp.sqrt(total + 1e-06)
    slope = moved(x, [far], [at(2)], part, (scale.reshape(1, 1), hidden, t))
    second = ring_sum(lambda b: term(x, slope, b), ix)
    total, _ = total_of(second, None)
    factor = jnp.minimum(1.0, math.sqrt(width * hidden_all) / jnp.sqrt(total + 1e-06))
    held = second.astype(BF16).T.reshape(N, -1, cols)
    parts = in_order(ring_swap(lambda k: lax.dynamic_index_in_dim(held, lax.rem(iy + k, N), 0, keepdims=False), "y"), iy)
    whole = jnp.concatenate([parts[k] for k in range(N)], axis=1)
    return whole.astype(F32) * factor


def solution(mesh):
    grid = Mesh(mesh.devices.reshape(N, N, N, 2), ("x", "y", "z", "c"))
    spec = P(("x", "y"), ("z", "c"))
    return jax.shard_map(
        per_device, mesh=grid, in_specs=(spec, spec, spec), out_specs=spec, check_vma=False
    )
```

```python
import math

import jax
import jax.numpy as jnp
from jax import lax
from jax.experimental import pallas as pl
from jax.experimental.pallas import tpu as pltpu
from jax.sharding import Mesh, PartitionSpec as P

BF16, F32 = jnp.bfloat16, jnp.float32
N = 4
NT = (((1,), (1,)), ((), ()))
PARAMS = pltpu.CompilerParams(vmem_limit_bytes=52 << 20)


def shift(value, axis, step):
    return lax.ppermute(value, axis, [(i, (i + step) % N) for i in range(N)])


def behind(value, *others):
    return lax.optimization_barrier((value, *others))[0]


def slope_of(hidden, target):
    root = math.sqrt(2.0 / math.pi)
    square = hidden * hidden
    bend = jnp.tanh(hidden * (root + (root * 0.044715) * square))
    half = 0.5 + 0.5 * bend
    deriv = half + (hidden * (1.0 - bend * bend)) * (0.5 * root + (1.5 * root * 0.044715) * square)
    return ((hidden * half - target.astype(F32)) * deriv).astype(BF16)


def joined(x_ref):
    return jnp.concatenate([x_ref[k] for k in range(x_ref.shape[0])], axis=1)


def cost(rows, deep, cols, exps=0):
    return pl.CostEstimate(
        flops=2 * rows * deep * cols, bytes_accessed=2 * deep * (rows + cols) + 4 * rows * cols, transcendentals=exps
    )


def first_kernel(x_ref, w_ref, t_ref, h_ref, s_ref):
    hidden = lax.dot_general(w_ref[...], joined(x_ref), NT, preferred_element_type=F32)
    h_ref[...] = hidden
    s_ref[...] = slope_of(hidden, t_ref[...])


def first_slopes(x, w, t):
    blocks, rows, wide = x.shape
    cols = w.shape[0]
    tile = rows // N
    out = pl.BlockSpec((cols, tile), lambda i: (0, i))
    return pl.pallas_call(
        first_kernel,
        grid=(N,),
        in_specs=[
            pl.BlockSpec((blocks, tile, wide), lambda i: (0, i, 0)),
            pl.BlockSpec(w.shape, lambda i: (0, 0)),
            out,
        ],
        out_specs=[out, out],
        out_shape=[jax.ShapeDtypeStruct((cols, rows), F32), jax.ShapeDtypeStruct((cols, rows), BF16)],
        compiler_params=PARAMS,
        cost_estimate=cost(cols, blocks * wide, rows, rows * cols),
    )(x, w, t)


def moved_kernel(count, started, last, *refs):
    refs = list(refs[1:])
    xs, fs = refs[:count], refs[count : 2 * count]
    rest = refs[2 * count :]
    part = sum(
        lax.dot_general(f[...], joined(x), NT, preferred_element_type=F32) for x, f in zip(xs, fs)
    )
    if started:
        part = part + rest.pop(0)[...]
    if last:
        scale, hidden, target, out = rest
        out[...] = slope_of(hidden[...] + scale[0, 0] * part, target[...])
    else:
        rest[0][...] = part


def moved(x, pieces, which, part=None, last=None):
    blocks, rows, wide = x.shape
    cols, deep = pieces[0].shape
    per = deep // wide
    tile = rows // N
    count = len(pieces)
    at = lambda j: pl.BlockSpec((per, tile, wide), lambda i, which: (which[j], i, 0))
    out = pl.BlockSpec((cols, tile), lambda i, which: (0, i))
    specs = [at(j) for j in range(count)] + [pl.BlockSpec((cols, deep), lambda i, which: (0, 0))] * count
    args = [x] * count + list(pieces)
    alias = {}
    if part is not None:
        if last is None:
            alias = {1 + len(args): 0}
        specs.append(out)
        args.append(part)
    if last is not None:
        specs += [pl.BlockSpec(memory_space=pltpu.SMEM), out, out]
        args += list(last)

    def kernel(*refs):
        moved_kernel(count, part is not None, last is not None, *refs)

    return pl.pallas_call(
        kernel,
        grid_spec=pltpu.PrefetchScalarGridSpec(
            num_scalar_prefetch=1, grid=(N,), in_specs=specs, out_specs=out
        ),
        out_shape=jax.ShapeDtypeStruct((cols, rows), F32 if last is None else BF16),
        input_output_aliases=alias,
        compiler_params=PARAMS,
        cost_estimate=cost(cols, deep * count, rows, 0 if last is None else rows * cols),
    )(jnp.stack(which).astype(jnp.int32), *args)


def term_kernel(which_ref, x_ref, s_ref, o_ref):
    part = jnp.dot(s_ref[...], joined(x_ref), preferred_element_type=F32)

    @pl.when(pl.program_id(0) == 0)
    def _():
        o_ref[...] = part

    @pl.when(pl.program_id(0) > 0)
    def _():
        o_ref[...] += part


def term(x, s, block):
    blocks, rows, wide = x.shape
    cols = s.shape[0]
    tile = rows // 2
    per = blocks // N
    return pl.pallas_call(
        term_kernel,
        grid_spec=pltpu.PrefetchScalarGridSpec(
            num_scalar_prefetch=1,
            grid=(rows // tile,),
            in_specs=[
                pl.BlockSpec((per, tile, wide), lambda i, which: (which[0], i, 0)),
                pl.BlockSpec((cols, tile), lambda i, which: (0, i)),
            ],
            out_specs=pl.BlockSpec((cols, per * wide), lambda i, which: (0, 0)),
        ),
        out_shape=jax.ShapeDtypeStruct((cols, per * wide), F32),
        compiler_params=PARAMS,
        cost_estimate=cost(cols, rows, per * wide),
    )(jnp.reshape(block, (1,)).astype(jnp.int32), x, s)


def ring_sum(part, me):
    block = lambda step: part(lax.rem(me + step, N))
    far = block(2).astype(BF16)
    half = far.shape[0] // 2
    far_next, far_prev = shift(far[:half], "x", 1), shift(far[half:], "x", -1)
    to_next, to_prev = block(1), block(3)
    next_low = shift(to_next[half:].astype(BF16), "x", 1)
    prev_high = shift(to_prev[:half].astype(BF16), "x", -1)
    next_high = shift((to_next[:half] + far_next.astype(F32)).astype(BF16), "x", 1)
    prev_low = shift((to_prev[half:] + far_prev.astype(F32)).astype(BF16), "x", -1)
    own = block(0)
    high = own[:half] + next_high.astype(F32) + prev_high.astype(F32)
    low = own[half:] + next_low.astype(F32) + prev_low.astype(F32)
    return jnp.concatenate([high, low], axis=0)


def ring_gather(value, axis):
    return [value, shift(value, axis, -1), shift(value, axis, 2), shift(value, axis, 1)]


def ring_gather_halves(value, axis):
    half = value.shape[0] // 2
    after, before = shift(value, axis, -1), shift(value, axis, 1)
    far = jnp.concatenate([shift(before[:half], axis, 1), shift(after[half:], axis, -1)], axis=0)
    return [value, after, far, before]


def ring_swap(chunk, axis):
    return [chunk(0), shift(chunk(3), axis, -1), shift(chunk(2), axis, 2), shift(chunk(1), axis, 1)]


def ring_swap_halves(chunk, axis):
    far = chunk(2)
    half = far.shape[0] // 2
    rows = 2 * half
    prev = shift(jnp.concatenate([chunk(1), far[:half]], axis=0), axis, 1)
    after = shift(jnp.concatenate([chunk(3), far[half:]], axis=0), axis, -1)
    high, low = shift(prev[rows:], axis, 1), shift(after[rows:], axis, -1)
    return [chunk(0), after[:rows], jnp.concatenate([high, low], axis=0), prev[:rows]], (prev, after)


def in_order(pieces, me):
    twice = jnp.stack(pieces + pieces)
    return lax.dynamic_slice_in_dim(twice, lax.rem(N - me, N), N, axis=0)


def total_of(value, beside):
    total = jnp.full((8, 128), jnp.sum(value * value), F32)
    total = total + lax.ppermute(total, "c", [(0, 1), (1, 0)])
    each = lax.all_to_all(
        jnp.broadcast_to(total[:1], (N * N * N, 128)), ("x", "y", "z"), split_axis=0, concat_axis=0, tiled=True
    )
    if beside is not None:
        each, beside = lax.optimization_barrier((each, beside))
    return jnp.sum(each[:, 0]), beside


def per_device(tokens, target, weight):
    ix, iy = lax.axis_index("x"), lax.axis_index("y")
    rows, wide = tokens.shape
    cols = weight.shape[1] // N
    width = wide * 2 * N
    hidden_all = weight.shape[1] * 2 * N

    x = lax.all_gather(tokens, ("z", "c", "y"), axis=0, tiled=True).reshape(2 * N, N * rows, wide)

    def columns(array):
        return lambda k: lax.dynamic_slice_in_dim(array, lax.rem(iy + k, N) * cols, cols, axis=1)

    t_pieces, first_hop = ring_swap_halves(columns(target), "y")
    t = in_order(t_pieces, iy)
    t = jnp.concatenate([t[k].T for k in range(N)], axis=1)

    w_rows = in_order(ring_swap(columns(behind(weight, *first_hop)), "y"), iy).reshape(-1, cols)
    w = in_order(ring_gather(w_rows.T, "x"), ix)
    w = jnp.concatenate([w[k] for k in range(N)], axis=1)
    hidden, slope = first_slopes(x, w, t)
    first = ring_sum(lambda b: term(x, slope, b), ix)
    own, after, far, before = ring_gather_halves(first.astype(BF16), "x")
    at = lambda k: lax.rem(ix + k, N)
    part = moved(x, [own, after, before], [at(0), at(1), at(3)])
    total, part = total_of(first, part)
    scale = 0.5 * math.sqrt(hidden_all) / jnp.sqrt(total + 1e-06)
    slope = moved(x, [far], [at(2)], part, (scale.reshape(1, 1), hidden, t))
    second = ring_sum(lambda b: term(x, slope, b), ix)
    total, _ = total_of(second, None)
    factor = jnp.minimum(1.0, math.sqrt(width * hidden_all) / jnp.sqrt(total + 1e-06))
    held = second.astype(BF16).T.reshape(N, -1, cols)
    parts = in_order(ring_swap(lambda k: lax.dynamic_index_in_dim(held, lax.rem(iy + k, N), 0, keepdims=False), "y"), iy)
    whole = jnp.concatenate([parts[k] for k in range(N)], axis=1)
    return whole.astype(F32) * factor


def solution(mesh):
    grid = Mesh(mesh.devices.reshape(N, N, N, 2), ("x", "y", "z", "c"))
    spec = P(("x", "y"), ("z", "c"))
    return jax.shard_map(
        per_device, mesh=grid, in_specs=(spec, spec, spec), out_specs=spec, check_vma=False
    )
```

```python
import math

import jax
import jax.numpy as jnp
from jax import lax
from jax.experimental import pallas as pl
from jax.experimental.pallas import tpu as pltpu
from jax.sharding import Mesh, PartitionSpec as P

BF16, F32 = jnp.bfloat16, jnp.float32
N = 4
NT = (((1,), (1,)), ((), ()))
PARAMS = pltpu.CompilerParams(vmem_limit_bytes=52 << 20)


def shift(value, axis, step):
    return lax.ppermute(value, axis, [(i, (i + step) % N) for i in range(N)])


def behind(value, *others):
    return lax.optimization_barrier((value, *others))[0]


def slope_of(hidden, target):
    root = math.sqrt(2.0 / math.pi)
    square = hidden * hidden
    bend = jnp.tanh(hidden * (root + (root * 0.044715) * square))
    half = 0.5 + 0.5 * bend
    deriv = half + (hidden * (1.0 - bend * bend)) * (0.5 * root + (1.5 * root * 0.044715) * square)
    return ((hidden * half - target.astype(F32)) * deriv).astype(BF16)


def cost(rows, deep, cols, exps=0):
    return pl.CostEstimate(
        flops=2 * rows * deep * cols, bytes_accessed=2 * deep * (rows + cols) + 4 * rows * cols, transcendentals=exps
    )


def first_slopes(x, w, t, order, held=None):
    blocks, rows, wide = x.shape
    cols = w.shape[0]
    tile = t.shape[1] // N
    skip = 0 if held is None else 1
    out = pl.BlockSpec((cols, tile), lambda i, order: (0, i + skip))

    def kernel(order_ref, x_ref, w_ref, t_ref, *refs):
        h_ref, s_ref = refs[-2:]
        x = jnp.concatenate([x_ref[order_ref[k]] for k in range(blocks)], axis=1)
        hidden = lax.dot_general(w_ref[...], x, NT, preferred_element_type=F32)
        h_ref[...] = hidden
        s_ref[...] = slope_of(hidden, t_ref[...])

    return pl.pallas_call(
        kernel,
        grid_spec=pltpu.PrefetchScalarGridSpec(
            num_scalar_prefetch=1,
            grid=(rows // tile,),
            in_specs=[
                pl.BlockSpec((blocks, tile, wide), lambda i, order: (0, i, 0)),
                pl.BlockSpec(w.shape, lambda i, order: (0, 0), pipeline_mode=pl.Buffered(1)),
                out,
            ]
            + ([] if held is None else [pl.BlockSpec(memory_space=pl.ANY)] * 2),
            out_specs=[out, out],
        ),
        out_shape=[jax.ShapeDtypeStruct(t.shape, F32), jax.ShapeDtypeStruct(t.shape, BF16)],
        input_output_aliases={} if held is None else {4: 0, 5: 1},
        compiler_params=PARAMS,
        cost_estimate=cost(cols, blocks * wide, rows, rows * cols),
    )(order, x, w, t, *(() if held is None else held))


def x_specs(x, j):
    gathered, passed, _ = x
    wide = gathered.shape[2]
    tile = passed.shape[1]
    one = lambda k: pl.BlockSpec(
        (1, tile, wide), lambda i, which: (which[3 * j + k], 0, 0), pipeline_mode=pl.Buffered(1)
    )
    return [pl.BlockSpec((2, tile, wide), lambda i, which: (which[3 * j], jnp.maximum(i - 1, 0), 0)), one(1), one(2)]


def places(x, blocks):
    order = x[2]
    return jnp.stack([place for b in blocks for place in (b, order[2 * b], order[2 * b + 1])]).astype(jnp.int32)


def take(refs, x_ref):
    gathered, left, right = refs

    @pl.when(pl.program_id(0) == 0)
    def _():
        x_ref[...] = jnp.concatenate([left[0], right[0]], axis=1)

    @pl.when(pl.program_id(0) > 0)
    def _():
        x_ref[...] = jnp.concatenate([gathered[0], gathered[1]], axis=1)


def moved(x, pieces, which, part=None, last=None):
    tile = x[1].shape[1]
    rows = N * tile
    cols, deep = pieces[0].shape
    count = len(pieces)
    out = pl.BlockSpec((cols, tile), lambda i, which: (0, i))
    specs = [spec for j in range(count) for spec in x_specs(x, j)]
    specs += [pl.BlockSpec((cols, deep), lambda i, which: (0, 0), pipeline_mode=pl.Buffered(1))] * count
    args = [x[0], x[1], x[1]] * count + list(pieces)
    if part is not None:
        specs.append(out)
        args.append(part)
    if last is not None:
        specs += [pl.BlockSpec(memory_space=pltpu.SMEM), out, out]
        args += list(last)

    def kernel(which_ref, *refs):
        xs, fs = refs[: 3 * count], refs[3 * count : 4 * count]
        rest = list(refs[4 * count : -1])
        x_ref = refs[-1]
        total = rest.pop(0)[...] if part is not None else None
        for j in range(count):
            take(xs[3 * j : 3 * j + 3], x_ref.at[j])
        for j in range(count):
            more = lax.dot_general(fs[j][...], x_ref[j], NT, preferred_element_type=F32)
            total = more if total is None else total + more
        if last is not None:
            scale, hidden, target, out_ref = rest
            out_ref[...] = slope_of(hidden[...] + scale[0, 0] * total, target[...])
        else:
            rest[0][...] = total

    return pl.pallas_call(
        kernel,
        grid_spec=pltpu.PrefetchScalarGridSpec(
            num_scalar_prefetch=1,
            grid=(N,),
            in_specs=specs,
            out_specs=out,
            scratch_shapes=[pltpu.VMEM((count, tile, deep), BF16)],
        ),
        out_shape=jax.ShapeDtypeStruct((cols, rows), F32 if last is None else BF16),
        compiler_params=PARAMS,
        cost_estimate=cost(cols, deep * count, rows, 0 if last is None else rows * cols),
    )(places(x, which), *args)


def term_kernel(which_ref, gathered, left, right, s_ref, o_ref, x_ref):
    take((gathered, left, right), x_ref)
    part = jnp.dot(s_ref[...], x_ref[...], preferred_element_type=F32)

    @pl.when(pl.program_id(0) == 0)
    def _():
        o_ref[...] = part

    @pl.when(pl.program_id(0) > 0)
    def _():
        o_ref[...] += part


def term(x, s, block):
    cols, rows = s.shape
    tile = rows // N
    deep = 2 * x[0].shape[2]
    return pl.pallas_call(
        term_kernel,
        grid_spec=pltpu.PrefetchScalarGridSpec(
            num_scalar_prefetch=1,
            grid=(N,),
            in_specs=x_specs(x, 0) + [pl.BlockSpec((cols, tile), lambda i, which: (0, i))],
            out_specs=pl.BlockSpec((cols, deep), lambda i, which: (0, 0)),
            scratch_shapes=[pltpu.VMEM((tile, deep), BF16)],
        ),
        out_shape=jax.ShapeDtypeStruct((cols, deep), F32),
        compiler_params=PARAMS,
        cost_estimate=cost(cols, rows, deep),
    )(places(x, [block]), x[0], x[1], x[1], s)


def ring_sum(part, me):
    block = lambda step: part(lax.rem(me + step, N))
    far = block(2).astype(BF16)
    half = far.shape[0] // 2
    far_next, far_prev = shift(far[:half], "x", 1), shift(far[half:], "x", -1)
    to_next, to_prev = block(1), block(3)
    next_low = shift(to_next[half:].astype(BF16), "x", 1)
    prev_high = shift(to_prev[:half].astype(BF16), "x", -1)
    next_high = shift((to_next[:half] + far_next.astype(F32)).astype(BF16), "x", 1)
    prev_low = shift((to_prev[half:] + far_prev.astype(F32)).astype(BF16), "x", -1)
    own = block(0)
    high = own[:half] + next_high.astype(F32) + prev_high.astype(F32)
    low = own[half:] + next_low.astype(F32) + prev_low.astype(F32)
    return jnp.concatenate([high, low], axis=0)


def ring_gather(value, axis):
    return [value, shift(value, axis, -1), shift(value, axis, 2), shift(value, axis, 1)]


def ring_gather_halves(value, axis):
    half = value.shape[0] // 2
    after, before = shift(value, axis, -1), shift(value, axis, 1)
    far = jnp.concatenate([shift(before[:half], axis, 1), shift(after[half:], axis, -1)], axis=0)
    return [value, after, far, before]


def ring_swap(chunk, axis):
    return [chunk(0), shift(chunk(3), axis, -1), shift(chunk(2), axis, 2), shift(chunk(1), axis, 1)]


def ring_swap_halves(chunk, axis):
    far = chunk(2)
    half = far.shape[0] // 2
    rows = 2 * half
    sent = [jnp.concatenate([chunk(1), far[:half]], axis=0), jnp.concatenate([chunk(3), far[half:]], axis=0)]
    prev, after = shift(sent[0], axis, 1), shift(sent[1], axis, -1)
    high, low = shift(prev[rows:], axis, 1), shift(after[rows:], axis, -1)
    return [chunk(0), after[:rows], jnp.concatenate([high, low], axis=0), prev[:rows]], sent


def in_order(pieces, me):
    twice = jnp.stack(pieces + pieces)
    return lax.dynamic_slice_in_dim(twice, lax.rem(N - me, N), N, axis=0)


def total_of(value, beside):
    total = jnp.full((8, 128), jnp.sum(value * value), F32)
    total = total + lax.ppermute(total, "c", [(0, 1), (1, 0)])
    each = lax.all_to_all(
        jnp.broadcast_to(total[:1], (N * N * N, 128)), ("x", "y", "z"), split_axis=0, concat_axis=0, tiled=True
    )
    if beside is not None:
        each, beside = lax.optimization_barrier((each, beside))
    return jnp.sum(each[:, 0]), beside


def per_device(tokens, target, weight):
    ix, iy, iz, ic = (lax.axis_index(axis) for axis in ("x", "y", "z", "c"))
    rows, wide = tokens.shape
    cols = weight.shape[1] // N
    width = wide * 2 * N
    hidden_all = weight.shape[1] * 2 * N

    most = rows * 3 // 4
    gathered = lax.all_gather(tokens[:most], ("z", "c", "y"), axis=0, tiled=True).reshape(2 * N, N * most, wide)

    def columns(array):
        return lambda k: lax.dynamic_slice_in_dim(array, lax.rem(iy + k, N) * cols, cols, axis=1)

    t_pieces, sent = ring_swap_halves(columns(target), "y")
    ring = jnp.concatenate(ring_gather(tokens[most:], "y"), axis=0)
    passed = jnp.stack(
        [half for piece in ring_gather(behind(ring, *sent), "z") for half in (piece, lax.ppermute(piece, "c", [(0, 1), (1, 0)]))]
    )
    order = jnp.stack([2 * lax.rem(z + N - iz, N) + lax.rem(c + ic, 2) for z in range(N) for c in range(2)])
    order = order.astype(jnp.int32)
    plain = jnp.arange(2 * N, dtype=jnp.int32)
    x = (gathered, passed, order)
    t = in_order(t_pieces, iy)
    t = jnp.concatenate([piece[most:].T for piece in t_pieces] + [t[k, :most].T for k in range(N)], axis=1)

    w_rows = in_order(ring_swap(columns(behind(weight, ring)), "y"), iy).reshape(-1, cols)
    w = in_order(ring_gather(w_rows.T, "x"), ix)
    w = jnp.concatenate([w[k] for k in range(N)], axis=1)
    hidden, slope = first_slopes(passed, w, t, order)
    hidden, slope = first_slopes(gathered, w, t, plain, (hidden, slope))
    first = ring_sum(lambda b: term(x, slope, b), ix)
    own, after, far, before = ring_gather_halves(first.astype(BF16), "x")
    at = lambda k: lax.rem(ix + k, N)
    part = moved(x, [own, after, before], [at(0), at(1), at(3)])
    total, part = total_of(first, part)
    scale = 0.5 * math.sqrt(hidden_all) / jnp.sqrt(total + 1e-06)
    slope = moved(x, [far], [at(2)], part, (scale.reshape(1, 1), hidden, t))
    second = ring_sum(lambda b: term(x, slope, b), ix)
    total, _ = total_of(second, None)
    factor = jnp.minimum(1.0, math.sqrt(width * hidden_all) / jnp.sqrt(total + 1e-06))
    held = second.astype(BF16).T.reshape(N, -1, cols)
    parts = in_order(ring_swap(lambda k: lax.dynamic_index_in_dim(held, lax.rem(iy + k, N), 0, keepdims=False), "y"), iy)
    whole = jnp.concatenate([parts[k] for k in range(N)], axis=1)
    return whole.astype(F32) * factor


def solution(mesh):
    grid = Mesh(mesh.devices.reshape(N, N, N, 2), ("x", "y", "z", "c"))
    spec = P(("x", "y"), ("z", "c"))
    return jax.shard_map(
        per_device, mesh=grid, in_specs=(spec, spec, spec), out_specs=spec, check_vma=False
    )
```

```python
import math

import jax
import jax.numpy as jnp
from jax import lax
from jax.experimental import pallas as pl
from jax.experimental.pallas import tpu as pltpu
from jax.sharding import Mesh, PartitionSpec as P

BF16, F32 = jnp.bfloat16, jnp.float32
N = 4
NT = (((1,), (1,)), ((), ()))
PARAMS = pltpu.CompilerParams(vmem_limit_bytes=52 << 20)


def shift(value, axis, step):
    return lax.ppermute(value, axis, [(i, (i + step) % N) for i in range(N)])


def behind(value, *others):
    return lax.optimization_barrier((value, *others))[0]


def slope_of(hidden, target):
    root = math.sqrt(2.0 / math.pi)
    square = hidden * hidden
    bend = jnp.tanh(hidden * (root + (root * 0.044715) * square))
    half = 0.5 + 0.5 * bend
    deriv = half + (hidden * (1.0 - bend * bend)) * (0.5 * root + (1.5 * root * 0.044715) * square)
    return ((hidden * half - target.astype(F32)) * deriv).astype(BF16)


def joined(x_ref):
    return jnp.concatenate([x_ref[k] for k in range(x_ref.shape[0])], axis=1)


def cost(rows, deep, cols, exps=0):
    return pl.CostEstimate(
        flops=2 * rows * deep * cols, bytes_accessed=2 * deep * (rows + cols) + 4 * rows * cols, transcendentals=exps
    )


def first_kernel(x_ref, w_ref, t_ref, h_ref, s_ref):
    hidden = lax.dot_general(w_ref[...], joined(x_ref), NT, preferred_element_type=F32)
    h_ref[...] = hidden
    s_ref[...] = slope_of(hidden, t_ref[...])


def first_slopes(x, w, t):
    blocks, rows, wide = x.shape
    cols = w.shape[0]
    tile = rows // N
    out = pl.BlockSpec((cols, tile), lambda i: (0, i))
    return pl.pallas_call(
        first_kernel,
        grid=(N,),
        in_specs=[
            pl.BlockSpec((blocks, tile, wide), lambda i: (0, i, 0)),
            pl.BlockSpec(w.shape, lambda i: (0, 0)),
            out,
        ],
        out_specs=[out, out],
        out_shape=[jax.ShapeDtypeStruct((cols, rows), F32), jax.ShapeDtypeStruct((cols, rows), BF16)],
        compiler_params=PARAMS,
        cost_estimate=cost(cols, blocks * wide, rows, rows * cols),
    )(x, w, t)


def moved_kernel(count, started, last, *refs):
    refs = list(refs[1:])
    xs, fs = refs[:count], refs[count : 2 * count]
    rest = refs[2 * count :]
    x = jnp.concatenate([x_ref[k] for x_ref in xs for k in range(x_ref.shape[0])], axis=1)
    f = jnp.concatenate([f_ref[...] for f_ref in fs], axis=1)
    part = lax.dot_general(f, x, NT, preferred_element_type=F32)
    if started:
        part = part + rest.pop(0)[...]
    if last:
        scale, hidden, target, out = rest
        out[...] = slope_of(hidden[...] + scale[0, 0] * part, target[...])
    else:
        rest[0][...] = part


def moved(x, pieces, which, part=None, last=None):
    blocks, rows, wide = x.shape
    cols, deep = pieces[0].shape
    per = deep // wide
    tile = rows // N
    count = len(pieces)
    at = lambda j: pl.BlockSpec((per, tile, wide), lambda i, which: (which[j], i, 0))
    out = pl.BlockSpec((cols, tile), lambda i, which: (0, i))
    specs = [at(j) for j in range(count)] + [pl.BlockSpec((cols, deep), lambda i, which: (0, 0))] * count
    args = [x] * count + list(pieces)
    alias = {}
    if part is not None:
        if last is None:
            alias = {1 + len(args): 0}
        specs.append(out)
        args.append(part)
    if last is not None:
        specs += [pl.BlockSpec(memory_space=pltpu.SMEM), out, out]
        args += list(last)

    def kernel(*refs):
        moved_kernel(count, part is not None, last is not None, *refs)

    return pl.pallas_call(
        kernel,
        grid_spec=pltpu.PrefetchScalarGridSpec(
            num_scalar_prefetch=1, grid=(N,), in_specs=specs, out_specs=out
        ),
        out_shape=jax.ShapeDtypeStruct((cols, rows), F32 if last is None else BF16),
        input_output_aliases=alias,
        compiler_params=PARAMS,
        cost_estimate=cost(cols, deep * count, rows, 0 if last is None else rows * cols),
    )(jnp.stack(which).astype(jnp.int32), *args)


def terms(x, s, which):
    blocks, rows, wide = x.shape
    cols = s.shape[0]
    tile = rows // 2
    per = blocks // N
    count = len(which)
    at = lambda j: pl.BlockSpec((per, tile, wide), lambda i, which: (which[j], i, 0))

    def kernel(which_ref, *refs):
        s_ref = refs[count]
        parts = [jnp.dot(s_ref[...], joined(refs[j]), preferred_element_type=F32) for j in range(count)]

        @pl.when(pl.program_id(0) == 0)
        def _():
            for j in range(count):
                refs[count + 1 + j][...] = parts[j]

        @pl.when(pl.program_id(0) > 0)
        def _():
            for j in range(count):
                refs[count + 1 + j][...] += parts[j]

    return pl.pallas_call(
        kernel,
        grid_spec=pltpu.PrefetchScalarGridSpec(
            num_scalar_prefetch=1,
            grid=(rows // tile,),
            in_specs=[at(j) for j in range(count)] + [pl.BlockSpec((cols, tile), lambda i, which: (0, i))],
            out_specs=[pl.BlockSpec((cols, per * wide), lambda i, which: (0, 0))] * count,
        ),
        out_shape=[jax.ShapeDtypeStruct((cols, per * wide), F32)] * count,
        compiler_params=PARAMS,
        cost_estimate=cost(cols, rows, per * wide * count),
    )(jnp.stack(which).astype(jnp.int32), *([x] * count), s)


def ring_sum(parts, me):
    at = lambda step: lax.rem(me + step, N)
    far = parts([at(2)])[0].astype(BF16)
    half = far.shape[0] // 2
    far_next, far_prev = shift(far[:half], "x", 1), shift(far[half:], "x", -1)
    to_next, to_prev = parts([at(1), at(3)])
    next_low = shift(to_next[half:].astype(BF16), "x", 1)
    prev_high = shift(to_prev[:half].astype(BF16), "x", -1)
    next_high = shift((to_next[:half] + far_next.astype(F32)).astype(BF16), "x", 1)
    prev_low = shift((to_prev[half:] + far_prev.astype(F32)).astype(BF16), "x", -1)
    own = parts([at(0)])[0]
    high = own[:half] + next_high.astype(F32) + prev_high.astype(F32)
    low = own[half:] + next_low.astype(F32) + prev_low.astype(F32)
    return jnp.concatenate([high, low], axis=0)


def ring_gather(value, axis):
    return [value, shift(value, axis, -1), shift(value, axis, 2), shift(value, axis, 1)]


def ring_gather_halves(value, axis):
    half = value.shape[0] // 2
    after, before = shift(value, axis, -1), shift(value, axis, 1)
    far = jnp.concatenate([shift(before[:half], axis, 1), shift(after[half:], axis, -1)], axis=0)
    return [value, after, far, before]


def ring_swap(chunk, axis):
    return [chunk(0), shift(chunk(3), axis, -1), shift(chunk(2), axis, 2), shift(chunk(1), axis, 1)]


def ring_swap_halves(chunk, axis):
    far = chunk(2)
    half = far.shape[0] // 2
    rows = 2 * half
    prev = shift(jnp.concatenate([chunk(1), far[:half]], axis=0), axis, 1)
    after = shift(jnp.concatenate([chunk(3), far[half:]], axis=0), axis, -1)
    high, low = shift(prev[rows:], axis, 1), shift(after[rows:], axis, -1)
    return [chunk(0), after[:rows], jnp.concatenate([high, low], axis=0), prev[:rows]], (prev, after)


def in_order(pieces, me):
    twice = jnp.stack(pieces + pieces)
    return lax.dynamic_slice_in_dim(twice, lax.rem(N - me, N), N, axis=0)


def total_of(value, beside):
    total = jnp.full((N * N * N, 128), jnp.sum(value * value), F32)
    total = total + lax.ppermute(total, "c", [(0, 1), (1, 0)])
    each = lax.all_to_all(total, ("x", "y", "z"), split_axis=0, concat_axis=0, tiled=True)
    if beside is not None:
        each, beside = lax.optimization_barrier((each, beside))
    return jnp.sum(each[:, 0]), beside


def per_device(tokens, target, weight):
    ix, iy = lax.axis_index("x"), lax.axis_index("y")
    rows, wide = tokens.shape
    cols = weight.shape[1] // N
    width = wide * 2 * N
    hidden_all = weight.shape[1] * 2 * N

    x = lax.all_gather(tokens, ("z", "c", "y"), axis=0, tiled=True).reshape(2 * N, N * rows, wide)

    def columns(array):
        return lambda k: lax.dynamic_slice_in_dim(array, lax.rem(iy + k, N) * cols, cols, axis=1)

    t_pieces, first_hop = ring_swap_halves(columns(target), "y")
    t = in_order(t_pieces, iy)
    t = jnp.concatenate([t[k].T for k in range(N)], axis=1)

    w_rows = in_order(ring_swap(columns(behind(weight, *first_hop)), "y"), iy).reshape(-1, cols)
    w = in_order(ring_gather(w_rows.T, "x"), ix)
    w = jnp.concatenate([w[k] for k in range(N)], axis=1)
    hidden, slope = first_slopes(x, w, t)
    first = ring_sum(lambda bs: terms(x, slope, bs), ix)
    own, after, far, before = ring_gather_halves(first.astype(BF16), "x")
    at = lambda k: lax.rem(ix + k, N)
    part = moved(x, [own, after, before], [at(0), at(1), at(3)])
    total, part = total_of(first, part)
    scale = 0.5 * math.sqrt(hidden_all) / jnp.sqrt(total + 1e-06)
    slope = moved(x, [far], [at(2)], part, (scale.reshape(1, 1), hidden, t))
    second = ring_sum(lambda bs: terms(x, slope, bs), ix)
    total, _ = total_of(second, None)
    factor = jnp.minimum(1.0, math.sqrt(width * hidden_all) / jnp.sqrt(total + 1e-06))
    held = second.astype(BF16).T.reshape(N, -1, cols)
    parts = in_order(ring_swap(lambda k: lax.dynamic_index_in_dim(held, lax.rem(iy + k, N), 0, keepdims=False), "y"), iy)
    whole = jnp.concatenate([parts[k] for k in range(N)], axis=1)
    return whole.astype(F32) * factor


def solution(mesh):
    grid = Mesh(mesh.devices.reshape(N, N, N, 2), ("x", "y", "z", "c"))
    spec = P(("x", "y"), ("z", "c"))
    return jax.shard_map(
        per_device, mesh=grid, in_specs=(spec, spec, spec), out_specs=spec, check_vma=False
    )
```

```python
import math

import jax
import jax.numpy as jnp
from jax import lax
from jax.experimental import pallas as pl
from jax.experimental.pallas import tpu as pltpu
from jax.sharding import Mesh, PartitionSpec as P

BF16, F32 = jnp.bfloat16, jnp.float32
N = 4
NT = (((1,), (1,)), ((), ()))
PARAMS = pltpu.CompilerParams(vmem_limit_bytes=52 << 20)


def shift(value, axis, step):
    return lax.ppermute(value, axis, [(i, (i + step) % N) for i in range(N)])


def behind(value, *others):
    return lax.optimization_barrier((value, *others))[0]


def slope_of(hidden, target):
    root = math.sqrt(2.0 / math.pi)
    square = hidden * hidden
    bend = jnp.tanh(hidden * (root + (root * 0.044715) * square))
    half = 0.5 + 0.5 * bend
    deriv = half + (hidden * (1.0 - bend * bend)) * (0.5 * root + (1.5 * root * 0.044715) * square)
    return ((hidden * half - target.astype(F32)) * deriv).astype(BF16)


def joined(x_ref):
    return jnp.concatenate([x_ref[k] for k in range(x_ref.shape[0])], axis=1)


def cost(rows, deep, cols, exps=0):
    return pl.CostEstimate(
        flops=2 * rows * deep * cols, bytes_accessed=2 * deep * (rows + cols) + 4 * rows * cols, transcendentals=exps
    )


def add_term(s, x, far_ref, total_ref):
    part = jnp.dot(s, x, preferred_element_type=F32)
    step = pl.program_id(0)

    @pl.when(step == 0)
    def _():
        total_ref[...] = part

    @pl.when(step > 0)
    def _():
        total_ref[...] += part

    @pl.when(step == pl.num_programs(0) - 1)
    def _():
        far_ref[...] = total_ref[...].astype(BF16)


def first_slopes(x, w, t, block):
    blocks, rows, wide = x.shape
    cols = w.shape[0]
    tile = rows // N
    per = blocks // N
    out = pl.BlockSpec((cols, tile), lambda i, which: (0, i))

    def kernel(which_ref, x_ref, w_ref, t_ref, h_ref, s_ref, far_ref, total_ref):
        hidden = lax.dot_general(w_ref[...], joined(x_ref), NT, preferred_element_type=F32)
        h_ref[...] = hidden
        s = slope_of(hidden, t_ref[...])
        s_ref[...] = s
        x = jnp.concatenate([x_ref[per * which_ref[0] + k] for k in range(per)], axis=1)
        add_term(s, x, far_ref, total_ref)

    return pl.pallas_call(
        kernel,
        grid_spec=pltpu.PrefetchScalarGridSpec(
            num_scalar_prefetch=1,
            grid=(N,),
            in_specs=[
                pl.BlockSpec((blocks, tile, wide), lambda i, which: (0, i, 0)),
                pl.BlockSpec(w.shape, lambda i, which: (0, 0), pipeline_mode=pl.Buffered(1)),
                out,
            ],
            out_specs=[out, out, pl.BlockSpec((cols, per * wide), lambda i, which: (0, 0))],
            scratch_shapes=[pltpu.VMEM((cols, per * wide), F32)],
        ),
        out_shape=[
            jax.ShapeDtypeStruct((cols, rows), F32),
            jax.ShapeDtypeStruct((cols, rows), BF16),
            jax.ShapeDtypeStruct((cols, per * wide), BF16),
        ],
        compiler_params=PARAMS,
        cost_estimate=cost(cols, (blocks + per) * wide, rows, rows * cols),
    )(jnp.reshape(block, (1,)).astype(jnp.int32), x, w, t)


def moved(x, pieces, which):
    blocks, rows, wide = x.shape
    cols, deep = pieces[0].shape
    per = deep // wide
    tile = rows // N
    count = len(pieces)
    at = lambda j: pl.BlockSpec((per, tile, wide), lambda i, which: (which[j], i, 0))

    def kernel(which_ref, *refs):
        xs, fs = refs[:count], refs[count : 2 * count]
        x = jnp.concatenate([x_ref[k] for x_ref in xs for k in range(per)], axis=1)
        f = jnp.concatenate([f_ref[...] for f_ref in fs], axis=1)
        refs[-1][...] = lax.dot_general(f, x, NT, preferred_element_type=F32)

    return pl.pallas_call(
        kernel,
        grid_spec=pltpu.PrefetchScalarGridSpec(
            num_scalar_prefetch=1,
            grid=(N,),
            in_specs=[at(j) for j in range(count)] + [pl.BlockSpec((cols, deep), lambda i, which: (0, 0))] * count,
            out_specs=pl.BlockSpec((cols, tile), lambda i, which: (0, i)),
        ),
        out_shape=jax.ShapeDtypeStruct((cols, rows), F32),
        compiler_params=PARAMS,
        cost_estimate=cost(cols, deep * count, rows),
    )(jnp.stack(which).astype(jnp.int32), *([x] * count), *pieces)


def second_slopes(x, piece, block, part, scale, hidden, t):
    blocks, rows, wide = x.shape
    cols, deep = piece.shape
    per = deep // wide
    tile = rows // N
    out = pl.BlockSpec((cols, tile), lambda i, which: (0, i))
    whole = pl.BlockSpec((cols, deep), lambda i, which: (0, 0))

    def kernel(which_ref, scale_ref, x_ref, f_ref, part_ref, h_ref, t_ref, s_ref, far_ref, total_ref):
        x = joined(x_ref)
        move = part_ref[...] + lax.dot_general(f_ref[...], x, NT, preferred_element_type=F32)
        s = slope_of(h_ref[...] + scale_ref[0, 0] * move, t_ref[...])
        s_ref[...] = s
        add_term(s, x, far_ref, total_ref)

    return pl.pallas_call(
        kernel,
        grid_spec=pltpu.PrefetchScalarGridSpec(
            num_scalar_prefetch=1,
            grid=(N,),
            in_specs=[
                pl.BlockSpec(memory_space=pltpu.SMEM),
                pl.BlockSpec((per, tile, wide), lambda i, which: (which[0], i, 0)),
                whole,
                out,
                out,
                out,
            ],
            out_specs=[out, whole],
            scratch_shapes=[pltpu.VMEM((cols, deep), F32)],
        ),
        out_shape=[jax.ShapeDtypeStruct((cols, rows), BF16), jax.ShapeDtypeStruct((cols, deep), BF16)],
        compiler_params=PARAMS,
        cost_estimate=cost(cols, 2 * deep, rows, rows * cols),
    )(jnp.reshape(block, (1,)).astype(jnp.int32), scale, x, piece, part, hidden, t)


def terms(x, s, which, cut):
    blocks, rows, wide = x.shape
    cols = s.shape[0]
    half = cols // 2
    tile = rows // 2
    per = blocks // N
    count = len(which)
    at = lambda j: pl.BlockSpec((per, tile, wide), lambda i, which: (which[j], i, 0))
    kinds = [F32, BF16, BF16, F32] if cut else [F32] * count
    tall = half if cut else cols

    def kernel(which_ref, *refs):
        s_ref = refs[count]
        outs, totals = refs[count + 1 : -count], refs[-count:]
        parts = [jnp.dot(s_ref[...], joined(refs[j]), preferred_element_type=F32) for j in range(count)]

        @pl.when(pl.program_id(0) == 0)
        def _():
            for j in range(count):
                totals[j][...] = parts[j]

        @pl.when(pl.program_id(0) > 0)
        def _():
            for j in range(count):
                total = totals[j][...] + parts[j]
                for n in range(cols // tall):
                    out = outs[j * (cols // tall) + n]
                    out[...] = total[n * tall : (n + 1) * tall].astype(out.dtype)

    return pl.pallas_call(
        kernel,
        grid_spec=pltpu.PrefetchScalarGridSpec(
            num_scalar_prefetch=1,
            grid=(rows // tile,),
            in_specs=[at(j) for j in range(count)] + [pl.BlockSpec((cols, tile), lambda i, which: (0, i))],
            out_specs=[pl.BlockSpec((tall, per * wide), lambda i, which: (0, 0))] * len(kinds),
            scratch_shapes=[pltpu.VMEM((cols, per * wide), F32)] * count,
        ),
        out_shape=[jax.ShapeDtypeStruct((tall, per * wide), kind) for kind in kinds],
        compiler_params=PARAMS,
        cost_estimate=cost(cols * count, rows, per * wide),
    )(jnp.stack(which).astype(jnp.int32), *([x] * count), s)


def ring_sum(x, s, far, me):
    at = lambda step: lax.rem(me + step, N)
    half = far.shape[0] // 2
    far_next, far_prev = shift(far[:half], "x", 1), shift(far[half:], "x", -1)
    high, to_next, to_prev, low = terms(x, s, [at(1), at(3)], True)
    next_low, prev_high = shift(to_next, "x", 1), shift(to_prev, "x", -1)
    next_high = shift((high + far_next.astype(F32)).astype(BF16), "x", 1)
    prev_low = shift((low + far_prev.astype(F32)).astype(BF16), "x", -1)
    (own,) = terms(x, s, [at(0)], False)
    high = own[:half] + next_high.astype(F32) + prev_high.astype(F32)
    low = own[half:] + next_low.astype(F32) + prev_low.astype(F32)
    return jnp.concatenate([high, low], axis=0)


def ring_gather(value, axis):
    return [value, shift(value, axis, -1), shift(value, axis, 2), shift(value, axis, 1)]


def ring_gather_halves(value, axis):
    half = value.shape[0] // 2
    after, before = shift(value, axis, -1), shift(value, axis, 1)
    far = jnp.concatenate([shift(before[:half], axis, 1), shift(after[half:], axis, -1)], axis=0)
    return [value, after, far, before]


def ring_swap(chunk, axis):
    return [chunk(0), shift(chunk(3), axis, -1), shift(chunk(2), axis, 2), shift(chunk(1), axis, 1)]


def ring_swap_halves(chunk, axis):
    far = chunk(2)
    half = far.shape[0] // 2
    rows = 2 * half
    prev = shift(jnp.concatenate([chunk(1), far[:half]], axis=0), axis, 1)
    after = shift(jnp.concatenate([chunk(3), far[half:]], axis=0), axis, -1)
    high, low = shift(prev[rows:], axis, 1), shift(after[rows:], axis, -1)
    return [chunk(0), after[:rows], jnp.concatenate([high, low], axis=0), prev[:rows]], (prev, after)


def in_order(pieces, me):
    twice = jnp.stack(pieces + pieces)
    return lax.dynamic_slice_in_dim(twice, lax.rem(N - me, N), N, axis=0)


def total_of(value, beside):
    total = jnp.full((N * N * N, 128), jnp.sum(value * value), F32)
    total = total + lax.ppermute(total, "c", [(0, 1), (1, 0)])
    each = lax.all_to_all(total, ("x", "y", "z"), split_axis=0, concat_axis=0, tiled=True)
    if beside is not None:
        each, beside = lax.optimization_barrier((each, beside))
    return jnp.sum(each[:, 0]), beside


def per_device(tokens, target, weight):
    ix, iy = lax.axis_index("x"), lax.axis_index("y")
    rows, wide = tokens.shape
    cols = weight.shape[1] // N
    width = wide * 2 * N
    hidden_all = weight.shape[1] * 2 * N

    x = lax.all_gather(tokens, ("z", "c", "y"), axis=0, tiled=True).reshape(2 * N, N * rows, wide)

    def columns(array):
        return lambda k: lax.dynamic_slice_in_dim(array, lax.rem(iy + k, N) * cols, cols, axis=1)

    t_pieces, first_hop = ring_swap_halves(columns(target), "y")
    t = in_order(t_pieces, iy)
    t = jnp.concatenate([t[k].T for k in range(N)], axis=1)

    w_rows = in_order(ring_swap(columns(behind(weight, *first_hop)), "y"), iy).reshape(-1, cols)
    w = in_order(ring_gather(w_rows.T, "x"), ix)
    w = jnp.concatenate([w[k] for k in range(N)], axis=1)
    at = lambda k: lax.rem(ix + k, N)
    hidden, slope, term = first_slopes(x, w, t, at(2))
    first = ring_sum(x, slope, term, ix)
    own, after, far, before = ring_gather_halves(first.astype(BF16), "x")
    part = moved(x, [own, after, before], [at(0), at(1), at(3)])
    total, part = total_of(first, part)
    scale = 0.5 * math.sqrt(hidden_all) / jnp.sqrt(total + 1e-06)
    slope, term = second_slopes(x, far, at(2), part, scale.reshape(1, 1), hidden, t)
    second = ring_sum(x, slope, term, ix)
    total, _ = total_of(second, None)
    factor = jnp.minimum(1.0, math.sqrt(width * hidden_all) / jnp.sqrt(total + 1e-06))
    held = second.astype(BF16).T.reshape(N, -1, cols)
    parts = in_order(ring_swap(lambda k: lax.dynamic_index_in_dim(held, lax.rem(iy + k, N), 0, keepdims=False), "y"), iy)
    whole = jnp.concatenate([parts[k] for k in range(N)], axis=1)
    return whole.astype(F32) * factor


def solution(mesh):
    grid = Mesh(mesh.devices.reshape(N, N, N, 2), ("x", "y", "z", "c"))
    spec = P(("x", "y"), ("z", "c"))
    return jax.shard_map(
        per_device, mesh=grid, in_specs=(spec, spec, spec), out_specs=spec, check_vma=False
    )
```

```python
import math

import jax
import jax.numpy as jnp
from jax import lax
from jax.experimental import pallas as pl
from jax.experimental.pallas import tpu as pltpu
from jax.sharding import Mesh, PartitionSpec as P

BF16, F32 = jnp.bfloat16, jnp.float32
N = 4
NT = (((1,), (1,)), ((), ()))
PARAMS = pltpu.CompilerParams(vmem_limit_bytes=52 << 20)


def shift(value, axis, step):
    return lax.ppermute(value, axis, [(i, (i + step) % N) for i in range(N)])


def behind(value, *others):
    return lax.optimization_barrier((value, *others))[0]


def slope_of(hidden, target):
    root = math.sqrt(2.0 / math.pi)
    square = hidden * hidden
    bend = jnp.tanh(hidden * (root + (root * 0.044715) * square))
    half = 0.5 + 0.5 * bend
    deriv = half + (hidden * (1.0 - bend * bend)) * (0.5 * root + (1.5 * root * 0.044715) * square)
    return ((hidden * half - target.astype(F32)) * deriv).astype(BF16)


def joined(x_ref):
    return jnp.concatenate([x_ref[k] for k in range(x_ref.shape[0])], axis=1)


def cost(rows, deep, cols, exps=0):
    return pl.CostEstimate(
        flops=2 * rows * deep * cols, bytes_accessed=2 * deep * (rows + cols) + 4 * rows * cols, transcendentals=exps
    )


def add_term(s, x, far_ref, total_ref):
    part = jnp.dot(s, x, preferred_element_type=F32)
    step = pl.program_id(0)

    @pl.when(step == 0)
    def _():
        total_ref[...] = part

    @pl.when(step > 0)
    def _():
        total_ref[...] += part

    @pl.when(step == pl.num_programs(0) - 1)
    def _():
        far_ref[...] = total_ref[...].astype(BF16)


def first_slopes(x, w, t, which):
    blocks, rows, wide = x.shape
    cols, deep = w[0].shape
    tile = rows // N
    per = deep // wide
    out = pl.BlockSpec((cols, tile), lambda i, which: (0, i))
    whole = pl.BlockSpec((cols, deep), lambda i, which: (0, 0), pipeline_mode=pl.Buffered(1))

    def kernel(which_ref, x_ref, *refs):
        w_refs, (t_ref, h_ref, s_ref, far_ref, total_ref) = refs[:N], refs[N:]
        block = lambda j: [x_ref[per * which_ref[j] + k] for k in range(per)]
        x = jnp.concatenate([part for j in range(N) for part in block(j)], axis=1)
        w = jnp.concatenate([w_ref[...] for w_ref in w_refs], axis=1)
        hidden = lax.dot_general(w, x, NT, preferred_element_type=F32)
        h_ref[...] = hidden
        s = slope_of(hidden, t_ref[...])
        s_ref[...] = s
        add_term(s, jnp.concatenate(block(2), axis=1), far_ref, total_ref)

    return pl.pallas_call(
        kernel,
        grid_spec=pltpu.PrefetchScalarGridSpec(
            num_scalar_prefetch=1,
            grid=(N,),
            in_specs=[pl.BlockSpec((blocks, tile, wide), lambda i, which: (0, i, 0))] + [whole] * N + [out],
            out_specs=[out, out, pl.BlockSpec((cols, deep), lambda i, which: (0, 0))],
            scratch_shapes=[pltpu.VMEM((cols, deep), F32)],
        ),
        out_shape=[
            jax.ShapeDtypeStruct((cols, rows), F32),
            jax.ShapeDtypeStruct((cols, rows), BF16),
            jax.ShapeDtypeStruct((cols, deep), BF16),
        ],
        compiler_params=PARAMS,
        cost_estimate=cost(cols, (blocks + per) * wide, rows, rows * cols),
    )(jnp.stack(which).astype(jnp.int32), x, *w, t)


def moved(x, pieces, which):
    blocks, rows, wide = x.shape
    cols, deep = pieces[0].shape
    per = deep // wide
    tile = rows // N
    count = len(pieces)
    at = lambda j: pl.BlockSpec((per, tile, wide), lambda i, which: (which[j], i, 0))

    def kernel(which_ref, *refs):
        xs, fs = refs[:count], refs[count : 2 * count]
        x = jnp.concatenate([x_ref[k] for x_ref in xs for k in range(per)], axis=1)
        f = jnp.concatenate([f_ref[...] for f_ref in fs], axis=1)
        refs[-1][...] = lax.dot_general(f, x, NT, preferred_element_type=F32)

    return pl.pallas_call(
        kernel,
        grid_spec=pltpu.PrefetchScalarGridSpec(
            num_scalar_prefetch=1,
            grid=(N,),
            in_specs=[at(j) for j in range(count)] + [pl.BlockSpec((cols, deep), lambda i, which: (0, 0))] * count,
            out_specs=pl.BlockSpec((cols, tile), lambda i, which: (0, i)),
        ),
        out_shape=jax.ShapeDtypeStruct((cols, rows), F32),
        compiler_params=PARAMS,
        cost_estimate=cost(cols, deep * count, rows),
    )(jnp.stack(which).astype(jnp.int32), *([x] * count), *pieces)


def second_slopes(x, piece, block, part, scale, hidden, t):
    blocks, rows, wide = x.shape
    cols, deep = piece.shape
    per = deep // wide
    tile = rows // N
    out = pl.BlockSpec((cols, tile), lambda i, which: (0, i))
    whole = pl.BlockSpec((cols, deep), lambda i, which: (0, 0))

    def kernel(which_ref, scale_ref, x_ref, f_ref, part_ref, h_ref, t_ref, s_ref, far_ref, total_ref):
        x = joined(x_ref)
        move = part_ref[...] + lax.dot_general(f_ref[...], x, NT, preferred_element_type=F32)
        s = slope_of(h_ref[...] + scale_ref[0, 0] * move, t_ref[...])
        s_ref[...] = s
        add_term(s, x, far_ref, total_ref)

    return pl.pallas_call(
        kernel,
        grid_spec=pltpu.PrefetchScalarGridSpec(
            num_scalar_prefetch=1,
            grid=(N,),
            in_specs=[
                pl.BlockSpec(memory_space=pltpu.SMEM),
                pl.BlockSpec((per, tile, wide), lambda i, which: (which[0], i, 0)),
                whole,
                out,
                out,
                out,
            ],
            out_specs=[out, whole],
            scratch_shapes=[pltpu.VMEM((cols, deep), F32)],
        ),
        out_shape=[jax.ShapeDtypeStruct((cols, rows), BF16), jax.ShapeDtypeStruct((cols, deep), BF16)],
        compiler_params=PARAMS,
        cost_estimate=cost(cols, 2 * deep, rows, rows * cols),
    )(jnp.reshape(block, (1,)).astype(jnp.int32), scale, x, piece, part, hidden, t)


def terms(x, s, which, cut):
    blocks, rows, wide = x.shape
    cols = s.shape[0]
    half = cols // 2
    tile = rows // 2
    per = blocks // N
    count = len(which)
    at = lambda j: pl.BlockSpec((per, tile, wide), lambda i, which: (which[j], i, 0))
    kinds = [F32, BF16, BF16, F32] if cut else [F32] * count
    tall = half if cut else cols

    def kernel(which_ref, *refs):
        s_ref = refs[count]
        outs, totals = refs[count + 1 : -count], refs[-count:]
        parts = [jnp.dot(s_ref[...], joined(refs[j]), preferred_element_type=F32) for j in range(count)]

        @pl.when(pl.program_id(0) == 0)
        def _():
            for j in range(count):
                totals[j][...] = parts[j]

        @pl.when(pl.program_id(0) > 0)
        def _():
            for j in range(count):
                total = totals[j][...] + parts[j]
                for n in range(cols // tall):
                    out = outs[j * (cols // tall) + n]
                    out[...] = total[n * tall : (n + 1) * tall].astype(out.dtype)

    return pl.pallas_call(
        kernel,
        grid_spec=pltpu.PrefetchScalarGridSpec(
            num_scalar_prefetch=1,
            grid=(rows // tile,),
            in_specs=[at(j) for j in range(count)] + [pl.BlockSpec((cols, tile), lambda i, which: (0, i))],
            out_specs=[pl.BlockSpec((tall, per * wide), lambda i, which: (0, 0))] * len(kinds),
            scratch_shapes=[pltpu.VMEM((cols, per * wide), F32)] * count,
        ),
        out_shape=[jax.ShapeDtypeStruct((tall, per * wide), kind) for kind in kinds],
        compiler_params=PARAMS,
        cost_estimate=cost(cols * count, rows, per * wide),
    )(jnp.stack(which).astype(jnp.int32), *([x] * count), s)


def ring_sum(x, s, far, me):
    at = lambda step: lax.rem(me + step, N)
    half = far.shape[0] // 2
    far_next, far_prev = shift(far[:half], "x", 1), shift(far[half:], "x", -1)
    high, to_next, to_prev, low = terms(x, s, [at(1), at(3)], True)
    next_low, prev_high = shift(to_next, "x", 1), shift(to_prev, "x", -1)
    next_high = shift((high + far_next.astype(F32)).astype(BF16), "x", 1)
    prev_low = shift((low + far_prev.astype(F32)).astype(BF16), "x", -1)
    (own,) = terms(x, s, [at(0)], False)
    high = own[:half] + next_high.astype(F32) + prev_high.astype(F32)
    low = own[half:] + next_low.astype(F32) + prev_low.astype(F32)
    return jnp.concatenate([high, low], axis=0)


def ring_gather(value, axis):
    return [value, shift(value, axis, -1), shift(value, axis, 2), shift(value, axis, 1)]


def ring_gather_halves(value, axis):
    half = value.shape[0] // 2
    after, before = shift(value, axis, -1), shift(value, axis, 1)
    far = jnp.concatenate([shift(before[:half], axis, 1), shift(after[half:], axis, -1)], axis=0)
    return [value, after, far, before]


def ring_swap(chunk, axis):
    return [chunk(0), shift(chunk(3), axis, -1), shift(chunk(2), axis, 2), shift(chunk(1), axis, 1)]


def cut_kernel(which_ref, own, after, far, before, to_next, to_prev, kept):
    rows = own.shape[0]
    half = rows // 2
    to_next[:rows], to_next[rows:] = after[...], far[:half]
    to_prev[:rows], to_prev[rows:] = before[...], far[half:]
    kept[...] = own[...]


def cut(array, me):
    rows, cols = array.shape[0], array.shape[1] // N
    at = lambda k: pl.BlockSpec((rows, cols), lambda i, which: (0, which[k]))
    tall = [rows + rows // 2, rows + rows // 2, rows]
    return pl.pallas_call(
        cut_kernel,
        grid_spec=pltpu.PrefetchScalarGridSpec(
            num_scalar_prefetch=1,
            grid=(1,),
            in_specs=[at(k) for k in range(N)],
            out_specs=[pl.BlockSpec((size, cols), lambda i, which: (0, 0)) for size in tall],
        ),
        out_shape=[jax.ShapeDtypeStruct((size, cols), array.dtype) for size in tall],
        compiler_params=PARAMS,
        cost_estimate=cost(0, 0, 0),
    )(jnp.stack([lax.rem(me + k, N) for k in range(N)]).astype(jnp.int32), *([array] * N))


def ring_swap_halves(to_next, to_prev, kept, axis):
    rows = kept.shape[0]
    prev, after = shift(to_next, axis, 1), shift(to_prev, axis, -1)
    high, low = shift(prev[rows:], axis, 1), shift(after[rows:], axis, -1)
    return [kept, after[:rows], jnp.concatenate([high, low], axis=0), prev[:rows]]


def in_order(pieces, me):
    twice = jnp.stack(pieces + pieces)
    return lax.dynamic_slice_in_dim(twice, lax.rem(N - me, N), N, axis=0)


def total_of(value, beside):
    total = jnp.full((N * N * N, 128), jnp.sum(value * value), F32)
    total = total + lax.ppermute(total, "c", [(0, 1), (1, 0)])
    each = lax.all_to_all(total, ("x", "y", "z"), split_axis=0, concat_axis=0, tiled=True)
    if beside is not None:
        each, beside = lax.optimization_barrier((each, beside))
    return jnp.sum(each[:, 0]), beside


def per_device(tokens, target, weight):
    ix, iy = lax.axis_index("x"), lax.axis_index("y")
    rows, wide = tokens.shape
    cols = weight.shape[1] // N
    width = wide * 2 * N
    hidden_all = weight.shape[1] * 2 * N

    x = lax.all_gather(tokens, ("z", "c", "y"), axis=0, tiled=True).reshape(2 * N, N * rows, wide)

    def columns(array):
        return lambda k: lax.dynamic_slice_in_dim(array, lax.rem(iy + k, N) * cols, cols, axis=1)

    to_next, to_prev, kept = cut(target, iy)
    w_pieces = ring_swap(columns(weight), "y")
    to_next, to_prev = lax.optimization_barrier((to_next, to_prev, *w_pieces))[:2]
    t = in_order(ring_swap_halves(to_next, to_prev, kept, "y"), iy)
    t = jnp.concatenate([t[k].T for k in range(N)], axis=1)
    w = ring_gather(in_order(w_pieces, iy).reshape(-1, cols).T, "x")

    at = lambda k: lax.rem(ix + k, N)
    hidden, slope, term = first_slopes(x, w, t, [at(k) for k in range(N)])
    first = ring_sum(x, slope, term, ix)
    own, after, far, before = ring_gather_halves(first.astype(BF16), "x")
    part = moved(x, [own, after, before], [at(0), at(1), at(3)])
    total, part = total_of(first, part)
    scale = 0.5 * math.sqrt(hidden_all) / jnp.sqrt(total + 1e-06)
    slope, term = second_slopes(x, far, at(2), part, scale.reshape(1, 1), hidden, t)
    second = ring_sum(x, slope, term, ix)
    total, _ = total_of(second, None)
    factor = jnp.minimum(1.0, math.sqrt(width * hidden_all) / jnp.sqrt(total + 1e-06))
    held = second.astype(BF16).T.reshape(N, -1, cols)
    parts = in_order(ring_swap(lambda k: lax.dynamic_index_in_dim(held, lax.rem(iy + k, N), 0, keepdims=False), "y"), iy)
    whole = jnp.concatenate([parts[k] for k in range(N)], axis=1)
    return whole.astype(F32) * factor


def solution(mesh):
    grid = Mesh(mesh.devices.reshape(N, N, N, 2), ("x", "y", "z", "c"))
    spec = P(("x", "y"), ("z", "c"))
    return jax.shard_map(
        per_device, mesh=grid, in_specs=(spec, spec, spec), out_specs=spec, check_vma=False
    )
```

```python
import math

import jax
import jax.numpy as jnp
from jax import lax
from jax.experimental import pallas as pl
from jax.experimental.pallas import tpu as pltpu
from jax.sharding import Mesh, PartitionSpec as P

BF16, F32 = jnp.bfloat16, jnp.float32
N = 4
NT = (((1,), (1,)), ((), ()))
PARAMS = pltpu.CompilerParams(vmem_limit_bytes=52 << 20)


def shift(value, axis, step):
    return lax.ppermute(value, axis, [(i, (i + step) % N) for i in range(N)])


def behind(value, *others):
    return lax.optimization_barrier((value, *others))[0]


def slope_of(hidden, target):
    root = math.sqrt(2.0 / math.pi)
    square = hidden * hidden
    bend = jnp.tanh(hidden * (root + (root * 0.044715) * square))
    half = 0.5 + 0.5 * bend
    deriv = half + (hidden * (1.0 - bend * bend)) * (0.5 * root + (1.5 * root * 0.044715) * square)
    return ((hidden * half - target.astype(F32)) * deriv).astype(BF16)


def joined(x_ref):
    return jnp.concatenate([x_ref[k] for k in range(x_ref.shape[0])], axis=1)


def cost(rows, deep, cols, exps=0):
    return pl.CostEstimate(
        flops=2 * rows * deep * cols, bytes_accessed=2 * deep * (rows + cols) + 4 * rows * cols, transcendentals=exps
    )


def add_term(s, x, far_ref, total_ref):
    part = jnp.dot(s, x, preferred_element_type=F32)
    step = pl.program_id(0)

    @pl.when(step == 0)
    def _():
        total_ref[...] = part

    @pl.when(step > 0)
    def _():
        total_ref[...] += part

    @pl.when(step == pl.num_programs(0) - 1)
    def _():
        far_ref[...] = total_ref[...].astype(BF16)


def first_slopes(x, w, t, which):
    blocks, rows, wide = x.shape
    cols, deep = w[0].shape
    tile = rows // N
    per = deep // wide
    out = pl.BlockSpec((cols, tile), lambda i, which: (0, i))
    whole = pl.BlockSpec((cols, deep), lambda i, which: (0, 0), pipeline_mode=pl.Buffered(1))

    def kernel(which_ref, x_ref, *refs):
        w_refs, (t_ref, h_ref, s_ref, far_ref, total_ref) = refs[:N], refs[N:]
        block = lambda j: [x_ref[per * which_ref[j] + k] for k in range(per)]
        x = jnp.concatenate([part for j in range(N) for part in block(j)], axis=1)
        w = jnp.concatenate([w_ref[...] for w_ref in w_refs], axis=1)
        hidden = lax.dot_general(w, x, NT, preferred_element_type=F32)
        h_ref[...] = hidden
        s = slope_of(hidden, t_ref[0])
        s_ref[...] = s
        add_term(s, jnp.concatenate(block(2), axis=1), far_ref, total_ref)

    return pl.pallas_call(
        kernel,
        grid_spec=pltpu.PrefetchScalarGridSpec(
            num_scalar_prefetch=1,
            grid=(N,),
            in_specs=[pl.BlockSpec((blocks, tile, wide), lambda i, which: (0, i, 0))]
            + [whole] * N
            + [pl.BlockSpec((1, cols, tile), lambda i, which: (which[N + i], 0, 0))],
            out_specs=[out, out, pl.BlockSpec((cols, deep), lambda i, which: (0, 0))],
            scratch_shapes=[pltpu.VMEM((cols, deep), F32)],
        ),
        out_shape=[
            jax.ShapeDtypeStruct((cols, rows), F32),
            jax.ShapeDtypeStruct((cols, rows), BF16),
            jax.ShapeDtypeStruct((cols, deep), BF16),
        ],
        compiler_params=PARAMS,
        cost_estimate=cost(cols, (blocks + per) * wide, rows, rows * cols),
    )(jnp.stack(which).astype(jnp.int32), x, *w, t)


def moved(x, pieces, which):
    blocks, rows, wide = x.shape
    cols, deep = pieces[0].shape
    per = deep // wide
    tile = rows // N
    count = len(pieces)
    at = lambda j: pl.BlockSpec((per, tile, wide), lambda i, which: (which[j], i, 0))

    def kernel(which_ref, *refs):
        xs, fs = refs[:count], refs[count : 2 * count]
        x = jnp.concatenate([x_ref[k] for x_ref in xs for k in range(per)], axis=1)
        f = jnp.concatenate([f_ref[...] for f_ref in fs], axis=1)
        refs[-1][...] = lax.dot_general(f, x, NT, preferred_element_type=F32)

    return pl.pallas_call(
        kernel,
        grid_spec=pltpu.PrefetchScalarGridSpec(
            num_scalar_prefetch=1,
            grid=(N,),
            in_specs=[at(j) for j in range(count)] + [pl.BlockSpec((cols, deep), lambda i, which: (0, 0))] * count,
            out_specs=pl.BlockSpec((cols, tile), lambda i, which: (0, i)),
        ),
        out_shape=jax.ShapeDtypeStruct((cols, rows), F32),
        compiler_params=PARAMS,
        cost_estimate=cost(cols, deep * count, rows),
    )(jnp.stack(which).astype(jnp.int32), *([x] * count), *pieces)


def second_slopes(x, piece, which, part, scale, hidden, t):
    blocks, rows, wide = x.shape
    cols, deep = piece.shape
    per = deep // wide
    tile = rows // N
    out = pl.BlockSpec((cols, tile), lambda i, which: (0, i))
    whole = pl.BlockSpec((cols, deep), lambda i, which: (0, 0))

    def kernel(which_ref, scale_ref, x_ref, f_ref, part_ref, h_ref, t_ref, s_ref, far_ref, total_ref):
        x = joined(x_ref)
        move = part_ref[...] + lax.dot_general(f_ref[...], x, NT, preferred_element_type=F32)
        s = slope_of(h_ref[...] + scale_ref[0, 0] * move, t_ref[0])
        s_ref[...] = s
        add_term(s, x, far_ref, total_ref)

    return pl.pallas_call(
        kernel,
        grid_spec=pltpu.PrefetchScalarGridSpec(
            num_scalar_prefetch=1,
            grid=(N,),
            in_specs=[
                pl.BlockSpec(memory_space=pltpu.SMEM),
                pl.BlockSpec((per, tile, wide), lambda i, which: (which[0], i, 0)),
                whole,
                out,
                out,
                pl.BlockSpec((1, cols, tile), lambda i, which: (which[1 + i], 0, 0)),
            ],
            out_specs=[out, whole],
            scratch_shapes=[pltpu.VMEM((cols, deep), F32)],
        ),
        out_shape=[jax.ShapeDtypeStruct((cols, rows), BF16), jax.ShapeDtypeStruct((cols, deep), BF16)],
        compiler_params=PARAMS,
        cost_estimate=cost(cols, 2 * deep, rows, rows * cols),
    )(jnp.stack(which).astype(jnp.int32), scale, x, piece, part, hidden, t)


def terms(x, s, which, cut):
    blocks, rows, wide = x.shape
    cols = s.shape[0]
    half = cols // 2
    tile = rows // 2
    per = blocks // N
    count = len(which)
    at = lambda j: pl.BlockSpec((per, tile, wide), lambda i, which: (which[j], i, 0))
    kinds = [F32, BF16, BF16, F32] if cut else [F32] * count
    tall = half if cut else cols

    def kernel(which_ref, *refs):
        s_ref = refs[count]
        outs, totals = refs[count + 1 : -count], refs[-count:]
        parts = [jnp.dot(s_ref[...], joined(refs[j]), preferred_element_type=F32) for j in range(count)]

        @pl.when(pl.program_id(0) == 0)
        def _():
            for j in range(count):
                totals[j][...] = parts[j]

        @pl.when(pl.program_id(0) > 0)
        def _():
            for j in range(count):
                total = totals[j][...] + parts[j]
                for n in range(cols // tall):
                    out = outs[j * (cols // tall) + n]
                    out[...] = total[n * tall : (n + 1) * tall].astype(out.dtype)

    return pl.pallas_call(
        kernel,
        grid_spec=pltpu.PrefetchScalarGridSpec(
            num_scalar_prefetch=1,
            grid=(rows // tile,),
            in_specs=[at(j) for j in range(count)] + [pl.BlockSpec((cols, tile), lambda i, which: (0, i))],
            out_specs=[pl.BlockSpec((tall, per * wide), lambda i, which: (0, 0))] * len(kinds),
            scratch_shapes=[pltpu.VMEM((cols, per * wide), F32)] * count,
        ),
        out_shape=[jax.ShapeDtypeStruct((tall, per * wide), kind) for kind in kinds],
        compiler_params=PARAMS,
        cost_estimate=cost(cols * count, rows, per * wide),
    )(jnp.stack(which).astype(jnp.int32), *([x] * count), s)


def ring_sum(x, s, far, me):
    at = lambda step: lax.rem(me + step, N)
    half = far.shape[0] // 2
    far_next, far_prev = shift(far[:half], "x", 1), shift(far[half:], "x", -1)
    high, to_next, to_prev, low = terms(x, s, [at(1), at(3)], True)
    next_low, prev_high = shift(to_next, "x", 1), shift(to_prev, "x", -1)
    next_high = shift((high + far_next.astype(F32)).astype(BF16), "x", 1)
    prev_low = shift((low + far_prev.astype(F32)).astype(BF16), "x", -1)
    (own,) = terms(x, s, [at(0)], False)
    high = own[:half] + next_high.astype(F32) + prev_high.astype(F32)
    low = own[half:] + next_low.astype(F32) + prev_low.astype(F32)
    return jnp.concatenate([high, low], axis=0)


def ring_gather(value, axis):
    return [value, shift(value, axis, -1), shift(value, axis, 2), shift(value, axis, 1)]


def ring_gather_halves(value, axis):
    half = value.shape[0] // 2
    after, before = shift(value, axis, -1), shift(value, axis, 1)
    far = jnp.concatenate([shift(before[:half], axis, 1), shift(after[half:], axis, -1)], axis=0)
    return [value, after, far, before]


def ring_swap(chunk, axis):
    return [chunk(0), shift(chunk(3), axis, -1), shift(chunk(2), axis, 2), shift(chunk(1), axis, 1)]


def cut_kernel(which_ref, own, after, far, before, to_next, to_prev, kept):
    rows = own.shape[0]
    half = rows // 2
    turned = far[...].T
    to_next[:, :rows], to_next[:, rows:] = after[...].T, turned[:, :half]
    to_prev[:, :rows], to_prev[:, rows:] = before[...].T, turned[:, half:]
    kept[...] = own[...].T


def cut(array, me):
    rows, cols = array.shape[0], array.shape[1] // N
    at = lambda k: pl.BlockSpec((rows, cols), lambda i, which: (0, which[k]))
    wide = [rows + rows // 2, rows + rows // 2, rows]
    return pl.pallas_call(
        cut_kernel,
        grid_spec=pltpu.PrefetchScalarGridSpec(
            num_scalar_prefetch=1,
            grid=(1,),
            in_specs=[at(k) for k in range(N)],
            out_specs=[pl.BlockSpec((cols, size), lambda i, which: (0, 0)) for size in wide],
        ),
        out_shape=[jax.ShapeDtypeStruct((cols, size), array.dtype) for size in wide],
        compiler_params=PARAMS,
        cost_estimate=cost(0, 0, 0),
    )(jnp.stack([lax.rem(me + k, N) for k in range(N)]).astype(jnp.int32), *([array] * N))


def ring_swap_halves(to_next, to_prev, kept, axis):
    size = kept.shape[1]
    prev, after = shift(to_next, axis, 1), shift(to_prev, axis, -1)
    high, low = shift(prev[:, size:], axis, 1), shift(after[:, size:], axis, -1)
    return [kept, after[:, :size], jnp.concatenate([high, low], axis=1), prev[:, :size]]


def in_order(pieces, me):
    twice = jnp.stack(pieces + pieces)
    return lax.dynamic_slice_in_dim(twice, lax.rem(N - me, N), N, axis=0)


def total_of(value, beside):
    total = jnp.full((N * N * N, 128), jnp.sum(value * value), F32)
    total = total + lax.ppermute(total, "c", [(0, 1), (1, 0)])
    each = lax.all_to_all(total, ("x", "y", "z"), split_axis=0, concat_axis=0, tiled=True)
    if beside is not None:
        each, beside = lax.optimization_barrier((each, beside))
    return jnp.sum(each[:, 0]), beside


def per_device(tokens, target, weight):
    ix, iy = lax.axis_index("x"), lax.axis_index("y")
    rows, wide = tokens.shape
    cols = weight.shape[1] // N
    width = wide * 2 * N
    hidden_all = weight.shape[1] * 2 * N

    x = lax.all_gather(tokens, ("z", "c", "y"), axis=0, tiled=True).reshape(2 * N, N * rows, wide)

    def columns(array):
        return lambda k: lax.dynamic_slice_in_dim(array, lax.rem(iy + k, N) * cols, cols, axis=1)

    to_next, to_prev, kept = cut(target, iy)
    w_pieces = ring_swap(columns(weight), "y")
    to_next, to_prev = lax.optimization_barrier((to_next, to_prev, *w_pieces))[:2]
    t = jnp.stack(ring_swap_halves(to_next, to_prev, kept, "y"))
    tiles = [lax.rem(k + N - iy, N) for k in range(N)]
    w = ring_gather(in_order(w_pieces, iy).reshape(-1, cols).T, "x")

    at = lambda k: lax.rem(ix + k, N)
    hidden, slope, term = first_slopes(x, w, t, [at(k) for k in range(N)] + tiles)
    first = ring_sum(x, slope, term, ix)
    own, after, far, before = ring_gather_halves(first.astype(BF16), "x")
    part = moved(x, [own, after, before], [at(0), at(1), at(3)])
    total, part = total_of(first, part)
    scale = 0.5 * math.sqrt(hidden_all) / jnp.sqrt(total + 1e-06)
    slope, term = second_slopes(x, far, [at(2)] + tiles, part, scale.reshape(1, 1), hidden, t)
    second = ring_sum(x, slope, term, ix)
    total, _ = total_of(second, None)
    factor = jnp.minimum(1.0, math.sqrt(width * hidden_all) / jnp.sqrt(total + 1e-06))
    held = second.astype(BF16).T.reshape(N, -1, cols)
    parts = in_order(ring_swap(lambda k: lax.dynamic_index_in_dim(held, lax.rem(iy + k, N), 0, keepdims=False), "y"), iy)
    whole = jnp.concatenate([parts[k] for k in range(N)], axis=1)
    return whole.astype(F32) * factor


def solution(mesh):
    grid = Mesh(mesh.devices.reshape(N, N, N, 2), ("x", "y", "z", "c"))
    spec = P(("x", "y"), ("z", "c"))
    return jax.shard_map(
        per_device, mesh=grid, in_specs=(spec, spec, spec), out_specs=spec, check_vma=False
    )
```

```python
import math

import jax
import jax.numpy as jnp
from jax import lax
from jax.experimental import pallas as pl
from jax.experimental.pallas import tpu as pltpu
from jax.sharding import Mesh, PartitionSpec as P

BF16, F32 = jnp.bfloat16, jnp.float32
N = 4
NT = (((1,), (1,)), ((), ()))
FIRST = pltpu.CompilerParams(vmem_limit_bytes=36 << 20)
MOVED = pltpu.CompilerParams(vmem_limit_bytes=24 << 20)
TERMS = pltpu.CompilerParams(vmem_limit_bytes=20 << 20)


def shift(value, axis, step):
    return lax.ppermute(value, axis, [(i, (i + step) % N) for i in range(N)])


def behind(value, *others):
    return lax.optimization_barrier((value, *others))[0]


def slope_of(hidden, target):
    root = math.sqrt(2.0 / math.pi)
    square = hidden * hidden
    bend = jnp.tanh(hidden * (root + (root * 0.044715) * square))
    half = 0.5 + 0.5 * bend
    deriv = half + (hidden * (1.0 - bend * bend)) * (0.5 * root + (1.5 * root * 0.044715) * square)
    return ((hidden * half - target.astype(F32)) * deriv).astype(BF16)


def joined(x_ref):
    return jnp.concatenate([x_ref[k] for k in range(x_ref.shape[0])], axis=1)


def cost(rows, deep, cols, exps=0):
    return pl.CostEstimate(
        flops=2 * rows * deep * cols, bytes_accessed=2 * deep * (rows + cols) + 4 * rows * cols, transcendentals=exps
    )


def add_term(s, x, far_ref, total_ref):
    part = jnp.dot(s, x, preferred_element_type=F32)
    step = pl.program_id(0)

    @pl.when(step == 0)
    def _():
        total_ref[...] = part

    @pl.when(step > 0)
    def _():
        total_ref[...] += part

    @pl.when(step == pl.num_programs(0) - 1)
    def _():
        far_ref[...] = total_ref[...].astype(BF16)


def first_slopes(x, w, t, which):
    blocks, rows, wide = x.shape
    cols, deep = w[0].shape
    tile = rows // N
    per = deep // wide
    out = pl.BlockSpec((cols, tile), lambda i, which: (0, i))
    whole = pl.BlockSpec((cols, deep), lambda i, which: (0, 0), pipeline_mode=pl.Buffered(1))

    def kernel(which_ref, x_ref, *refs):
        w_refs, (t_ref, h_ref, s_ref, far_ref, total_ref) = refs[:N], refs[N:]
        block = lambda j: [x_ref[per * which_ref[j] + k] for k in range(per)]
        x = jnp.concatenate([part for j in range(N) for part in block(j)], axis=1)
        w = jnp.concatenate([w_ref[...] for w_ref in w_refs], axis=1)
        hidden = lax.dot_general(w, x, NT, preferred_element_type=F32)
        h_ref[...] = hidden
        s = slope_of(hidden, t_ref[0])
        s_ref[...] = s
        add_term(s, jnp.concatenate(block(2), axis=1), far_ref, total_ref)

    return pl.pallas_call(
        kernel,
        grid_spec=pltpu.PrefetchScalarGridSpec(
            num_scalar_prefetch=1,
            grid=(N,),
            in_specs=[pl.BlockSpec((blocks, tile, wide), lambda i, which: (0, i, 0))]
            + [whole] * N
            + [pl.BlockSpec((1, cols, tile), lambda i, which: (which[N + i], 0, 0))],
            out_specs=[out, out, pl.BlockSpec((cols, deep), lambda i, which: (0, 0))],
            scratch_shapes=[pltpu.VMEM((cols, deep), F32)],
        ),
        out_shape=[
            jax.ShapeDtypeStruct((cols, rows), F32),
            jax.ShapeDtypeStruct((cols, rows), BF16),
            jax.ShapeDtypeStruct((cols, deep), BF16),
        ],
        compiler_params=FIRST,
        cost_estimate=cost(cols, (blocks + per) * wide, rows, rows * cols),
    )(jnp.stack(which).astype(jnp.int32), x, *w, t)


def moved(x, pieces, which):
    blocks, rows, wide = x.shape
    cols, deep = pieces[0].shape
    per = deep // wide
    tile = rows // N
    count = len(pieces)
    at = lambda j: pl.BlockSpec((per, tile, wide), lambda i, which: (which[j], i, 0))

    def kernel(which_ref, *refs):
        xs, fs = refs[:count], refs[count : 2 * count]
        x = jnp.concatenate([x_ref[k] for x_ref in xs for k in range(per)], axis=1)
        f = jnp.concatenate([f_ref[...] for f_ref in fs], axis=1)
        refs[-1][...] = lax.dot_general(f, x, NT, preferred_element_type=F32)

    return pl.pallas_call(
        kernel,
        grid_spec=pltpu.PrefetchScalarGridSpec(
            num_scalar_prefetch=1,
            grid=(N,),
            in_specs=[at(j) for j in range(count)] + [pl.BlockSpec((cols, deep), lambda i, which: (0, 0))] * count,
            out_specs=pl.BlockSpec((cols, tile), lambda i, which: (0, i)),
        ),
        out_shape=jax.ShapeDtypeStruct((cols, rows), F32),
        compiler_params=MOVED,
        cost_estimate=cost(cols, deep * count, rows),
    )(jnp.stack(which).astype(jnp.int32), *([x] * count), *pieces)


def second_slopes(x, piece, which, part, scale, hidden, t):
    blocks, rows, wide = x.shape
    cols, deep = piece.shape
    per = deep // wide
    tile = rows // N
    out = pl.BlockSpec((cols, tile), lambda i, which: (0, i))
    whole = pl.BlockSpec((cols, deep), lambda i, which: (0, 0))

    def kernel(which_ref, scale_ref, x_ref, f_ref, part_ref, h_ref, t_ref, s_ref, far_ref, total_ref):
        x = joined(x_ref)
        move = part_ref[...] + lax.dot_general(f_ref[...], x, NT, preferred_element_type=F32)
        s = slope_of(h_ref[...] + scale_ref[0, 0] * move, t_ref[0])
        s_ref[...] = s
        add_term(s, x, far_ref, total_ref)

    return pl.pallas_call(
        kernel,
        grid_spec=pltpu.PrefetchScalarGridSpec(
            num_scalar_prefetch=1,
            grid=(N,),
            in_specs=[
                pl.BlockSpec(memory_space=pltpu.SMEM),
                pl.BlockSpec((per, tile, wide), lambda i, which: (which[0], i, 0)),
                whole,
                out,
                out,
                pl.BlockSpec((1, cols, tile), lambda i, which: (which[1 + i], 0, 0)),
            ],
            out_specs=[out, whole],
            scratch_shapes=[pltpu.VMEM((cols, deep), F32)],
        ),
        out_shape=[jax.ShapeDtypeStruct((cols, rows), BF16), jax.ShapeDtypeStruct((cols, deep), BF16)],
        compiler_params=MOVED,
        cost_estimate=cost(cols, 2 * deep, rows, rows * cols),
    )(jnp.stack(which).astype(jnp.int32), scale, x, piece, part, hidden, t)


def terms(x, s, which, cut):
    blocks, rows, wide = x.shape
    cols = s.shape[0]
    half = cols // 2
    tile = rows // 2
    per = blocks // N
    count = len(which)
    at = lambda j: pl.BlockSpec((per, tile, wide), lambda i, which: (which[j], i, 0))
    kinds = [F32, BF16, BF16, F32] if cut else [F32] * count
    tall = half if cut else cols

    def kernel(which_ref, *refs):
        s_ref = refs[count]
        outs, totals = refs[count + 1 : -count], refs[-count:]
        parts = [jnp.dot(s_ref[...], joined(refs[j]), preferred_element_type=F32) for j in range(count)]

        @pl.when(pl.program_id(0) == 0)
        def _():
            for j in range(count):
                totals[j][...] = parts[j]

        @pl.when(pl.program_id(0) > 0)
        def _():
            for j in range(count):
                total = totals[j][...] + parts[j]
                for n in range(cols // tall):
                    out = outs[j * (cols // tall) + n]
                    out[...] = total[n * tall : (n + 1) * tall].astype(out.dtype)

    return pl.pallas_call(
        kernel,
        grid_spec=pltpu.PrefetchScalarGridSpec(
            num_scalar_prefetch=1,
            grid=(rows // tile,),
            in_specs=[at(j) for j in range(count)] + [pl.BlockSpec((cols, tile), lambda i, which: (0, i))],
            out_specs=[pl.BlockSpec((tall, per * wide), lambda i, which: (0, 0))] * len(kinds),
            scratch_shapes=[pltpu.VMEM((cols, per * wide), F32)] * count,
        ),
        out_shape=[jax.ShapeDtypeStruct((tall, per * wide), kind) for kind in kinds],
        compiler_params=TERMS,
        cost_estimate=cost(cols * count, rows, per * wide),
    )(jnp.stack(which).astype(jnp.int32), *([x] * count), s)


def ring_sum(x, s, far, me):
    at = lambda step: lax.rem(me + step, N)
    half = far.shape[0] // 2
    far_next, far_prev = shift(far[:half], "x", 1), shift(far[half:], "x", -1)
    high, to_next, to_prev, low = terms(x, s, [at(1), at(3)], True)
    next_low, prev_high = shift(to_next, "x", 1), shift(to_prev, "x", -1)
    next_high = shift((high + far_next.astype(F32)).astype(BF16), "x", 1)
    prev_low = shift((low + far_prev.astype(F32)).astype(BF16), "x", -1)
    (own,) = terms(x, s, [at(0)], False)
    high = own[:half] + next_high.astype(F32) + prev_high.astype(F32)
    low = own[half:] + next_low.astype(F32) + prev_low.astype(F32)
    return jnp.concatenate([high, low], axis=0)


def ring_gather(value, axis):
    return [value, shift(value, axis, -1), shift(value, axis, 2), shift(value, axis, 1)]


def ring_gather_halves(value, axis):
    half = value.shape[0] // 2
    after, before = shift(value, axis, -1), shift(value, axis, 1)
    far = jnp.concatenate([shift(before[:half], axis, 1), shift(after[half:], axis, -1)], axis=0)
    return [value, after, far, before]


def ring_swap(chunk, axis):
    return [chunk(0), shift(chunk(3), axis, -1), shift(chunk(2), axis, 2), shift(chunk(1), axis, 1)]


def cut_kernel(which_ref, own, after, far, before, to_next, to_prev, kept):
    rows = own.shape[0]
    half = rows // 2
    turned = far[...].T
    to_next[:, :rows], to_next[:, rows:] = after[...].T, turned[:, :half]
    to_prev[:, :rows], to_prev[:, rows:] = before[...].T, turned[:, half:]
    kept[...] = own[...].T


def cut(array, me):
    rows, cols = array.shape[0], array.shape[1] // N
    at = lambda k: pl.BlockSpec((rows, cols), lambda i, which: (0, which[k]))
    wide = [rows + rows // 2, rows + rows // 2, rows]
    return pl.pallas_call(
        cut_kernel,
        grid_spec=pltpu.PrefetchScalarGridSpec(
            num_scalar_prefetch=1,
            grid=(1,),
            in_specs=[at(k) for k in range(N)],
            out_specs=[pl.BlockSpec((cols, size), lambda i, which: (0, 0)) for size in wide],
        ),
        out_shape=[jax.ShapeDtypeStruct((cols, size), array.dtype) for size in wide],
        compiler_params=FIRST,
        cost_estimate=cost(0, 0, 0),
    )(jnp.stack([lax.rem(me + k, N) for k in range(N)]).astype(jnp.int32), *([array] * N))


def ring_swap_halves(to_next, to_prev, kept, axis):
    size = kept.shape[1]
    prev, after = shift(to_next, axis, 1), shift(to_prev, axis, -1)
    high, low = shift(prev[:, size:], axis, 1), shift(after[:, size:], axis, -1)
    return [kept, after[:, :size], jnp.concatenate([high, low], axis=1), prev[:, :size]]


def in_order(pieces, me):
    twice = jnp.stack(pieces + pieces)
    return lax.dynamic_slice_in_dim(twice, lax.rem(N - me, N), N, axis=0)


def total_of(value, beside):
    total = jnp.full((N * N * N, 128), jnp.sum(value * value), F32)
    total = total + lax.ppermute(total, "c", [(0, 1), (1, 0)])
    each = lax.all_to_all(total, ("x", "y", "z"), split_axis=0, concat_axis=0, tiled=True)
    if beside is not None:
        each, beside = lax.optimization_barrier((each, beside))
    return jnp.sum(each[:, 0]), beside


def per_device(tokens, target, weight):
    ix, iy = lax.axis_index("x"), lax.axis_index("y")
    rows, wide = tokens.shape
    cols = weight.shape[1] // N
    width = wide * 2 * N
    hidden_all = weight.shape[1] * 2 * N

    x = lax.all_gather(tokens, ("z", "c", "y"), axis=0, tiled=True).reshape(2 * N, N * rows, wide)

    def columns(array):
        return lambda k: lax.dynamic_slice_in_dim(array, lax.rem(iy + k, N) * cols, cols, axis=1)

    to_next, to_prev, kept = cut(target, iy)
    w_pieces = ring_swap(columns(weight), "y")
    to_next, to_prev = lax.optimization_barrier((to_next, to_prev, *w_pieces))[:2]
    t = jnp.stack(ring_swap_halves(to_next, to_prev, kept, "y"))
    tiles = [lax.rem(k + N - iy, N) for k in range(N)]
    w = ring_gather(in_order(w_pieces, iy).reshape(-1, cols).T, "x")

    at = lambda k: lax.rem(ix + k, N)
    x = pltpu.with_memory_space_constraint(x, pltpu.HBM)
    hidden, slope, term = first_slopes(x, w, t, [at(k) for k in range(N)] + tiles)
    first = ring_sum(x, slope, term, ix)
    own, after, far, before = ring_gather_halves(first.astype(BF16), "x")
    part = moved(x, [own, after, before], [at(0), at(1), at(3)])
    total, part = total_of(first, part)
    scale = 0.5 * math.sqrt(hidden_all) / jnp.sqrt(total + 1e-06)
    slope, term = second_slopes(x, far, [at(2)] + tiles, part, scale.reshape(1, 1), hidden, t)
    second = ring_sum(x, slope, term, ix)
    total, _ = total_of(second, None)
    factor = jnp.minimum(1.0, math.sqrt(width * hidden_all) / jnp.sqrt(total + 1e-06))
    held = second.astype(BF16).T.reshape(N, -1, cols)
    parts = in_order(ring_swap(lambda k: lax.dynamic_index_in_dim(held, lax.rem(iy + k, N), 0, keepdims=False), "y"), iy)
    whole = jnp.concatenate([parts[k] for k in range(N)], axis=1)
    return whole.astype(F32) * factor


def solution(mesh):
    grid = Mesh(mesh.devices.reshape(N, N, N, 2), ("x", "y", "z", "c"))
    spec = P(("x", "y"), ("z", "c"))
    return jax.shard_map(
        per_device, mesh=grid, in_specs=(spec, spec, spec), out_specs=spec, check_vma=False
    )
```

```python
import math

import jax
import jax.numpy as jnp
from jax import lax
from jax.experimental import pallas as pl
from jax.experimental.pallas import tpu as pltpu
from jax.sharding import Mesh, PartitionSpec as P

BF16, F32 = jnp.bfloat16, jnp.float32
N = 4
NT = (((1,), (1,)), ((), ()))
PARAMS = pltpu.CompilerParams(vmem_limit_bytes=52 << 20)


def shift(value, axis, step):
    return lax.ppermute(value, axis, [(i, (i + step) % N) for i in range(N)])


def behind(value, *others):
    return lax.optimization_barrier((value, *others))[0]


def slope_of(hidden, target):
    root = math.sqrt(2.0 / math.pi)
    square = hidden * hidden
    bend = jnp.tanh(hidden * (root + (root * 0.044715) * square))
    half = 0.5 + 0.5 * bend
    deriv = half + (hidden * (1.0 - bend * bend)) * (0.5 * root + (1.5 * root * 0.044715) * square)
    return ((hidden * half - target.astype(F32)) * deriv).astype(BF16)


def joined(x_ref):
    groups = [
        jnp.concatenate([x_ref[g, k] for k in range(x_ref.shape[1])], axis=1) for g in range(x_ref.shape[0])
    ]
    return groups[0] if len(groups) == 1 else jnp.concatenate(groups, axis=0)


def cost(rows, deep, cols, exps=0):
    return pl.CostEstimate(
        flops=2 * rows * deep * cols, bytes_accessed=2 * deep * (rows + cols) + 4 * rows * cols, transcendentals=exps
    )


def add_term(s, x, far_ref, total_ref):
    part = jnp.dot(s, x, preferred_element_type=F32)
    step = pl.program_id(0)

    @pl.when(step == 0)
    def _():
        total_ref[...] = part

    @pl.when(step > 0)
    def _():
        total_ref[...] += part

    @pl.when(step == pl.num_programs(0) - 1)
    def _():
        far_ref[...] = total_ref[...].astype(BF16)


def first_slopes(x, w, t, which):
    groups, blocks, tile, wide = x.shape
    rows = groups * tile
    cols, deep = w[0].shape
    per = deep // wide
    out = pl.BlockSpec((cols, tile), lambda i, which: (0, i))
    whole = pl.BlockSpec((cols, deep), lambda i, which: (0, 0), pipeline_mode=pl.Buffered(1))

    def kernel(which_ref, x_ref, *refs):
        w_refs, (t_ref, h_ref, s_ref, far_ref, total_ref) = refs[:N], refs[N:]
        block = lambda j: [x_ref[0, per * which_ref[j] + k] for k in range(per)]
        x = jnp.concatenate([part for j in range(N) for part in block(j)], axis=1)
        w = jnp.concatenate([w_ref[...] for w_ref in w_refs], axis=1)
        hidden = lax.dot_general(w, x, NT, preferred_element_type=F32)
        h_ref[...] = hidden
        s = slope_of(hidden, t_ref[0])
        s_ref[...] = s
        add_term(s, jnp.concatenate(block(2), axis=1), far_ref, total_ref)

    return pl.pallas_call(
        kernel,
        grid_spec=pltpu.PrefetchScalarGridSpec(
            num_scalar_prefetch=1,
            grid=(N,),
            in_specs=[pl.BlockSpec((1, blocks, tile, wide), lambda i, which: (i, 0, 0, 0))]
            + [whole] * N
            + [pl.BlockSpec((1, cols, tile), lambda i, which: (which[N + i], 0, 0))],
            out_specs=[out, out, pl.BlockSpec((cols, deep), lambda i, which: (0, 0))],
            scratch_shapes=[pltpu.VMEM((cols, deep), F32)],
        ),
        out_shape=[
            jax.ShapeDtypeStruct((cols, rows), F32),
            jax.ShapeDtypeStruct((cols, rows), BF16),
            jax.ShapeDtypeStruct((cols, deep), BF16),
        ],
        compiler_params=PARAMS,
        cost_estimate=cost(cols, (blocks + per) * wide, rows, rows * cols),
    )(jnp.stack(which).astype(jnp.int32), x, *w, t)


def moved(x, pieces, which):
    groups, blocks, tile, wide = x.shape
    rows = groups * tile
    cols, deep = pieces[0].shape
    per = deep // wide
    count = len(pieces)
    at = lambda j: pl.BlockSpec((1, per, tile, wide), lambda i, which: (i, which[j], 0, 0))

    def kernel(which_ref, *refs):
        xs, fs = refs[:count], refs[count : 2 * count]
        x = jnp.concatenate([x_ref[0, k] for x_ref in xs for k in range(per)], axis=1)
        f = jnp.concatenate([f_ref[...] for f_ref in fs], axis=1)
        refs[-1][...] = lax.dot_general(f, x, NT, preferred_element_type=F32)

    return pl.pallas_call(
        kernel,
        grid_spec=pltpu.PrefetchScalarGridSpec(
            num_scalar_prefetch=1,
            grid=(N,),
            in_specs=[at(j) for j in range(count)] + [pl.BlockSpec((cols, deep), lambda i, which: (0, 0))] * count,
            out_specs=pl.BlockSpec((cols, tile), lambda i, which: (0, i)),
        ),
        out_shape=jax.ShapeDtypeStruct((cols, rows), F32),
        compiler_params=PARAMS,
        cost_estimate=cost(cols, deep * count, rows),
    )(jnp.stack(which).astype(jnp.int32), *([x] * count), *pieces)


def second_slopes(x, piece, which, part, scale, hidden, t):
    groups, blocks, tile, wide = x.shape
    rows = groups * tile
    cols, deep = piece.shape
    per = deep // wide
    out = pl.BlockSpec((cols, tile), lambda i, which: (0, i))
    whole = pl.BlockSpec((cols, deep), lambda i, which: (0, 0))

    def kernel(which_ref, scale_ref, x_ref, f_ref, part_ref, h_ref, t_ref, s_ref, far_ref, total_ref):
        x = joined(x_ref)
        move = part_ref[...] + lax.dot_general(f_ref[...], x, NT, preferred_element_type=F32)
        s = slope_of(h_ref[...] + scale_ref[0, 0] * move, t_ref[0])
        s_ref[...] = s
        add_term(s, x, far_ref, total_ref)

    return pl.pallas_call(
        kernel,
        grid_spec=pltpu.PrefetchScalarGridSpec(
            num_scalar_prefetch=1,
            grid=(N,),
            in_specs=[
                pl.BlockSpec(memory_space=pltpu.SMEM),
                pl.BlockSpec((1, per, tile, wide), lambda i, which: (i, which[0], 0, 0)),
                whole,
                out,
                out,
                pl.BlockSpec((1, cols, tile), lambda i, which: (which[1 + i], 0, 0)),
            ],
            out_specs=[out, whole],
            scratch_shapes=[pltpu.VMEM((cols, deep), F32)],
        ),
        out_shape=[jax.ShapeDtypeStruct((cols, rows), BF16), jax.ShapeDtypeStruct((cols, deep), BF16)],
        compiler_params=PARAMS,
        cost_estimate=cost(cols, 2 * deep, rows, rows * cols),
    )(jnp.stack(which).astype(jnp.int32), scale, x, piece, part, hidden, t)


def terms(x, s, which, cut):
    groups, blocks, size, wide = x.shape
    rows = groups * size
    cols = s.shape[0]
    half = cols // 2
    tile = rows // 2
    per = blocks // N
    count = len(which)
    at = lambda j: pl.BlockSpec((groups // 2, per, size, wide), lambda i, which: (i, which[j], 0, 0))
    kinds = [F32, BF16, BF16, F32] if cut else [F32] * count
    tall = half if cut else cols

    def kernel(which_ref, *refs):
        s_ref = refs[count]
        outs, totals = refs[count + 1 : -count], refs[-count:]
        parts = [jnp.dot(s_ref[...], joined(refs[j]), preferred_element_type=F32) for j in range(count)]

        @pl.when(pl.program_id(0) == 0)
        def _():
            for j in range(count):
                totals[j][...] = parts[j]

        @pl.when(pl.program_id(0) > 0)
        def _():
            for j in range(count):
                total = totals[j][...] + parts[j]
                for n in range(cols // tall):
                    out = outs[j * (cols // tall) + n]
                    out[...] = total[n * tall : (n + 1) * tall].astype(out.dtype)

    return pl.pallas_call(
        kernel,
        grid_spec=pltpu.PrefetchScalarGridSpec(
            num_scalar_prefetch=1,
            grid=(rows // tile,),
            in_specs=[at(j) for j in range(count)] + [pl.BlockSpec((cols, tile), lambda i, which: (0, i))],
            out_specs=[pl.BlockSpec((tall, per * wide), lambda i, which: (0, 0))] * len(kinds),
            scratch_shapes=[pltpu.VMEM((cols, per * wide), F32)] * count,
        ),
        out_shape=[jax.ShapeDtypeStruct((tall, per * wide), kind) for kind in kinds],
        compiler_params=PARAMS,
        cost_estimate=cost(cols * count, rows, per * wide),
    )(jnp.stack(which).astype(jnp.int32), *([x] * count), s)


def ring_sum(x, s, far, me):
    at = lambda step: lax.rem(me + step, N)
    half = far.shape[0] // 2
    far_next, far_prev = shift(far[:half], "x", 1), shift(far[half:], "x", -1)
    high, to_next, to_prev, low = terms(x, s, [at(1), at(3)], True)
    next_low, prev_high = shift(to_next, "x", 1), shift(to_prev, "x", -1)
    next_high = shift((high + far_next.astype(F32)).astype(BF16), "x", 1)
    prev_low = shift((low + far_prev.astype(F32)).astype(BF16), "x", -1)
    (own,) = terms(x, s, [at(0)], False)
    high = own[:half] + next_high.astype(F32) + prev_high.astype(F32)
    low = own[half:] + next_low.astype(F32) + prev_low.astype(F32)
    return jnp.concatenate([high, low], axis=0)


def ring_gather(value, axis):
    return [value, shift(value, axis, -1), shift(value, axis, 2), shift(value, axis, 1)]


def ring_gather_halves(value, axis):
    half = value.shape[0] // 2
    after, before = shift(value, axis, -1), shift(value, axis, 1)
    far = jnp.concatenate([shift(before[:half], axis, 1), shift(after[half:], axis, -1)], axis=0)
    return [value, after, far, before]


def ring_swap(chunk, axis):
    return [chunk(0), shift(chunk(3), axis, -1), shift(chunk(2), axis, 2), shift(chunk(1), axis, 1)]


def cut_kernel(which_ref, own, after, far, before, to_next, to_prev, kept):
    rows = own.shape[0]
    half = rows // 2
    turned = far[...].T
    to_next[:, :rows], to_next[:, rows:] = after[...].T, turned[:, :half]
    to_prev[:, :rows], to_prev[:, rows:] = before[...].T, turned[:, half:]
    kept[...] = own[...].T


def cut(array, me):
    rows, cols = array.shape[0], array.shape[1] // N
    at = lambda k: pl.BlockSpec((rows, cols), lambda i, which: (0, which[k]))
    wide = [rows + rows // 2, rows + rows // 2, rows]
    return pl.pallas_call(
        cut_kernel,
        grid_spec=pltpu.PrefetchScalarGridSpec(
            num_scalar_prefetch=1,
            grid=(1,),
            in_specs=[at(k) for k in range(N)],
            out_specs=[pl.BlockSpec((cols, size), lambda i, which: (0, 0)) for size in wide],
        ),
        out_shape=[jax.ShapeDtypeStruct((cols, size), array.dtype) for size in wide],
        compiler_params=PARAMS,
        cost_estimate=cost(0, 0, 0),
    )(jnp.stack([lax.rem(me + k, N) for k in range(N)]).astype(jnp.int32), *([array] * N))


def ring_swap_halves(to_next, to_prev, kept, axis):
    size = kept.shape[1]
    prev, after = shift(to_next, axis, 1), shift(to_prev, axis, -1)
    high, low = shift(prev[:, size:], axis, 1), shift(after[:, size:], axis, -1)
    return [kept, after[:, :size], jnp.concatenate([high, low], axis=1), prev[:, :size]]


def in_order(pieces, me):
    twice = jnp.stack(pieces + pieces)
    return lax.dynamic_slice_in_dim(twice, lax.rem(N - me, N), N, axis=0)


def total_of(value, beside):
    total = jnp.full((N * N * N, 128), jnp.sum(value * value), F32)
    total = total + lax.ppermute(total, "c", [(0, 1), (1, 0)])
    each = lax.all_to_all(total, ("x", "y", "z"), split_axis=0, concat_axis=0, tiled=True)
    if beside is not None:
        each, beside = lax.optimization_barrier((each, beside))
    return jnp.sum(each[:, 0]), beside


def per_device(tokens, target, weight):
    ix, iy = lax.axis_index("x"), lax.axis_index("y")
    rows, wide = tokens.shape
    cols = weight.shape[1] // N
    width = wide * 2 * N
    hidden_all = weight.shape[1] * 2 * N

    x = lax.all_gather(tokens, ("y", "z", "c"), axis=0, tiled=True).reshape(N, 2 * N, rows, wide)

    def columns(array):
        return lambda k: lax.dynamic_slice_in_dim(array, lax.rem(iy + k, N) * cols, cols, axis=1)

    to_next, to_prev, kept = cut(target, iy)
    w_pieces = ring_swap(columns(weight), "y")
    to_next, to_prev = lax.optimization_barrier((to_next, to_prev, *w_pieces))[:2]
    t = jnp.stack(ring_swap_halves(to_next, to_prev, kept, "y"))
    tiles = [lax.rem(k + N - iy, N) for k in range(N)]
    w = ring_gather(in_order(w_pieces, iy).reshape(-1, cols).T, "x")

    at = lambda k: lax.rem(ix + k, N)
    hidden, slope, term = first_slopes(x, w, t, [at(k) for k in range(N)] + tiles)
    first = ring_sum(x, slope, term, ix)
    own, after, far, before = ring_gather_halves(first.astype(BF16), "x")
    part = moved(x, [own, after, before], [at(0), at(1), at(3)])
    total, part = total_of(first, part)
    scale = 0.5 * math.sqrt(hidden_all) / jnp.sqrt(total + 1e-06)
    slope, term = second_slopes(x, far, [at(2)] + tiles, part, scale.reshape(1, 1), hidden, t)
    second = ring_sum(x, slope, term, ix)
    total, _ = total_of(second, None)
    factor = jnp.minimum(1.0, math.sqrt(width * hidden_all) / jnp.sqrt(total + 1e-06))
    held = second.astype(BF16).T.reshape(N, -1, cols)
    parts = in_order(ring_swap(lambda k: lax.dynamic_index_in_dim(held, lax.rem(iy + k, N), 0, keepdims=False), "y"), iy)
    whole = jnp.concatenate([parts[k] for k in range(N)], axis=1)
    return whole.astype(F32) * factor


def solution(mesh):
    grid = Mesh(mesh.devices.reshape(N, N, N, 2), ("x", "y", "z", "c"))
    spec = P(("x", "y"), ("z", "c"))
    return jax.shard_map(
        per_device, mesh=grid, in_specs=(spec, spec, spec), out_specs=spec, check_vma=False
    )
```

```python
import math

import jax
import jax.numpy as jnp
from jax import lax
from jax.experimental import pallas as pl
from jax.experimental.pallas import tpu as pltpu
from jax.sharding import Mesh, PartitionSpec as P

BF16, F32 = jnp.bfloat16, jnp.float32
N = 4
NT = (((1,), (1,)), ((), ()))
PARAMS = pltpu.CompilerParams(vmem_limit_bytes=52 << 20)


def shift(value, axis, step):
    return lax.ppermute(value, axis, [(i, (i + step) % N) for i in range(N)])


def behind(value, *others):
    return lax.optimization_barrier((value, *others))[0]


def slope_of(hidden, target):
    root = math.sqrt(2.0 / math.pi)
    square = hidden * hidden
    bend = jnp.tanh(hidden * (root + (root * 0.044715) * square))
    half = 0.5 + 0.5 * bend
    deriv = half + (hidden * (1.0 - bend * bend)) * (0.5 * root + (1.5 * root * 0.044715) * square)
    return ((hidden * half - target.astype(F32)) * deriv).astype(BF16)


def joined(x_ref):
    groups = [
        jnp.concatenate([x_ref[g, k] for k in range(x_ref.shape[1])], axis=1) for g in range(x_ref.shape[0])
    ]
    return groups[0] if len(groups) == 1 else jnp.concatenate(groups, axis=0)


def cost(rows, deep, cols, exps=0):
    return pl.CostEstimate(
        flops=2 * rows * deep * cols, bytes_accessed=2 * deep * (rows + cols) + 4 * rows * cols, transcendentals=exps
    )


def add_term(s, x, far_ref, total_ref):
    part = jnp.dot(s, x, preferred_element_type=F32)
    step = pl.program_id(0)

    @pl.when(step == 0)
    def _():
        total_ref[...] = part

    @pl.when(step > 0)
    def _():
        total_ref[...] += part

    @pl.when(step == pl.num_programs(0) - 1)
    def _():
        far_ref[...] = total_ref[...].astype(BF16)


def first_slopes(x, w, t, which):
    groups, blocks, tile, wide = x.shape
    rows = groups * tile
    cols, deep = w[0].shape
    per = deep // wide
    out = pl.BlockSpec((cols, tile), lambda i, which: (0, i))
    whole = pl.BlockSpec((cols, deep), lambda i, which: (0, 0), pipeline_mode=pl.Buffered(1))

    def kernel(which_ref, x_ref, *refs):
        w_refs, (t_ref, h_ref, s_ref, far_ref, total_ref) = refs[:N], refs[N:]
        block = lambda j: [x_ref[0, per * which_ref[j] + k] for k in range(per)]
        x = jnp.concatenate([part for j in range(N) for part in block(j)], axis=1)
        w = jnp.concatenate([w_ref[...] for w_ref in w_refs], axis=1)
        hidden = lax.dot_general(w, x, NT, preferred_element_type=F32)
        h_ref[...] = hidden
        s = slope_of(hidden, t_ref[0])
        s_ref[...] = s
        add_term(s, jnp.concatenate(block(2), axis=1), far_ref, total_ref)

    return pl.pallas_call(
        kernel,
        grid_spec=pltpu.PrefetchScalarGridSpec(
            num_scalar_prefetch=1,
            grid=(N,),
            in_specs=[pl.BlockSpec((1, blocks, tile, wide), lambda i, which: (i, 0, 0, 0))]
            + [whole] * N
            + [pl.BlockSpec((1, cols, tile), lambda i, which: (which[N + i], 0, 0))],
            out_specs=[out, out, pl.BlockSpec((cols, deep), lambda i, which: (0, 0))],
            scratch_shapes=[pltpu.VMEM((cols, deep), F32)],
        ),
        out_shape=[
            jax.ShapeDtypeStruct((cols, rows), F32),
            jax.ShapeDtypeStruct((cols, rows), BF16),
            jax.ShapeDtypeStruct((cols, deep), BF16),
        ],
        compiler_params=PARAMS,
        cost_estimate=cost(cols, (blocks + per) * wide, rows, rows * cols),
    )(jnp.stack(which).astype(jnp.int32), x, *w, t)


def moved(x, pieces, which):
    groups, blocks, tile, wide = x.shape
    rows = groups * tile
    cols, deep = pieces[0].shape
    per = deep // wide
    count = len(pieces)
    at = lambda j: pl.BlockSpec((1, per, tile, wide), lambda i, which: (i, which[j], 0, 0))

    def kernel(which_ref, *refs):
        xs, fs = refs[:count], refs[count : 2 * count]
        x = jnp.concatenate([x_ref[0, k] for x_ref in xs for k in range(per)], axis=1)
        f = jnp.concatenate([f_ref[...] for f_ref in fs], axis=1)
        refs[-1][...] = lax.dot_general(f, x, NT, preferred_element_type=F32)

    return pl.pallas_call(
        kernel,
        grid_spec=pltpu.PrefetchScalarGridSpec(
            num_scalar_prefetch=1,
            grid=(N,),
            in_specs=[at(j) for j in range(count)] + [pl.BlockSpec((cols, deep), lambda i, which: (0, 0))] * count,
            out_specs=pl.BlockSpec((cols, tile), lambda i, which: (0, i)),
        ),
        out_shape=jax.ShapeDtypeStruct((cols, rows), F32),
        compiler_params=PARAMS,
        cost_estimate=cost(cols, deep * count, rows),
    )(jnp.stack(which).astype(jnp.int32), *([x] * count), *pieces)


def second_slopes(x, piece, which, part, scale, hidden, t):
    groups, blocks, tile, wide = x.shape
    rows = groups * tile
    cols, deep = piece.shape
    per = deep // wide
    out = pl.BlockSpec((cols, tile), lambda i, which: (0, i))
    whole = pl.BlockSpec((cols, deep), lambda i, which: (0, 0))

    def kernel(which_ref, scale_ref, x_ref, f_ref, part_ref, h_ref, t_ref, s_ref, far_ref, total_ref):
        x = joined(x_ref)
        move = part_ref[...] + lax.dot_general(f_ref[...], x, NT, preferred_element_type=F32)
        s = slope_of(h_ref[...] + scale_ref[0, 0] * move, t_ref[0])
        s_ref[...] = s
        add_term(s, x, far_ref, total_ref)

    return pl.pallas_call(
        kernel,
        grid_spec=pltpu.PrefetchScalarGridSpec(
            num_scalar_prefetch=1,
            grid=(N,),
            in_specs=[
                pl.BlockSpec(memory_space=pltpu.SMEM),
                pl.BlockSpec((1, per, tile, wide), lambda i, which: (i, which[0], 0, 0)),
                whole,
                out,
                out,
                pl.BlockSpec((1, cols, tile), lambda i, which: (which[1 + i], 0, 0)),
            ],
            out_specs=[out, whole],
            scratch_shapes=[pltpu.VMEM((cols, deep), F32)],
        ),
        out_shape=[jax.ShapeDtypeStruct((cols, rows), BF16), jax.ShapeDtypeStruct((cols, deep), BF16)],
        compiler_params=PARAMS,
        cost_estimate=cost(cols, 2 * deep, rows, rows * cols),
    )(jnp.stack(which).astype(jnp.int32), scale, x, piece, part, hidden, t)


def terms(x, s, which, cut):
    groups, blocks, size, wide = x.shape
    rows = groups * size
    cols = s.shape[0]
    half = cols // 2
    tile = rows // 2
    per = blocks // N
    count = len(which)
    at = lambda j: pl.BlockSpec((groups // 2, per, size, wide), lambda i, which: (i, which[j], 0, 0))
    kinds = [F32, BF16, BF16, F32] if cut else [F32] * count
    tall = half if cut else cols

    def kernel(which_ref, *refs):
        s_ref = refs[count]
        outs, totals = refs[count + 1 : -count], refs[-count:]
        parts = [jnp.dot(s_ref[...], joined(refs[j]), preferred_element_type=F32) for j in range(count)]

        @pl.when(pl.program_id(0) == 0)
        def _():
            for j in range(count):
                totals[j][...] = parts[j]

        @pl.when(pl.program_id(0) > 0)
        def _():
            for j in range(count):
                total = totals[j][...] + parts[j]
                for n in range(cols // tall):
                    out = outs[j * (cols // tall) + n]
                    out[...] = total[n * tall : (n + 1) * tall].astype(out.dtype)

    return pl.pallas_call(
        kernel,
        grid_spec=pltpu.PrefetchScalarGridSpec(
            num_scalar_prefetch=1,
            grid=(rows // tile,),
            in_specs=[at(j) for j in range(count)] + [pl.BlockSpec((cols, tile), lambda i, which: (0, i))],
            out_specs=[pl.BlockSpec((tall, per * wide), lambda i, which: (0, 0))] * len(kinds),
            scratch_shapes=[pltpu.VMEM((cols, per * wide), F32)] * count,
        ),
        out_shape=[jax.ShapeDtypeStruct((tall, per * wide), kind) for kind in kinds],
        compiler_params=PARAMS,
        cost_estimate=cost(cols * count, rows, per * wide),
    )(jnp.stack(which).astype(jnp.int32), *([x] * count), s)


def ring_sum(x, s, far, me):
    at = lambda step: lax.rem(me + step, N)
    half = far.shape[0] // 2
    far_next, far_prev = shift(far[:half], "x", 1), shift(far[half:], "x", -1)
    high, to_next, to_prev, low = terms(x, s, [at(1), at(3)], True)
    next_low, prev_high = shift(to_next, "x", 1), shift(to_prev, "x", -1)
    next_high = shift((high + far_next.astype(F32)).astype(BF16), "x", 1)
    prev_low = shift((low + far_prev.astype(F32)).astype(BF16), "x", -1)
    (own,) = terms(x, s, [at(0)], False)
    high = own[:half] + next_high.astype(F32) + prev_high.astype(F32)
    low = own[half:] + next_low.astype(F32) + prev_low.astype(F32)
    return jnp.concatenate([high, low], axis=0)


def ring_gather(value, axis):
    return [value, shift(value, axis, -1), shift(value, axis, 2), shift(value, axis, 1)]


def ring_gather_halves(value, axis):
    half = value.shape[0] // 2
    after, before = shift(value, axis, -1), shift(value, axis, 1)
    far = jnp.concatenate([shift(before[:half], axis, 1), shift(after[half:], axis, -1)], axis=0)
    return [value, after, far, before]


def ring_swap(chunk, axis):
    return [chunk(0), shift(chunk(3), axis, -1), shift(chunk(2), axis, 2), shift(chunk(1), axis, 1)]


def cut_kernel(which_ref, own, after, far, before, to_next, to_prev, kept):
    rows = own.shape[0]
    half = rows // 2
    turned = far[...].T
    to_next[:, :rows], to_next[:, rows:] = after[...].T, turned[:, :half]
    to_prev[:, :rows], to_prev[:, rows:] = before[...].T, turned[:, half:]
    kept[...] = own[...].T


def cut(array, me):
    rows, cols = array.shape[0], array.shape[1] // N
    at = lambda k: pl.BlockSpec((rows, cols), lambda i, which: (0, which[k]))
    wide = [rows + rows // 2, rows + rows // 2, rows]
    return pl.pallas_call(
        cut_kernel,
        grid_spec=pltpu.PrefetchScalarGridSpec(
            num_scalar_prefetch=1,
            grid=(1,),
            in_specs=[at(k) for k in range(N)],
            out_specs=[pl.BlockSpec((cols, size), lambda i, which: (0, 0)) for size in wide],
        ),
        out_shape=[jax.ShapeDtypeStruct((cols, size), array.dtype) for size in wide],
        compiler_params=PARAMS,
        cost_estimate=cost(0, 0, 0),
    )(jnp.stack([lax.rem(me + k, N) for k in range(N)]).astype(jnp.int32), *([array] * N))


def ring_swap_halves(to_next, to_prev, kept, axis):
    size = kept.shape[1]
    prev, after = shift(to_next, axis, 1), shift(to_prev, axis, -1)
    high, low = shift(prev[:, size:], axis, 1), shift(after[:, size:], axis, -1)
    return [kept, after[:, :size], jnp.concatenate([high, low], axis=1), prev[:, :size]]


def in_order(pieces, me):
    twice = jnp.stack(pieces + pieces)
    return lax.dynamic_slice_in_dim(twice, lax.rem(N - me, N), N, axis=0)


def both(value):
    return value + lax.ppermute(value, "c", [(0, 1), (1, 0)])


def spread(value):
    return lax.all_to_all(value, ("x", "y", "z"), split_axis=0, concat_axis=0, tiled=True)


def total_beside(value, beside):
    part = jnp.full((N * N * N, 128), jnp.sum(value * value), F32)
    each, beside = lax.optimization_barrier((spread(both(part)), beside))
    return jnp.sum(each[:, 0]), beside


def total_of(value):
    each = spread(jnp.full((N * N * N, 128), jnp.sum(value * value), F32))
    return both(jnp.full((8, 128), jnp.sum(each[:, 0]), F32))[0, 0]


def per_device(tokens, target, weight):
    ix, iy = lax.axis_index("x"), lax.axis_index("y")
    rows, wide = tokens.shape
    cols = weight.shape[1] // N
    width = wide * 2 * N
    hidden_all = weight.shape[1] * 2 * N

    x = lax.all_gather(tokens, ("y", "z", "c"), axis=0, tiled=True).reshape(N, 2 * N, rows, wide)

    def columns(array):
        return lambda k: lax.dynamic_slice_in_dim(array, lax.rem(iy + k, N) * cols, cols, axis=1)

    to_next, to_prev, kept = cut(target, iy)
    w_pieces = ring_swap(columns(weight), "y")
    to_next, to_prev = lax.optimization_barrier((to_next, to_prev, *w_pieces))[:2]
    t = jnp.stack(ring_swap_halves(to_next, to_prev, kept, "y"))
    tiles = [lax.rem(k + N - iy, N) for k in range(N)]
    w = ring_gather(in_order(w_pieces, iy).reshape(-1, cols).T, "x")

    at = lambda k: lax.rem(ix + k, N)
    hidden, slope, term = first_slopes(x, w, t, [at(k) for k in range(N)] + tiles)
    first = ring_sum(x, slope, term, ix)
    own, after, far, before = ring_gather_halves(first.astype(BF16), "x")
    part = moved(x, [own, after, before], [at(0), at(1), at(3)])
    total, part = total_beside(first, part)
    scale = 0.5 * math.sqrt(hidden_all) / jnp.sqrt(total + 1e-06)
    slope, term = second_slopes(x, far, [at(2)] + tiles, part, scale.reshape(1, 1), hidden, t)
    second = ring_sum(x, slope, term, ix)
    total = total_of(second)
    factor = jnp.minimum(1.0, math.sqrt(width * hidden_all) / jnp.sqrt(total + 1e-06))
    held = second.astype(BF16).T.reshape(N, -1, cols)
    parts = in_order(ring_swap(lambda k: lax.dynamic_index_in_dim(held, lax.rem(iy + k, N), 0, keepdims=False), "y"), iy)
    whole = jnp.concatenate([parts[k] for k in range(N)], axis=1)
    return whole.astype(F32) * factor


def solution(mesh):
    grid = Mesh(mesh.devices.reshape(N, N, N, 2), ("x", "y", "z", "c"))
    spec = P(("x", "y"), ("z", "c"))
    return jax.shard_map(
        per_device, mesh=grid, in_specs=(spec, spec, spec), out_specs=spec, check_vma=False
    )
```

```python
import math

import jax
import jax.numpy as jnp
from jax import lax
from jax.experimental import pallas as pl
from jax.experimental.pallas import tpu as pltpu
from jax.sharding import Mesh, PartitionSpec as P

BF16, F32 = jnp.bfloat16, jnp.float32
N = 4
NT = (((1,), (1,)), ((), ()))
PARAMS = pltpu.CompilerParams(vmem_limit_bytes=52 << 20)


def shift(value, axis, step):
    return lax.ppermute(value, axis, [(i, (i + step) % N) for i in range(N)])


def behind(value, *others):
    return lax.optimization_barrier((value, *others))[0]


def slope_of(hidden, target):
    root = math.sqrt(2.0 / math.pi)
    square = hidden * hidden
    bend = jnp.tanh(hidden * (root + (root * 0.044715) * square))
    half = 0.5 + 0.5 * bend
    deriv = half + (hidden * (1.0 - bend * bend)) * (0.5 * root + (1.5 * root * 0.044715) * square)
    return ((hidden * half - target.astype(F32)) * deriv).astype(BF16)


def joined(x_ref):
    groups = [
        jnp.concatenate([x_ref[g, k] for k in range(x_ref.shape[1])], axis=1) for g in range(x_ref.shape[0])
    ]
    return groups[0] if len(groups) == 1 else jnp.concatenate(groups, axis=0)


def cost(rows, deep, cols, exps=0):
    return pl.CostEstimate(
        flops=2 * rows * deep * cols, bytes_accessed=2 * deep * (rows + cols) + 4 * rows * cols, transcendentals=exps
    )


def add_term(s, x, far_ref, total_ref):
    part = jnp.dot(s, x, preferred_element_type=F32)
    step = pl.program_id(0)

    @pl.when(step == 0)
    def _():
        total_ref[...] = part

    @pl.when(step > 0)
    def _():
        total_ref[...] += part

    @pl.when(step == pl.num_programs(0) - 1)
    def _():
        far_ref[...] = total_ref[...].astype(BF16)


def first_slopes(x, w, t, which):
    groups, blocks, tile, wide = x.shape
    rows = groups * tile
    cols, deep = w[0].shape
    per = deep // wide
    out = pl.BlockSpec((cols, tile), lambda i, which: (0, i))
    whole = pl.BlockSpec((cols, deep), lambda i, which: (0, 0), pipeline_mode=pl.Buffered(1))

    def kernel(which_ref, x_ref, *refs):
        w_refs, (t_ref, h_ref, s_ref, far_ref, total_ref) = refs[:N], refs[N:]
        block = lambda j: [x_ref[0, per * which_ref[j] + k] for k in range(per)]
        x = jnp.concatenate([part for j in range(N) for part in block(j)], axis=1)
        w = jnp.concatenate([w_ref[...] for w_ref in w_refs], axis=1)
        hidden = lax.dot_general(w, x, NT, preferred_element_type=F32)
        h_ref[...] = hidden
        s = slope_of(hidden, t_ref[0])
        s_ref[...] = s
        add_term(s, jnp.concatenate(block(2), axis=1), far_ref, total_ref)

    return pl.pallas_call(
        kernel,
        grid_spec=pltpu.PrefetchScalarGridSpec(
            num_scalar_prefetch=1,
            grid=(N,),
            in_specs=[pl.BlockSpec((1, blocks, tile, wide), lambda i, which: (i, 0, 0, 0))]
            + [whole] * N
            + [pl.BlockSpec((1, cols, tile), lambda i, which: (which[N + i], 0, 0))],
            out_specs=[out, out, pl.BlockSpec((cols, deep), lambda i, which: (0, 0))],
            scratch_shapes=[pltpu.VMEM((cols, deep), F32)],
        ),
        out_shape=[
            jax.ShapeDtypeStruct((cols, rows), F32),
            jax.ShapeDtypeStruct((cols, rows), BF16),
            jax.ShapeDtypeStruct((cols, deep), BF16),
        ],
        compiler_params=PARAMS,
        cost_estimate=cost(cols, (blocks + per) * wide, rows, rows * cols),
    )(jnp.stack(which).astype(jnp.int32), x, *w, t)


def moved(x, pieces, which):
    groups, blocks, tile, wide = x.shape
    rows = groups * tile
    cols, deep = pieces[0].shape
    per = deep // wide
    count = len(pieces)
    at = lambda j: pl.BlockSpec((1, per, tile, wide), lambda i, which: (i, which[j], 0, 0))

    def kernel(which_ref, *refs):
        xs, fs = refs[:count], refs[count : 2 * count]
        x = jnp.concatenate([x_ref[0, k] for x_ref in xs for k in range(per)], axis=1)
        f = jnp.concatenate([f_ref[...] for f_ref in fs], axis=1)
        refs[-1][...] = lax.dot_general(f, x, NT, preferred_element_type=F32)

    return pl.pallas_call(
        kernel,
        grid_spec=pltpu.PrefetchScalarGridSpec(
            num_scalar_prefetch=1,
            grid=(N,),
            in_specs=[at(j) for j in range(count)] + [pl.BlockSpec((cols, deep), lambda i, which: (0, 0))] * count,
            out_specs=pl.BlockSpec((cols, tile), lambda i, which: (0, i)),
        ),
        out_shape=jax.ShapeDtypeStruct((cols, rows), F32),
        compiler_params=PARAMS,
        cost_estimate=cost(cols, deep * count, rows),
    )(jnp.stack(which).astype(jnp.int32), *([x] * count), *pieces)


def second_slopes(x, piece, which, part, scale, hidden, t):
    groups, blocks, tile, wide = x.shape
    rows = groups * tile
    cols, deep = piece.shape
    per = deep // wide
    out = pl.BlockSpec((cols, tile), lambda i, which: (0, i))
    whole = pl.BlockSpec((cols, deep), lambda i, which: (0, 0))

    def kernel(which_ref, scale_ref, x_ref, f_ref, part_ref, h_ref, t_ref, s_ref, far_ref, total_ref):
        x = joined(x_ref)
        move = part_ref[...] + lax.dot_general(f_ref[...], x, NT, preferred_element_type=F32)
        s = slope_of(h_ref[...] + scale_ref[0, 0] * move, t_ref[0])
        s_ref[...] = s
        add_term(s, x, far_ref, total_ref)

    return pl.pallas_call(
        kernel,
        grid_spec=pltpu.PrefetchScalarGridSpec(
            num_scalar_prefetch=1,
            grid=(N,),
            in_specs=[
                pl.BlockSpec(memory_space=pltpu.SMEM),
                pl.BlockSpec((1, per, tile, wide), lambda i, which: (i, which[0], 0, 0)),
                whole,
                out,
                out,
                pl.BlockSpec((1, cols, tile), lambda i, which: (which[1 + i], 0, 0)),
            ],
            out_specs=[out, whole],
            scratch_shapes=[pltpu.VMEM((cols, deep), F32)],
        ),
        out_shape=[jax.ShapeDtypeStruct((cols, rows), BF16), jax.ShapeDtypeStruct((cols, deep), BF16)],
        compiler_params=PARAMS,
        cost_estimate=cost(cols, 2 * deep, rows, rows * cols),
    )(jnp.stack(which).astype(jnp.int32), scale, x, piece, part, hidden, t)


def terms(x, s, which, cut):
    groups, blocks, size, wide = x.shape
    rows = groups * size
    cols = s.shape[0]
    half = cols // 2
    tile = rows // 2
    per = blocks // N
    count = len(which)
    at = lambda j: pl.BlockSpec((groups // 2, per, size, wide), lambda i, which: (i, which[j], 0, 0))
    kinds = [F32, BF16, BF16, F32] if cut else [F32] * count
    tall = half if cut else cols

    def kernel(which_ref, *refs):
        s_ref = refs[count]
        outs, totals = refs[count + 1 : -count], refs[-count:]
        parts = [jnp.dot(s_ref[...], joined(refs[j]), preferred_element_type=F32) for j in range(count)]

        @pl.when(pl.program_id(0) == 0)
        def _():
            for j in range(count):
                totals[j][...] = parts[j]

        @pl.when(pl.program_id(0) > 0)
        def _():
            for j in range(count):
                total = totals[j][...] + parts[j]
                for n in range(cols // tall):
                    out = outs[j * (cols // tall) + n]
                    out[...] = total[n * tall : (n + 1) * tall].astype(out.dtype)

    return pl.pallas_call(
        kernel,
        grid_spec=pltpu.PrefetchScalarGridSpec(
            num_scalar_prefetch=1,
            grid=(rows // tile,),
            in_specs=[at(j) for j in range(count)] + [pl.BlockSpec((cols, tile), lambda i, which: (0, i))],
            out_specs=[pl.BlockSpec((tall, per * wide), lambda i, which: (0, 0))] * len(kinds),
            scratch_shapes=[pltpu.VMEM((cols, per * wide), F32)] * count,
        ),
        out_shape=[jax.ShapeDtypeStruct((tall, per * wide), kind) for kind in kinds],
        compiler_params=PARAMS,
        cost_estimate=cost(cols * count, rows, per * wide),
    )(jnp.stack(which).astype(jnp.int32), *([x] * count), s)


def ring_sum(x, s, far, me):
    at = lambda step: lax.rem(me + step, N)
    half = far.shape[0] // 2
    far_next, far_prev = shift(far[:half], "x", 1), shift(far[half:], "x", -1)
    high, to_next, to_prev, low = terms(x, s, [at(1), at(3)], True)
    next_low, prev_high = shift(to_next, "x", 1), shift(to_prev, "x", -1)
    next_high = shift((high + far_next.astype(F32)).astype(BF16), "x", 1)
    prev_low = shift((low + far_prev.astype(F32)).astype(BF16), "x", -1)
    (own,) = terms(x, s, [at(0)], False)
    high = own[:half] + next_high.astype(F32) + prev_high.astype(F32)
    low = own[half:] + next_low.astype(F32) + prev_low.astype(F32)
    return jnp.concatenate([high, low], axis=0)


def ring_gather(value, axis):
    return [value, shift(value, axis, -1), shift(value, axis, 2), shift(value, axis, 1)]


def ring_gather_halves(value, axis):
    half = value.shape[0] // 2
    after, before = shift(value, axis, -1), shift(value, axis, 1)
    far = jnp.concatenate([shift(before[:half], axis, 1), shift(after[half:], axis, -1)], axis=0)
    return [value, after, far, before]


def ring_swap(chunk, axis):
    return [chunk(0), shift(chunk(3), axis, -1), shift(chunk(2), axis, 2), shift(chunk(1), axis, 1)]


def cut_kernel(which_ref, own, after, far, before, to_next, to_prev, kept):
    rows = own.shape[0]
    half = rows // 2
    turned = far[...].T
    to_next[:, :rows], to_next[:, rows:] = after[...].T, turned[:, :half]
    to_prev[:, :rows], to_prev[:, rows:] = before[...].T, turned[:, half:]
    kept[...] = own[...].T


def cut(array, me):
    rows, cols = array.shape[0], array.shape[1] // N
    at = lambda k: pl.BlockSpec((rows, cols), lambda i, which: (0, which[k]))
    wide = [rows + rows // 2, rows + rows // 2, rows]
    return pl.pallas_call(
        cut_kernel,
        grid_spec=pltpu.PrefetchScalarGridSpec(
            num_scalar_prefetch=1,
            grid=(1,),
            in_specs=[at(k) for k in range(N)],
            out_specs=[pl.BlockSpec((cols, size), lambda i, which: (0, 0)) for size in wide],
        ),
        out_shape=[jax.ShapeDtypeStruct((cols, size), array.dtype) for size in wide],
        compiler_params=PARAMS,
        cost_estimate=cost(0, 0, 0),
    )(jnp.stack([lax.rem(me + k, N) for k in range(N)]).astype(jnp.int32), *([array] * N))


def ring_swap_halves(to_next, to_prev, kept, axis):
    size = kept.shape[1]
    prev, after = shift(to_next, axis, 1), shift(to_prev, axis, -1)
    high, low = shift(prev[:, size:], axis, 1), shift(after[:, size:], axis, -1)
    return [kept, after[:, :size], jnp.concatenate([high, low], axis=1), prev[:, :size]]


def in_order(pieces, me):
    twice = jnp.stack(pieces + pieces)
    return lax.dynamic_slice_in_dim(twice, lax.rem(N - me, N), N, axis=0)


def part_of(value):
    part = jnp.full((N * N * N, 128), jnp.sum(value * value), F32)
    return part + lax.ppermute(part, "c", [(0, 1), (1, 0)])


def spread(part):
    return lax.all_to_all(part, ("x", "y", "z"), split_axis=0, concat_axis=0, tiled=True)


def per_device(tokens, target, weight):
    ix, iy = lax.axis_index("x"), lax.axis_index("y")
    rows, wide = tokens.shape
    cols = weight.shape[1] // N
    width = wide * 2 * N
    hidden_all = weight.shape[1] * 2 * N

    x = lax.all_gather(tokens, ("y", "z", "c"), axis=0, tiled=True).reshape(N, 2 * N, rows, wide)

    def columns(array):
        return lambda k: lax.dynamic_slice_in_dim(array, lax.rem(iy + k, N) * cols, cols, axis=1)

    to_next, to_prev, kept = cut(target, iy)
    w_pieces = ring_swap(columns(weight), "y")
    to_next, to_prev = lax.optimization_barrier((to_next, to_prev, *w_pieces))[:2]
    t = jnp.stack(ring_swap_halves(to_next, to_prev, kept, "y"))
    tiles = [lax.rem(k + N - iy, N) for k in range(N)]
    w = ring_gather(in_order(w_pieces, iy).reshape(-1, cols).T, "x")

    at = lambda k: lax.rem(ix + k, N)
    hidden, slope, term = first_slopes(x, w, t, [at(k) for k in range(N)] + tiles)
    first = ring_sum(x, slope, term, ix)
    own, after, far, before = ring_gather_halves(first.astype(BF16), "x")
    part = moved(x, [own, after, before], [at(0), at(1), at(3)])
    each, part = lax.optimization_barrier((spread(part_of(first)), part))
    scale = 0.5 * math.sqrt(hidden_all) / jnp.sqrt(jnp.sum(each[:, 0]) + 1e-06)
    slope, term = second_slopes(x, far, [at(2)] + tiles, part, scale.reshape(1, 1), hidden, t)
    second = ring_sum(x, slope, term, ix)
    share, second = lax.optimization_barrier((part_of(second), second.astype(BF16)))
    total = jnp.sum(spread(share)[:, 0])
    factor = jnp.minimum(1.0, math.sqrt(width * hidden_all) / jnp.sqrt(total + 1e-06))
    held = second.T.reshape(N, -1, cols)
    parts = in_order(ring_swap(lambda k: lax.dynamic_index_in_dim(held, lax.rem(iy + k, N), 0, keepdims=False), "y"), iy)
    whole = jnp.concatenate([parts[k] for k in range(N)], axis=1)
    return whole.astype(F32) * factor


def solution(mesh):
    grid = Mesh(mesh.devices.reshape(N, N, N, 2), ("x", "y", "z", "c"))
    spec = P(("x", "y"), ("z", "c"))
    return jax.shard_map(
        per_device, mesh=grid, in_specs=(spec, spec, spec), out_specs=spec, check_vma=False
    )
```

```python
import math

import jax
import jax.numpy as jnp
from jax import lax
from jax.experimental import pallas as pl
from jax.experimental.pallas import tpu as pltpu
from jax.sharding import Mesh, PartitionSpec as P

BF16, F32 = jnp.bfloat16, jnp.float32
N = 4
NT = (((1,), (1,)), ((), ()))
PARAMS = pltpu.CompilerParams(vmem_limit_bytes=52 << 20)


def shift(value, axis, step):
    return lax.ppermute(value, axis, [(i, (i + step) % N) for i in range(N)])


def behind(value, *others):
    return lax.optimization_barrier((value, *others))[0]


def slope_of(hidden, target):
    root = math.sqrt(2.0 / math.pi)
    square = hidden * hidden
    bend = jnp.tanh(hidden * (root + (root * 0.044715) * square))
    half = 0.5 + 0.5 * bend
    deriv = half + (hidden * (1.0 - bend * bend)) * (0.5 * root + (1.5 * root * 0.044715) * square)
    return ((hidden * half - target.astype(F32)) * deriv).astype(BF16)


def joined(x_ref):
    groups = [
        jnp.concatenate([x_ref[g, k] for k in range(x_ref.shape[1])], axis=1) for g in range(x_ref.shape[0])
    ]
    return groups[0] if len(groups) == 1 else jnp.concatenate(groups, axis=0)


def cost(rows, deep, cols, exps=0):
    return pl.CostEstimate(
        flops=2 * rows * deep * cols, bytes_accessed=2 * deep * (rows + cols) + 4 * rows * cols, transcendentals=exps
    )


def add_term(s, x, far_ref, total_ref):
    part = jnp.dot(s, x, preferred_element_type=F32)
    step = pl.program_id(0)

    @pl.when(step == 0)
    def _():
        total_ref[...] = part

    @pl.when(step > 0)
    def _():
        total_ref[...] += part

    @pl.when(step == pl.num_programs(0) - 1)
    def _():
        far_ref[...] = total_ref[...].astype(BF16)


def first_slopes(x, w, t, which):
    groups, blocks, tile, wide = x.shape
    rows = groups * tile
    cols, deep = w[0].shape
    per = deep // wide
    out = pl.BlockSpec((cols, tile), lambda i, which: (0, i))
    whole = pl.BlockSpec((cols, deep), lambda i, which: (0, 0), pipeline_mode=pl.Buffered(1))

    def kernel(which_ref, x_ref, *refs):
        w_refs, (t_ref, h_ref, s_ref, far_ref, total_ref) = refs[:N], refs[N:]
        block = lambda j: [x_ref[0, per * which_ref[j] + k] for k in range(per)]
        x = jnp.concatenate([part for j in range(N) for part in block(j)], axis=1)
        w = jnp.concatenate([w_ref[...] for w_ref in w_refs], axis=1)
        hidden = lax.dot_general(w, x, NT, preferred_element_type=F32)
        h_ref[...] = hidden
        s = slope_of(hidden, t_ref[0])
        s_ref[...] = s
        add_term(s, jnp.concatenate(block(2), axis=1), far_ref, total_ref)

    return pl.pallas_call(
        kernel,
        grid_spec=pltpu.PrefetchScalarGridSpec(
            num_scalar_prefetch=1,
            grid=(N,),
            in_specs=[pl.BlockSpec((1, blocks, tile, wide), lambda i, which: (i, 0, 0, 0))]
            + [whole] * N
            + [pl.BlockSpec((1, cols, tile), lambda i, which: (which[N + i], 0, 0))],
            out_specs=[out, out, pl.BlockSpec((cols, deep), lambda i, which: (0, 0))],
            scratch_shapes=[pltpu.VMEM((cols, deep), F32)],
        ),
        out_shape=[
            jax.ShapeDtypeStruct((cols, rows), F32),
            jax.ShapeDtypeStruct((cols, rows), BF16),
            jax.ShapeDtypeStruct((cols, deep), BF16),
        ],
        compiler_params=PARAMS,
        cost_estimate=cost(cols, (blocks + per) * wide, rows, rows * cols),
    )(jnp.stack(which).astype(jnp.int32), x, *w, t)


def moved(x, pieces, which):
    groups, blocks, tile, wide = x.shape
    rows = groups * tile
    cols, deep = pieces[0].shape
    per = deep // wide
    count = len(pieces)
    at = lambda j: pl.BlockSpec((1, per, tile, wide), lambda i, which: (i, which[j], 0, 0))

    def kernel(which_ref, *refs):
        xs, fs = refs[:count], refs[count : 2 * count]
        x = jnp.concatenate([x_ref[0, k] for x_ref in xs for k in range(per)], axis=1)
        f = jnp.concatenate([f_ref[...] for f_ref in fs], axis=1)
        refs[-1][...] = lax.dot_general(f, x, NT, preferred_element_type=F32)

    return pl.pallas_call(
        kernel,
        grid_spec=pltpu.PrefetchScalarGridSpec(
            num_scalar_prefetch=1,
            grid=(N,),
            in_specs=[at(j) for j in range(count)] + [pl.BlockSpec((cols, deep), lambda i, which: (0, 0))] * count,
            out_specs=pl.BlockSpec((cols, tile), lambda i, which: (0, i)),
        ),
        out_shape=jax.ShapeDtypeStruct((cols, rows), F32),
        compiler_params=PARAMS,
        cost_estimate=cost(cols, deep * count, rows),
    )(jnp.stack(which).astype(jnp.int32), *([x] * count), *pieces)


def second_slopes(x, piece, which, part, scale, hidden, t):
    groups, blocks, tile, wide = x.shape
    rows = groups * tile
    cols, deep = piece.shape
    per = deep // wide
    out = pl.BlockSpec((cols, tile), lambda i, which: (0, i))
    whole = pl.BlockSpec((cols, deep), lambda i, which: (0, 0))

    def kernel(which_ref, scale_ref, x_ref, f_ref, part_ref, h_ref, t_ref, s_ref, far_ref, total_ref):
        x = joined(x_ref)
        move = part_ref[...] + lax.dot_general(f_ref[...], x, NT, preferred_element_type=F32)
        s = slope_of(h_ref[...] + scale_ref[0, 0] * move, t_ref[0])
        s_ref[...] = s
        add_term(s, x, far_ref, total_ref)

    return pl.pallas_call(
        kernel,
        grid_spec=pltpu.PrefetchScalarGridSpec(
            num_scalar_prefetch=1,
            grid=(N,),
            in_specs=[
                pl.BlockSpec(memory_space=pltpu.SMEM),
                pl.BlockSpec((1, per, tile, wide), lambda i, which: (i, which[0], 0, 0)),
                whole,
                out,
                out,
                pl.BlockSpec((1, cols, tile), lambda i, which: (which[1 + i], 0, 0)),
            ],
            out_specs=[out, whole],
            scratch_shapes=[pltpu.VMEM((cols, deep), F32)],
        ),
        out_shape=[jax.ShapeDtypeStruct((cols, rows), BF16), jax.ShapeDtypeStruct((cols, deep), BF16)],
        compiler_params=PARAMS,
        cost_estimate=cost(cols, 2 * deep, rows, rows * cols),
    )(jnp.stack(which).astype(jnp.int32), scale, x, piece, part, hidden, t)


def terms(x, s, which, cut):
    groups, blocks, size, wide = x.shape
    rows = groups * size
    cols = s.shape[0]
    half = cols // 2
    tile = rows // 2
    per = blocks // N
    count = len(which)
    at = lambda j: pl.BlockSpec((groups // 2, per, size, wide), lambda i, which: (i, which[j], 0, 0))
    kinds = [F32, BF16, BF16, F32] if cut else [F32] * count
    tall = half if cut else cols

    def kernel(which_ref, *refs):
        s_ref = refs[count]
        outs, totals = refs[count + 1 : -count], refs[-count:]
        parts = [jnp.dot(s_ref[...], joined(refs[j]), preferred_element_type=F32) for j in range(count)]

        @pl.when(pl.program_id(0) == 0)
        def _():
            for j in range(count):
                totals[j][...] = parts[j]

        @pl.when(pl.program_id(0) > 0)
        def _():
            for j in range(count):
                total = totals[j][...] + parts[j]
                for n in range(cols // tall):
                    out = outs[j * (cols // tall) + n]
                    out[...] = total[n * tall : (n + 1) * tall].astype(out.dtype)

    return pl.pallas_call(
        kernel,
        grid_spec=pltpu.PrefetchScalarGridSpec(
            num_scalar_prefetch=1,
            grid=(rows // tile,),
            in_specs=[at(j) for j in range(count)] + [pl.BlockSpec((cols, tile), lambda i, which: (0, i))],
            out_specs=[pl.BlockSpec((tall, per * wide), lambda i, which: (0, 0))] * len(kinds),
            scratch_shapes=[pltpu.VMEM((cols, per * wide), F32)] * count,
        ),
        out_shape=[jax.ShapeDtypeStruct((tall, per * wide), kind) for kind in kinds],
        compiler_params=PARAMS,
        cost_estimate=cost(cols * count, rows, per * wide),
    )(jnp.stack(which).astype(jnp.int32), *([x] * count), s)


def ring_sum(x, s, far, me):
    at = lambda step: lax.rem(me + step, N)
    half = far.shape[0] // 2
    far_next, far_prev = shift(far[:half], "x", 1), shift(far[half:], "x", -1)
    high, to_next, to_prev, low = terms(x, s, [at(1), at(3)], True)
    next_low, prev_high = shift(to_next, "x", 1), shift(to_prev, "x", -1)
    next_high = shift((high + far_next.astype(F32)).astype(BF16), "x", 1)
    prev_low = shift((low + far_prev.astype(F32)).astype(BF16), "x", -1)
    (own,) = terms(x, s, [at(0)], False)
    high = own[:half] + next_high.astype(F32) + prev_high.astype(F32)
    low = own[half:] + next_low.astype(F32) + prev_low.astype(F32)
    return jnp.concatenate([high, low], axis=0)


def ring_gather(value, axis):
    return [value, shift(value, axis, -1), shift(value, axis, 2), shift(value, axis, 1)]


def ring_gather_halves(value, axis):
    half = value.shape[0] // 2
    after, before = shift(value, axis, -1), shift(value, axis, 1)
    far = jnp.concatenate([shift(before[:half], axis, 1), shift(after[half:], axis, -1)], axis=0)
    return [value, after, far, before]


def ring_swap(chunk, axis):
    return [chunk(0), shift(chunk(3), axis, -1), shift(chunk(2), axis, 2), shift(chunk(1), axis, 1)]


def cut_kernel(which_ref, own, after, far, before, to_next, to_prev, kept):
    rows = own.shape[0]
    half = rows // 2
    turned = far[...].T
    to_next[:, :rows], to_next[:, rows:] = after[...].T, turned[:, :half]
    to_prev[:, :rows], to_prev[:, rows:] = before[...].T, turned[:, half:]
    kept[...] = own[...].T


def cut(array, me):
    rows, cols = array.shape[0], array.shape[1] // N
    at = lambda k: pl.BlockSpec((rows, cols), lambda i, which: (0, which[k]))
    wide = [rows + rows // 2, rows + rows // 2, rows]
    return pl.pallas_call(
        cut_kernel,
        grid_spec=pltpu.PrefetchScalarGridSpec(
            num_scalar_prefetch=1,
            grid=(1,),
            in_specs=[at(k) for k in range(N)],
            out_specs=[pl.BlockSpec((cols, size), lambda i, which: (0, 0)) for size in wide],
        ),
        out_shape=[jax.ShapeDtypeStruct((cols, size), array.dtype) for size in wide],
        compiler_params=PARAMS,
        cost_estimate=cost(0, 0, 0),
    )(jnp.stack([lax.rem(me + k, N) for k in range(N)]).astype(jnp.int32), *([array] * N))


def ring_swap_halves(to_next, to_prev, kept, axis):
    size = kept.shape[1]
    prev, after = shift(to_next, axis, 1), shift(to_prev, axis, -1)
    sent_on = prev[:, size:], after[:, size:]
    high, low = shift(sent_on[0], axis, 1), shift(sent_on[1], axis, -1)
    return [kept, after[:, :size], jnp.concatenate([high, low], axis=1), prev[:, :size]], sent_on


def in_order(pieces, me):
    twice = jnp.stack(pieces + pieces)
    return lax.dynamic_slice_in_dim(twice, lax.rem(N - me, N), N, axis=0)


def part_of(value):
    part = jnp.full((N * N * N, 128), jnp.sum(value * value), F32)
    return part + lax.ppermute(part, "c", [(0, 1), (1, 0)])


def spread(part):
    return lax.all_to_all(part, ("x", "y", "z"), split_axis=0, concat_axis=0, tiled=True)


def per_device(tokens, target, weight):
    ix, iy = lax.axis_index("x"), lax.axis_index("y")
    rows, wide = tokens.shape
    cols = weight.shape[1] // N
    width = wide * 2 * N
    hidden_all = weight.shape[1] * 2 * N

    x = lax.all_gather(tokens, ("y", "z", "c"), axis=0, tiled=True).reshape(N, 2 * N, rows, wide)

    def columns(array):
        return lambda k: lax.dynamic_slice_in_dim(array, lax.rem(iy + k, N) * cols, cols, axis=1)

    to_next, to_prev, kept = cut(target, iy)
    t_pieces, sent_on = ring_swap_halves(to_next, to_prev, kept, "y")
    t = jnp.stack(t_pieces)
    w_pieces = ring_swap(columns(behind(weight, *sent_on)), "y")
    tiles = [lax.rem(k + N - iy, N) for k in range(N)]
    w = ring_gather(in_order(w_pieces, iy).reshape(-1, cols).T, "x")

    at = lambda k: lax.rem(ix + k, N)
    hidden, slope, term = first_slopes(x, w, t, [at(k) for k in range(N)] + tiles)
    first = ring_sum(x, slope, term, ix)
    own, after, far, before = ring_gather_halves(first.astype(BF16), "x")
    part = moved(x, [own, after, before], [at(0), at(1), at(3)])
    each, part = lax.optimization_barrier((spread(part_of(first)), part))
    scale = 0.5 * math.sqrt(hidden_all) / jnp.sqrt(jnp.sum(each[:, 0]) + 1e-06)
    slope, term = second_slopes(x, far, [at(2)] + tiles, part, scale.reshape(1, 1), hidden, t)
    second = ring_sum(x, slope, term, ix)
    share, second = lax.optimization_barrier((part_of(second), second.astype(BF16)))
    total = jnp.sum(spread(share)[:, 0])
    factor = jnp.minimum(1.0, math.sqrt(width * hidden_all) / jnp.sqrt(total + 1e-06))
    held = second.T.reshape(N, -1, cols)
    parts = in_order(ring_swap(lambda k: lax.dynamic_index_in_dim(held, lax.rem(iy + k, N), 0, keepdims=False), "y"), iy)
    whole = jnp.concatenate([parts[k] for k in range(N)], axis=1)
    return whole.astype(F32) * factor


def solution(mesh):
    grid = Mesh(mesh.devices.reshape(N, N, N, 2), ("x", "y", "z", "c"))
    spec = P(("x", "y"), ("z", "c"))
    return jax.shard_map(
        per_device, mesh=grid, in_specs=(spec, spec, spec), out_specs=spec, check_vma=False
    )
```

```python
import math

import jax
import jax.numpy as jnp
from jax import lax
from jax.experimental import pallas as pl
from jax.experimental.pallas import tpu as pltpu
from jax.sharding import Mesh, PartitionSpec as P

BF16, F32 = jnp.bfloat16, jnp.float32
N = 4
NT = (((1,), (1,)), ((), ()))
PARAMS = pltpu.CompilerParams(vmem_limit_bytes=46 << 20)


def shift(value, axis, step):
    return lax.ppermute(value, axis, [(i, (i + step) % N) for i in range(N)])


def behind(value, *others):
    return lax.optimization_barrier((value, *others))[0]


def slope_of(hidden, target):
    root = math.sqrt(2.0 / math.pi)
    square = hidden * hidden
    bend = jnp.tanh(hidden * (root + (root * 0.044715) * square))
    half = 0.5 + 0.5 * bend
    deriv = half + (hidden * (1.0 - bend * bend)) * (0.5 * root + (1.5 * root * 0.044715) * square)
    return ((hidden * half - target.astype(F32)) * deriv).astype(BF16)


def joined(x_ref):
    return jnp.concatenate([x_ref[k] for k in range(x_ref.shape[0])], axis=1)


def cost(rows, deep, cols, exps=0):
    return pl.CostEstimate(
        flops=2 * rows * deep * cols, bytes_accessed=2 * deep * (rows + cols) + 4 * rows * cols, transcendentals=exps
    )


def add_term(s, x, far_ref, total_ref):
    part = jnp.dot(s, x, preferred_element_type=F32)
    step = pl.program_id(0)

    @pl.when(step == 0)
    def _():
        total_ref[...] = part

    @pl.when(step > 0)
    def _():
        total_ref[...] += part

    @pl.when(step == pl.num_programs(0) - 1)
    def _():
        far_ref[...] = total_ref[...].astype(BF16)


def first_slopes(x, w, t, which):
    blocks, rows, wide = x.shape
    cols, deep = w[0].shape
    tile = rows // N
    per = deep // wide
    out = pl.BlockSpec((cols, tile), lambda i, which: (0, i))
    whole = pl.BlockSpec((cols, deep), lambda i, which: (0, 0), pipeline_mode=pl.Buffered(1))

    def kernel(which_ref, x_ref, *refs):
        w_refs, (t_ref, h_ref, s_ref, far_ref, total_ref) = refs[:N], refs[N:]
        block = lambda j: [x_ref[per * which_ref[j] + k] for k in range(per)]
        x = jnp.concatenate([part for j in range(N) for part in block(j)], axis=1)
        w = jnp.concatenate([w_ref[...] for w_ref in w_refs], axis=1)
        hidden = lax.dot_general(w, x, NT, preferred_element_type=F32)
        h_ref[...] = hidden
        s = slope_of(hidden, t_ref[...])
        s_ref[...] = s
        add_term(s, jnp.concatenate(block(2), axis=1), far_ref, total_ref)

    return pl.pallas_call(
        kernel,
        grid_spec=pltpu.PrefetchScalarGridSpec(
            num_scalar_prefetch=1,
            grid=(N,),
            in_specs=[pl.BlockSpec((blocks, tile, wide), lambda i, which: (0, i, 0))] + [whole] * N + [out],
            out_specs=[out, out, pl.BlockSpec((cols, deep), lambda i, which: (0, 0))],
            scratch_shapes=[pltpu.VMEM((cols, deep), F32)],
        ),
        out_shape=[
            jax.ShapeDtypeStruct((cols, rows), F32),
            jax.ShapeDtypeStruct((cols, rows), BF16),
            jax.ShapeDtypeStruct((cols, deep), BF16),
        ],
        compiler_params=PARAMS,
        cost_estimate=cost(cols, (blocks + per) * wide, rows, rows * cols),
    )(jnp.stack(which).astype(jnp.int32), x, *w, t)


def moved(x, pieces, which):
    blocks, rows, wide = x.shape
    cols, deep = pieces[0].shape
    per = deep // wide
    tile = rows // N
    count = len(pieces)
    at = lambda j: pl.BlockSpec((per, tile, wide), lambda i, which: (which[j], i, 0))

    def kernel(which_ref, *refs):
        xs, fs = refs[:count], refs[count : 2 * count]
        x = jnp.concatenate([x_ref[k] for x_ref in xs for k in range(per)], axis=1)
        f = jnp.concatenate([f_ref[...] for f_ref in fs], axis=1)
        refs[-1][...] = lax.dot_general(f, x, NT, preferred_element_type=F32)

    return pl.pallas_call(
        kernel,
        grid_spec=pltpu.PrefetchScalarGridSpec(
            num_scalar_prefetch=1,
            grid=(N,),
            in_specs=[at(j) for j in range(count)] + [pl.BlockSpec((cols, deep), lambda i, which: (0, 0))] * count,
            out_specs=pl.BlockSpec((cols, tile), lambda i, which: (0, i)),
        ),
        out_shape=jax.ShapeDtypeStruct((cols, rows), F32),
        compiler_params=PARAMS,
        cost_estimate=cost(cols, deep * count, rows),
    )(jnp.stack(which).astype(jnp.int32), *([x] * count), *pieces)


def second_slopes(x, piece, block, part, scale, hidden, t):
    blocks, rows, wide = x.shape
    cols, deep = piece.shape
    per = deep // wide
    tile = rows // N
    out = pl.BlockSpec((cols, tile), lambda i, which: (0, i))
    whole = pl.BlockSpec((cols, deep), lambda i, which: (0, 0))

    def kernel(which_ref, scale_ref, x_ref, f_ref, part_ref, h_ref, t_ref, s_ref, far_ref, total_ref):
        x = joined(x_ref)
        move = part_ref[...] + lax.dot_general(f_ref[...], x, NT, preferred_element_type=F32)
        s = slope_of(h_ref[...] + scale_ref[0, 0] * move, t_ref[...])
        s_ref[...] = s
        add_term(s, x, far_ref, total_ref)

    return pl.pallas_call(
        kernel,
        grid_spec=pltpu.PrefetchScalarGridSpec(
            num_scalar_prefetch=1,
            grid=(N,),
            in_specs=[
                pl.BlockSpec(memory_space=pltpu.SMEM),
                pl.BlockSpec((per, tile, wide), lambda i, which: (which[0], i, 0)),
                whole,
                out,
                out,
                out,
            ],
            out_specs=[out, whole],
            scratch_shapes=[pltpu.VMEM((cols, deep), F32)],
        ),
        out_shape=[jax.ShapeDtypeStruct((cols, rows), BF16), jax.ShapeDtypeStruct((cols, deep), BF16)],
        compiler_params=PARAMS,
        cost_estimate=cost(cols, 2 * deep, rows, rows * cols),
    )(jnp.reshape(block, (1,)).astype(jnp.int32), scale, x, piece, part, hidden, t)


def terms(x, s, which, cut):
    blocks, rows, wide = x.shape
    cols = s.shape[0]
    half = cols // 2
    tile = rows // 2
    per = blocks // N
    count = len(which)
    at = lambda j: pl.BlockSpec((per, tile, wide), lambda i, which: (which[j], i, 0))
    kinds = [F32, BF16, BF16, F32] if cut else [F32] * count
    tall = half if cut else cols

    def kernel(which_ref, *refs):
        s_ref = refs[count]
        outs, totals = refs[count + 1 : -count], refs[-count:]
        parts = [jnp.dot(s_ref[...], joined(refs[j]), preferred_element_type=F32) for j in range(count)]

        @pl.when(pl.program_id(0) == 0)
        def _():
            for j in range(count):
                totals[j][...] = parts[j]

        @pl.when(pl.program_id(0) > 0)
        def _():
            for j in range(count):
                total = totals[j][...] + parts[j]
                for n in range(cols // tall):
                    out = outs[j * (cols // tall) + n]
                    out[...] = total[n * tall : (n + 1) * tall].astype(out.dtype)

    return pl.pallas_call(
        kernel,
        grid_spec=pltpu.PrefetchScalarGridSpec(
            num_scalar_prefetch=1,
            grid=(rows // tile,),
            in_specs=[at(j) for j in range(count)] + [pl.BlockSpec((cols, tile), lambda i, which: (0, i))],
            out_specs=[pl.BlockSpec((tall, per * wide), lambda i, which: (0, 0))] * len(kinds),
            scratch_shapes=[pltpu.VMEM((cols, per * wide), F32)] * count,
        ),
        out_shape=[jax.ShapeDtypeStruct((tall, per * wide), kind) for kind in kinds],
        compiler_params=PARAMS,
        cost_estimate=cost(cols * count, rows, per * wide),
    )(jnp.stack(which).astype(jnp.int32), *([x] * count), s)


def ring_sum(x, s, far, me):
    at = lambda step: lax.rem(me + step, N)
    half = far.shape[0] // 2
    far_next, far_prev = shift(far[:half], "x", 1), shift(far[half:], "x", -1)
    high, to_next, to_prev, low = terms(x, s, [at(1), at(3)], True)
    next_low, prev_high = shift(to_next, "x", 1), shift(to_prev, "x", -1)
    next_high = shift((high + far_next.astype(F32)).astype(BF16), "x", 1)
    prev_low = shift((low + far_prev.astype(F32)).astype(BF16), "x", -1)
    (own,) = terms(x, s, [at(0)], False)
    high = own[:half] + next_high.astype(F32) + prev_high.astype(F32)
    low = own[half:] + next_low.astype(F32) + prev_low.astype(F32)
    return jnp.concatenate([high, low], axis=0)


def ring_gather(value, axis):
    return [value, shift(value, axis, -1), shift(value, axis, 2), shift(value, axis, 1)]


def ring_gather_halves(value, axis):
    half = value.shape[0] // 2
    after, before = shift(value, axis, -1), shift(value, axis, 1)
    far = jnp.concatenate([shift(before[:half], axis, 1), shift(after[half:], axis, -1)], axis=0)
    return [value, after, far, before]


def ring_swap(chunk, axis):
    return [chunk(0), shift(chunk(3), axis, -1), shift(chunk(2), axis, 2), shift(chunk(1), axis, 1)]


def cut_kernel(which_ref, own, after, far, before, to_next, to_prev, kept):
    rows = own.shape[0]
    half = rows // 2
    to_next[:rows], to_next[rows:] = after[...], far[:half]
    to_prev[:rows], to_prev[rows:] = before[...], far[half:]
    kept[...] = own[...]


def cut(array, me):
    rows, cols = array.shape[0], array.shape[1] // N
    at = lambda k: pl.BlockSpec((rows, cols), lambda i, which: (0, which[k]))
    tall = [rows + rows // 2, rows + rows // 2, rows]
    return pl.pallas_call(
        cut_kernel,
        grid_spec=pltpu.PrefetchScalarGridSpec(
            num_scalar_prefetch=1,
            grid=(1,),
            in_specs=[at(k) for k in range(N)],
            out_specs=[pl.BlockSpec((size, cols), lambda i, which: (0, 0)) for size in tall],
        ),
        out_shape=[jax.ShapeDtypeStruct((size, cols), array.dtype) for size in tall],
        compiler_params=PARAMS,
        cost_estimate=cost(0, 0, 0),
    )(jnp.stack([lax.rem(me + k, N) for k in range(N)]).astype(jnp.int32), *([array] * N))


def ring_swap_halves(to_next, to_prev, kept, axis):
    rows = kept.shape[0]
    prev, after = shift(to_next, axis, 1), shift(to_prev, axis, -1)
    high, low = shift(prev[rows:], axis, 1), shift(after[rows:], axis, -1)
    return [kept, after[:rows], jnp.concatenate([high, low], axis=0), prev[:rows]]


def in_order(pieces, me):
    twice = jnp.stack(pieces + pieces)
    return lax.dynamic_slice_in_dim(twice, lax.rem(N - me, N), N, axis=0)


def total_of(value, beside):
    total = jnp.full((N * N * N, 128), jnp.sum(value * value), F32)
    total = total + lax.ppermute(total, "c", [(0, 1), (1, 0)])
    each = lax.all_to_all(total, ("x", "y", "z"), split_axis=0, concat_axis=0, tiled=True)
    if beside is not None:
        each, beside = lax.optimization_barrier((each, beside))
    return jnp.sum(each[:, 0]), beside


def per_device(tokens, target, weight):
    ix, iy = lax.axis_index("x"), lax.axis_index("y")
    rows, wide = tokens.shape
    cols = weight.shape[1] // N
    width = wide * 2 * N
    hidden_all = weight.shape[1] * 2 * N

    x = lax.all_gather(tokens, ("z", "c", "y"), axis=0, tiled=True).reshape(2 * N, N * rows, wide)

    def columns(array):
        return lambda k: lax.dynamic_slice_in_dim(array, lax.rem(iy + k, N) * cols, cols, axis=1)

    to_next, to_prev, kept = cut(target, iy)
    w_pieces = ring_swap(columns(weight), "y")
    to_next, to_prev = lax.optimization_barrier((to_next, to_prev, *w_pieces))[:2]
    t = in_order(ring_swap_halves(to_next, to_prev, kept, "y"), iy)
    t = jnp.concatenate([t[k].T for k in range(N)], axis=1)
    w = ring_gather(in_order(w_pieces, iy).reshape(-1, cols).T, "x")

    at = lambda k: lax.rem(ix + k, N)
    hidden, slope, term = first_slopes(x, w, t, [at(k) for k in range(N)])
    first = ring_sum(x, slope, term, ix)
    own, after, far, before = ring_gather_halves(first.astype(BF16), "x")
    part = moved(x, [own, after, before], [at(0), at(1), at(3)])
    total, part = total_of(first, part)
    scale = 0.5 * math.sqrt(hidden_all) / jnp.sqrt(total + 1e-06)
    slope, term = second_slopes(x, far, at(2), part, scale.reshape(1, 1), hidden, t)
    second = ring_sum(x, slope, term, ix)
    total, _ = total_of(second, None)
    factor = jnp.minimum(1.0, math.sqrt(width * hidden_all) / jnp.sqrt(total + 1e-06))
    held = second.astype(BF16).T.reshape(N, -1, cols)
    parts = in_order(ring_swap(lambda k: lax.dynamic_index_in_dim(held, lax.rem(iy + k, N), 0, keepdims=False), "y"), iy)
    whole = jnp.concatenate([parts[k] for k in range(N)], axis=1)
    return whole.astype(F32) * factor


def solution(mesh):
    grid = Mesh(mesh.devices.reshape(N, N, N, 2), ("x", "y", "z", "c"))
    spec = P(("x", "y"), ("z", "c"))
    return jax.shard_map(
        per_device, mesh=grid, in_specs=(spec, spec, spec), out_specs=spec, check_vma=False
    )
```

```python
import math

import jax
import jax.numpy as jnp
from jax import lax
from jax.experimental import pallas as pl
from jax.experimental.pallas import tpu as pltpu
from jax.sharding import Mesh, PartitionSpec as P

BF16, F32 = jnp.bfloat16, jnp.float32
N = 4
NT = (((1,), (1,)), ((), ()))
WIDE = pltpu.CompilerParams(vmem_limit_bytes=52 << 20)
PARAMS = pltpu.CompilerParams(vmem_limit_bytes=46 << 20)


def shift(value, axis, step):
    return lax.ppermute(value, axis, [(i, (i + step) % N) for i in range(N)])


def behind(value, *others):
    return lax.optimization_barrier((value, *others))[0]


def slope_of(hidden, target):
    root = math.sqrt(2.0 / math.pi)
    square = hidden * hidden
    bend = jnp.tanh(hidden * (root + (root * 0.044715) * square))
    half = 0.5 + 0.5 * bend
    deriv = half + (hidden * (1.0 - bend * bend)) * (0.5 * root + (1.5 * root * 0.044715) * square)
    return ((hidden * half - target.astype(F32)) * deriv).astype(BF16)


def joined(x_ref):
    return jnp.concatenate([x_ref[k] for k in range(x_ref.shape[0])], axis=1)


def cost(rows, deep, cols, exps=0):
    return pl.CostEstimate(
        flops=2 * rows * deep * cols, bytes_accessed=2 * deep * (rows + cols) + 4 * rows * cols, transcendentals=exps
    )


def add_term(s, x, far_ref, total_ref):
    part = jnp.dot(s, x, preferred_element_type=F32)
    step = pl.program_id(0)

    @pl.when(step == 0)
    def _():
        total_ref[...] = part

    @pl.when(step > 0)
    def _():
        total_ref[...] += part

    @pl.when(step == pl.num_programs(0) - 1)
    def _():
        far_ref[...] = total_ref[...].astype(BF16)


def first_slopes(x, w, t, which):
    blocks, rows, wide = x.shape
    cols, deep = w[0].shape
    tile = rows // N
    per = deep // wide
    out = pl.BlockSpec((cols, tile), lambda i, which: (0, i))
    whole = pl.BlockSpec((cols, deep), lambda i, which: (0, 0), pipeline_mode=pl.Buffered(1))

    def kernel(which_ref, x_ref, *refs):
        w_refs, (t_ref, h_ref, s_ref, far_ref, total_ref) = refs[:N], refs[N:]
        block = lambda j: [x_ref[per * which_ref[j] + k] for k in range(per)]
        x = jnp.concatenate([part for j in range(N) for part in block(j)], axis=1)
        w = jnp.concatenate([w_ref[...] for w_ref in w_refs], axis=1)
        hidden = lax.dot_general(w, x, NT, preferred_element_type=F32)
        h_ref[...] = hidden
        s = slope_of(hidden, t_ref[...])
        s_ref[...] = s
        add_term(s, jnp.concatenate(block(2), axis=1), far_ref, total_ref)

    return pl.pallas_call(
        kernel,
        grid_spec=pltpu.PrefetchScalarGridSpec(
            num_scalar_prefetch=1,
            grid=(N,),
            in_specs=[pl.BlockSpec((blocks, tile, wide), lambda i, which: (0, i, 0))] + [whole] * N + [out],
            out_specs=[out, out, pl.BlockSpec((cols, deep), lambda i, which: (0, 0))],
            scratch_shapes=[pltpu.VMEM((cols, deep), F32)],
        ),
        out_shape=[
            jax.ShapeDtypeStruct((cols, rows), F32),
            jax.ShapeDtypeStruct((cols, rows), BF16),
            jax.ShapeDtypeStruct((cols, deep), BF16),
        ],
        compiler_params=WIDE,
        cost_estimate=cost(cols, (blocks + per) * wide, rows, rows * cols),
    )(jnp.stack(which).astype(jnp.int32), x, *w, t)


def moved(x, pieces, which):
    blocks, rows, wide = x.shape
    cols, deep = pieces[0].shape
    per = deep // wide
    tile = rows // N
    count = len(pieces)
    at = lambda j: pl.BlockSpec((per, tile, wide), lambda i, which: (which[j], i, 0))

    def kernel(which_ref, *refs):
        xs, fs = refs[:count], refs[count : 2 * count]
        x = jnp.concatenate([x_ref[k] for x_ref in xs for k in range(per)], axis=1)
        f = jnp.concatenate([f_ref[...] for f_ref in fs], axis=1)
        refs[-1][...] = lax.dot_general(f, x, NT, preferred_element_type=F32)

    return pl.pallas_call(
        kernel,
        grid_spec=pltpu.PrefetchScalarGridSpec(
            num_scalar_prefetch=1,
            grid=(N,),
            in_specs=[at(j) for j in range(count)] + [pl.BlockSpec((cols, deep), lambda i, which: (0, 0))] * count,
            out_specs=pl.BlockSpec((cols, tile), lambda i, which: (0, i)),
        ),
        out_shape=jax.ShapeDtypeStruct((cols, rows), F32),
        compiler_params=WIDE,
        cost_estimate=cost(cols, deep * count, rows),
    )(jnp.stack(which).astype(jnp.int32), *([x] * count), *pieces)


def second_slopes(x, piece, block, part, scale, hidden, t):
    blocks, rows, wide = x.shape
    cols, deep = piece.shape
    per = deep // wide
    tile = rows // N
    out = pl.BlockSpec((cols, tile), lambda i, which: (0, i))
    whole = pl.BlockSpec((cols, deep), lambda i, which: (0, 0))

    def kernel(which_ref, scale_ref, x_ref, f_ref, part_ref, h_ref, t_ref, s_ref, far_ref, total_ref):
        x = joined(x_ref)
        move = part_ref[...] + lax.dot_general(f_ref[...], x, NT, preferred_element_type=F32)
        s = slope_of(h_ref[...] + scale_ref[0, 0] * move, t_ref[...])
        s_ref[...] = s
        add_term(s, x, far_ref, total_ref)

    return pl.pallas_call(
        kernel,
        grid_spec=pltpu.PrefetchScalarGridSpec(
            num_scalar_prefetch=1,
            grid=(N,),
            in_specs=[
                pl.BlockSpec(memory_space=pltpu.SMEM),
                pl.BlockSpec((per, tile, wide), lambda i, which: (which[0], i, 0)),
                whole,
                out,
                out,
                out,
            ],
            out_specs=[out, whole],
            scratch_shapes=[pltpu.VMEM((cols, deep), F32)],
        ),
        out_shape=[jax.ShapeDtypeStruct((cols, rows), BF16), jax.ShapeDtypeStruct((cols, deep), BF16)],
        compiler_params=PARAMS,
        cost_estimate=cost(cols, 2 * deep, rows, rows * cols),
    )(jnp.reshape(block, (1,)).astype(jnp.int32), scale, x, piece, part, hidden, t)


def terms(x, s, which, cut):
    blocks, rows, wide = x.shape
    cols = s.shape[0]
    half = cols // 2
    tile = rows // 2
    per = blocks // N
    count = len(which)
    at = lambda j: pl.BlockSpec((per, tile, wide), lambda i, which: (which[j], i, 0))
    kinds = [F32, BF16, BF16, F32] if cut else [F32] * count
    tall = half if cut else cols

    def kernel(which_ref, *refs):
        s_ref = refs[count]
        outs, totals = refs[count + 1 : -count], refs[-count:]
        parts = [jnp.dot(s_ref[...], joined(refs[j]), preferred_element_type=F32) for j in range(count)]

        @pl.when(pl.program_id(0) == 0)
        def _():
            for j in range(count):
                totals[j][...] = parts[j]

        @pl.when(pl.program_id(0) > 0)
        def _():
            for j in range(count):
                total = totals[j][...] + parts[j]
                for n in range(cols // tall):
                    out = outs[j * (cols // tall) + n]
                    out[...] = total[n * tall : (n + 1) * tall].astype(out.dtype)

    return pl.pallas_call(
        kernel,
        grid_spec=pltpu.PrefetchScalarGridSpec(
            num_scalar_prefetch=1,
            grid=(rows // tile,),
            in_specs=[at(j) for j in range(count)] + [pl.BlockSpec((cols, tile), lambda i, which: (0, i))],
            out_specs=[pl.BlockSpec((tall, per * wide), lambda i, which: (0, 0))] * len(kinds),
            scratch_shapes=[pltpu.VMEM((cols, per * wide), F32)] * count,
        ),
        out_shape=[jax.ShapeDtypeStruct((tall, per * wide), kind) for kind in kinds],
        compiler_params=PARAMS,
        cost_estimate=cost(cols * count, rows, per * wide),
    )(jnp.stack(which).astype(jnp.int32), *([x] * count), s)


def ring_sum(x, s, far, me):
    at = lambda step: lax.rem(me + step, N)
    half = far.shape[0] // 2
    far_next, far_prev = shift(far[:half], "x", 1), shift(far[half:], "x", -1)
    high, to_next, to_prev, low = terms(x, s, [at(1), at(3)], True)
    next_low, prev_high = shift(to_next, "x", 1), shift(to_prev, "x", -1)
    next_high = shift((high + far_next.astype(F32)).astype(BF16), "x", 1)
    prev_low = shift((low + far_prev.astype(F32)).astype(BF16), "x", -1)
    (own,) = terms(x, s, [at(0)], False)
    high = own[:half] + next_high.astype(F32) + prev_high.astype(F32)
    low = own[half:] + next_low.astype(F32) + prev_low.astype(F32)
    return jnp.concatenate([high, low], axis=0)


def ring_gather(value, axis):
    return [value, shift(value, axis, -1), shift(value, axis, 2), shift(value, axis, 1)]


def ring_gather_halves(value, axis):
    half = value.shape[0] // 2
    after, before = shift(value, axis, -1), shift(value, axis, 1)
    far = jnp.concatenate([shift(before[:half], axis, 1), shift(after[half:], axis, -1)], axis=0)
    return [value, after, far, before]


def ring_swap(chunk, axis):
    return [chunk(0), shift(chunk(3), axis, -1), shift(chunk(2), axis, 2), shift(chunk(1), axis, 1)]


def cut_kernel(which_ref, own, after, far, before, to_next, to_prev, kept):
    rows = own.shape[0]
    half = rows // 2
    to_next[:rows], to_next[rows:] = after[...], far[:half]
    to_prev[:rows], to_prev[rows:] = before[...], far[half:]
    kept[...] = own[...]


def cut(array, me):
    rows, cols = array.shape[0], array.shape[1] // N
    at = lambda k: pl.BlockSpec((rows, cols), lambda i, which: (0, which[k]))
    tall = [rows + rows // 2, rows + rows // 2, rows]
    return pl.pallas_call(
        cut_kernel,
        grid_spec=pltpu.PrefetchScalarGridSpec(
            num_scalar_prefetch=1,
            grid=(1,),
            in_specs=[at(k) for k in range(N)],
            out_specs=[pl.BlockSpec((size, cols), lambda i, which: (0, 0)) for size in tall],
        ),
        out_shape=[jax.ShapeDtypeStruct((size, cols), array.dtype) for size in tall],
        compiler_params=WIDE,
        cost_estimate=cost(0, 0, 0),
    )(jnp.stack([lax.rem(me + k, N) for k in range(N)]).astype(jnp.int32), *([array] * N))


def ring_swap_halves(to_next, to_prev, kept, axis):
    rows = kept.shape[0]
    prev, after = shift(to_next, axis, 1), shift(to_prev, axis, -1)
    high, low = shift(prev[rows:], axis, 1), shift(after[rows:], axis, -1)
    return [kept, after[:rows], jnp.concatenate([high, low], axis=0), prev[:rows]]


def in_order(pieces, me):
    twice = jnp.stack(pieces + pieces)
    return lax.dynamic_slice_in_dim(twice, lax.rem(N - me, N), N, axis=0)


def total_of(value, beside):
    total = jnp.full((N * N * N, 128), jnp.sum(value * value), F32)
    total = total + lax.ppermute(total, "c", [(0, 1), (1, 0)])
    each = lax.all_to_all(total, ("x", "y", "z"), split_axis=0, concat_axis=0, tiled=True)
    if beside is not None:
        each, beside = lax.optimization_barrier((each, beside))
    return jnp.sum(each[:, 0]), beside


def per_device(tokens, target, weight):
    ix, iy = lax.axis_index("x"), lax.axis_index("y")
    rows, wide = tokens.shape
    cols = weight.shape[1] // N
    width = wide * 2 * N
    hidden_all = weight.shape[1] * 2 * N

    x = lax.all_gather(tokens, ("z", "c", "y"), axis=0, tiled=True).reshape(2 * N, N * rows, wide)

    def columns(array):
        return lambda k: lax.dynamic_slice_in_dim(array, lax.rem(iy + k, N) * cols, cols, axis=1)

    to_next, to_prev, kept = cut(target, iy)
    w_pieces = ring_swap(columns(weight), "y")
    to_next, to_prev = lax.optimization_barrier((to_next, to_prev, *w_pieces))[:2]
    t = in_order(ring_swap_halves(to_next, to_prev, kept, "y"), iy)
    t = jnp.concatenate([t[k].T for k in range(N)], axis=1)
    w = ring_gather(in_order(w_pieces, iy).reshape(-1, cols).T, "x")

    at = lambda k: lax.rem(ix + k, N)
    hidden, slope, term = first_slopes(x, w, t, [at(k) for k in range(N)])
    first = ring_sum(x, slope, term, ix)
    own, after, far, before = ring_gather_halves(first.astype(BF16), "x")
    part = moved(x, [own, after, before], [at(0), at(1), at(3)])
    total, part = total_of(first, part)
    scale = 0.5 * math.sqrt(hidden_all) / jnp.sqrt(total + 1e-06)
    slope, term = second_slopes(x, far, at(2), part, scale.reshape(1, 1), hidden, t)
    second = ring_sum(x, slope, term, ix)
    total, _ = total_of(second, None)
    factor = jnp.minimum(1.0, math.sqrt(width * hidden_all) / jnp.sqrt(total + 1e-06))
    held = second.astype(BF16).T.reshape(N, -1, cols)
    parts = in_order(ring_swap(lambda k: lax.dynamic_index_in_dim(held, lax.rem(iy + k, N), 0, keepdims=False), "y"), iy)
    whole = jnp.concatenate([parts[k] for k in range(N)], axis=1)
    return whole.astype(F32) * factor


def solution(mesh):
    grid = Mesh(mesh.devices.reshape(N, N, N, 2), ("x", "y", "z", "c"))
    spec = P(("x", "y"), ("z", "c"))
    return jax.shard_map(
        per_device, mesh=grid, in_specs=(spec, spec, spec), out_specs=spec, check_vma=False
    )
```

```python
import math

import jax
import jax.numpy as jnp
from jax import lax
from jax.experimental import pallas as pl
from jax.experimental.pallas import tpu as pltpu
from jax.sharding import Mesh, PartitionSpec as P

BF16, F32 = jnp.bfloat16, jnp.float32
N = 4
NT = (((1,), (1,)), ((), ()))
PARAMS = pltpu.CompilerParams(vmem_limit_bytes=52 << 20)


def shift(value, axis, step):
    return lax.ppermute(value, axis, [(i, (i + step) % N) for i in range(N)])


def behind(value, *others):
    return lax.optimization_barrier((value, *others))[0]


def slope_of(hidden, target):
    root = math.sqrt(2.0 / math.pi)
    square = hidden * hidden
    bend = jnp.tanh(hidden * (root + (root * 0.044715) * square))
    half = 0.5 + 0.5 * bend
    deriv = half + (hidden * (1.0 - bend * bend)) * (0.5 * root + (1.5 * root * 0.044715) * square)
    return ((hidden * half - target.astype(F32)) * deriv).astype(BF16)


def joined(x_ref):
    return jnp.concatenate([x_ref[k] for k in range(x_ref.shape[0])], axis=1)


def cost(rows, deep, cols, exps=0):
    return pl.CostEstimate(
        flops=2 * rows * deep * cols, bytes_accessed=2 * deep * (rows + cols) + 4 * rows * cols, transcendentals=exps
    )


def add_term(s, x, far_ref, total_ref):
    part = jnp.dot(s, x, preferred_element_type=F32)
    step = pl.program_id(0)

    @pl.when(step == 0)
    def _():
        total_ref[...] = part

    @pl.when(step > 0)
    def _():
        total_ref[...] += part

    @pl.when(step == pl.num_programs(0) - 1)
    def _():
        far_ref[...] = total_ref[...].astype(BF16)


def first_slopes(x, w, t, which):
    blocks, rows, wide = x.shape
    cols, deep = w[0].shape
    tile = rows // N
    per = deep // wide
    out = pl.BlockSpec((cols, tile), lambda i, which: (0, i))
    whole = pl.BlockSpec((cols, deep), lambda i, which: (0, 0), pipeline_mode=pl.Buffered(1))

    def kernel(which_ref, x_ref, *refs):
        w_refs, (t_ref, h_ref, s_ref, far_ref, total_ref, w_all) = refs[:N], refs[N:]

        @pl.when(pl.program_id(0) == 0)
        def _():
            w_all[...] = jnp.concatenate([w_ref[...] for w_ref in w_refs], axis=1)

        block = lambda j: [x_ref[per * which_ref[j] + k] for k in range(per)]
        x = jnp.concatenate([part for j in range(N) for part in block(j)], axis=1)
        hidden = lax.dot_general(w_all[...], x, NT, preferred_element_type=F32)
        h_ref[...] = hidden
        s = slope_of(hidden, t_ref[...])
        s_ref[...] = s
        add_term(s, jnp.concatenate(block(2), axis=1), far_ref, total_ref)

    return pl.pallas_call(
        kernel,
        grid_spec=pltpu.PrefetchScalarGridSpec(
            num_scalar_prefetch=1,
            grid=(N,),
            in_specs=[pl.BlockSpec((blocks, tile, wide), lambda i, which: (0, i, 0))] + [whole] * N + [out],
            out_specs=[out, out, pl.BlockSpec((cols, deep), lambda i, which: (0, 0))],
            scratch_shapes=[pltpu.VMEM((cols, deep), F32), pltpu.VMEM((cols, N * deep), BF16)],
        ),
        out_shape=[
            jax.ShapeDtypeStruct((cols, rows), F32),
            jax.ShapeDtypeStruct((cols, rows), BF16),
            jax.ShapeDtypeStruct((cols, deep), BF16),
        ],
        compiler_params=PARAMS,
        cost_estimate=cost(cols, (blocks + per) * wide, rows, rows * cols),
    )(jnp.stack(which).astype(jnp.int32), x, *w, t)


def moved(x, pieces, which):
    blocks, rows, wide = x.shape
    cols, deep = pieces[0].shape
    per = deep // wide
    tile = rows // N
    count = len(pieces)
    at = lambda j: pl.BlockSpec((per, tile, wide), lambda i, which: (which[j], i, 0))

    def kernel(which_ref, *refs):
        xs, fs = refs[:count], refs[count : 2 * count]
        x = jnp.concatenate([x_ref[k] for x_ref in xs for k in range(per)], axis=1)
        f = jnp.concatenate([f_ref[...] for f_ref in fs], axis=1)
        refs[-1][...] = lax.dot_general(f, x, NT, preferred_element_type=F32)

    return pl.pallas_call(
        kernel,
        grid_spec=pltpu.PrefetchScalarGridSpec(
            num_scalar_prefetch=1,
            grid=(N,),
            in_specs=[at(j) for j in range(count)] + [pl.BlockSpec((cols, deep), lambda i, which: (0, 0))] * count,
            out_specs=pl.BlockSpec((cols, tile), lambda i, which: (0, i)),
        ),
        out_shape=jax.ShapeDtypeStruct((cols, rows), F32),
        compiler_params=PARAMS,
        cost_estimate=cost(cols, deep * count, rows),
    )(jnp.stack(which).astype(jnp.int32), *([x] * count), *pieces)


def second_slopes(x, piece, block, part, scale, hidden, t):
    blocks, rows, wide = x.shape
    cols, deep = piece.shape
    per = deep // wide
    tile = rows // N
    out = pl.BlockSpec((cols, tile), lambda i, which: (0, i))
    whole = pl.BlockSpec((cols, deep), lambda i, which: (0, 0))

    def kernel(which_ref, scale_ref, x_ref, f_ref, part_ref, h_ref, t_ref, s_ref, far_ref, total_ref):
        x = joined(x_ref)
        move = part_ref[...] + lax.dot_general(f_ref[...], x, NT, preferred_element_type=F32)
        s = slope_of(h_ref[...] + scale_ref[0, 0] * move, t_ref[...])
        s_ref[...] = s
        add_term(s, x, far_ref, total_ref)

    return pl.pallas_call(
        kernel,
        grid_spec=pltpu.PrefetchScalarGridSpec(
            num_scalar_prefetch=1,
            grid=(N,),
            in_specs=[
                pl.BlockSpec(memory_space=pltpu.SMEM),
                pl.BlockSpec((per, tile, wide), lambda i, which: (which[0], i, 0)),
                whole,
                out,
                out,
                out,
            ],
            out_specs=[out, whole],
            scratch_shapes=[pltpu.VMEM((cols, deep), F32)],
        ),
        out_shape=[jax.ShapeDtypeStruct((cols, rows), BF16), jax.ShapeDtypeStruct((cols, deep), BF16)],
        compiler_params=PARAMS,
        cost_estimate=cost(cols, 2 * deep, rows, rows * cols),
    )(jnp.reshape(block, (1,)).astype(jnp.int32), scale, x, piece, part, hidden, t)


def terms(x, s, which, cut):
    blocks, rows, wide = x.shape
    cols = s.shape[0]
    half = cols // 2
    tile = rows // 2
    per = blocks // N
    count = len(which)
    at = lambda j: pl.BlockSpec((per, tile, wide), lambda i, which: (which[j], i, 0))
    kinds = [F32, BF16, BF16, F32] if cut else [F32] * count
    tall = half if cut else cols

    def kernel(which_ref, *refs):
        s_ref = refs[count]
        outs, totals = refs[count + 1 : -count], refs[-count:]
        parts = [jnp.dot(s_ref[...], joined(refs[j]), preferred_element_type=F32) for j in range(count)]

        @pl.when(pl.program_id(0) == 0)
        def _():
            for j in range(count):
                totals[j][...] = parts[j]

        @pl.when(pl.program_id(0) > 0)
        def _():
            for j in range(count):
                total = totals[j][...] + parts[j]
                for n in range(cols // tall):
                    out = outs[j * (cols // tall) + n]
                    out[...] = total[n * tall : (n + 1) * tall].astype(out.dtype)

    return pl.pallas_call(
        kernel,
        grid_spec=pltpu.PrefetchScalarGridSpec(
            num_scalar_prefetch=1,
            grid=(rows // tile,),
            in_specs=[at(j) for j in range(count)] + [pl.BlockSpec((cols, tile), lambda i, which: (0, i))],
            out_specs=[pl.BlockSpec((tall, per * wide), lambda i, which: (0, 0))] * len(kinds),
            scratch_shapes=[pltpu.VMEM((cols, per * wide), F32)] * count,
        ),
        out_shape=[jax.ShapeDtypeStruct((tall, per * wide), kind) for kind in kinds],
        compiler_params=PARAMS,
        cost_estimate=cost(cols * count, rows, per * wide),
    )(jnp.stack(which).astype(jnp.int32), *([x] * count), s)


def ring_sum(x, s, far, me):
    at = lambda step: lax.rem(me + step, N)
    half = far.shape[0] // 2
    far_next, far_prev = shift(far[:half], "x", 1), shift(far[half:], "x", -1)
    high, to_next, to_prev, low = terms(x, s, [at(1), at(3)], True)
    next_low, prev_high = shift(to_next, "x", 1), shift(to_prev, "x", -1)
    next_high = shift((high + far_next.astype(F32)).astype(BF16), "x", 1)
    prev_low = shift((low + far_prev.astype(F32)).astype(BF16), "x", -1)
    (own,) = terms(x, s, [at(0)], False)
    high = own[:half] + next_high.astype(F32) + prev_high.astype(F32)
    low = own[half:] + next_low.astype(F32) + prev_low.astype(F32)
    return jnp.concatenate([high, low], axis=0)


def ring_gather(value, axis):
    return [value, shift(value, axis, -1), shift(value, axis, 2), shift(value, axis, 1)]


def ring_gather_halves(value, axis):
    half = value.shape[0] // 2
    after, before = shift(value, axis, -1), shift(value, axis, 1)
    far = jnp.concatenate([shift(before[:half], axis, 1), shift(after[half:], axis, -1)], axis=0)
    return [value, after, far, before]


def ring_swap(chunk, axis):
    return [chunk(0), shift(chunk(3), axis, -1), shift(chunk(2), axis, 2), shift(chunk(1), axis, 1)]


def cut_kernel(which_ref, own, after, far, before, to_next, to_prev, kept):
    rows = own.shape[0]
    half = rows // 2
    to_next[:rows], to_next[rows:] = after[...], far[:half]
    to_prev[:rows], to_prev[rows:] = before[...], far[half:]
    kept[...] = own[...]


def cut(array, me):
    rows, cols = array.shape[0], array.shape[1] // N
    at = lambda k: pl.BlockSpec((rows, cols), lambda i, which: (0, which[k]))
    tall = [rows + rows // 2, rows + rows // 2, rows]
    return pl.pallas_call(
        cut_kernel,
        grid_spec=pltpu.PrefetchScalarGridSpec(
            num_scalar_prefetch=1,
            grid=(1,),
            in_specs=[at(k) for k in range(N)],
            out_specs=[pl.BlockSpec((size, cols), lambda i, which: (0, 0)) for size in tall],
        ),
        out_shape=[jax.ShapeDtypeStruct((size, cols), array.dtype) for size in tall],
        compiler_params=PARAMS,
        cost_estimate=cost(0, 0, 0),
    )(jnp.stack([lax.rem(me + k, N) for k in range(N)]).astype(jnp.int32), *([array] * N))


def ring_swap_halves(to_next, to_prev, kept, axis):
    rows = kept.shape[0]
    prev, after = shift(to_next, axis, 1), shift(to_prev, axis, -1)
    high, low = shift(prev[rows:], axis, 1), shift(after[rows:], axis, -1)
    return [kept, after[:rows], jnp.concatenate([high, low], axis=0), prev[:rows]]


def in_order(pieces, me):
    twice = jnp.stack(pieces + pieces)
    return lax.dynamic_slice_in_dim(twice, lax.rem(N - me, N), N, axis=0)


def total_of(value, beside):
    total = jnp.full((N * N * N, 128), jnp.sum(value * value), F32)
    total = total + lax.ppermute(total, "c", [(0, 1), (1, 0)])
    each = lax.all_to_all(total, ("x", "y", "z"), split_axis=0, concat_axis=0, tiled=True)
    if beside is not None:
        each, beside = lax.optimization_barrier((each, beside))
    return jnp.sum(each[:, 0]), beside


def per_device(tokens, target, weight):
    ix, iy = lax.axis_index("x"), lax.axis_index("y")
    rows, wide = tokens.shape
    cols = weight.shape[1] // N
    width = wide * 2 * N
    hidden_all = weight.shape[1] * 2 * N

    x = lax.all_gather(tokens, ("z", "c", "y"), axis=0, tiled=True).reshape(2 * N, N * rows, wide)

    def columns(array):
        return lambda k: lax.dynamic_slice_in_dim(array, lax.rem(iy + k, N) * cols, cols, axis=1)

    to_next, to_prev, kept = cut(target, iy)
    w_pieces = ring_swap(columns(weight), "y")
    to_next, to_prev = lax.optimization_barrier((to_next, to_prev, *w_pieces))[:2]
    t = in_order(ring_swap_halves(to_next, to_prev, kept, "y"), iy)
    t = jnp.concatenate([t[k].T for k in range(N)], axis=1)
    w = ring_gather(in_order(w_pieces, iy).reshape(-1, cols).T, "x")

    at = lambda k: lax.rem(ix + k, N)
    hidden, slope, term = first_slopes(x, w, t, [at(k) for k in range(N)])
    first = ring_sum(x, slope, term, ix)
    own, after, far, before = ring_gather_halves(first.astype(BF16), "x")
    part = moved(x, [own, after, before], [at(0), at(1), at(3)])
    total, part = total_of(first, part)
    scale = 0.5 * math.sqrt(hidden_all) / jnp.sqrt(total + 1e-06)
    slope, term = second_slopes(x, far, at(2), part, scale.reshape(1, 1), hidden, t)
    second = ring_sum(x, slope, term, ix)
    total, _ = total_of(second, None)
    factor = jnp.minimum(1.0, math.sqrt(width * hidden_all) / jnp.sqrt(total + 1e-06))
    held = second.astype(BF16).T.reshape(N, -1, cols)
    parts = in_order(ring_swap(lambda k: lax.dynamic_index_in_dim(held, lax.rem(iy + k, N), 0, keepdims=False), "y"), iy)
    whole = jnp.concatenate([parts[k] for k in range(N)], axis=1)
    return whole.astype(F32) * factor


def solution(mesh):
    grid = Mesh(mesh.devices.reshape(N, N, N, 2), ("x", "y", "z", "c"))
    spec = P(("x", "y"), ("z", "c"))
    return jax.shard_map(
        per_device, mesh=grid, in_specs=(spec, spec, spec), out_specs=spec, check_vma=False
    )
```
